32 devices in a mesh: batch: 8 (over z, y), tensor: 4 (over x, core).
Axes of the slice: x: 2, y: 2, z: 4, core: 2. Of those that a mesh axis runs over, the one named last changes fastest.
Arguments:
- tokens: bfloat16 [8, 1024, 768], P('batch'), may hold values from -6 to 6
- ln1_gain: float32 [768], replicated, may hold values from 0.5 to 1.5
- ln1_bias: float32 [768], replicated, may hold values from -1.75 to 1.75
- qkv_weight: bfloat16 [768, 3, 768], P(None, None, 'tensor'), may hold values from -0.3125 to 0.3125
- qkv_bias: float32 [2, 12, 64], P(None, 'tensor'), may hold values from -3 to 3
- out_weight: bfloat16 [768, 768], P('tensor'), may hold values from -0.625 to 0.625
- out_bias: float32 [768], replicated, may hold values from -1.75 to 1.75
- ln2_gain: float32 [768], replicated, may hold values from 0.5 to 1.5
- ln2_bias: float32 [768], replicated, may hold values from -1.75 to 1.75
- fc1_weight: bfloat16 [768, 3072], P(None, 'tensor'), may hold values from -0.21875 to 0.21875
- fc1_bias: float32 [48, 64], P('tensor'), may hold values from -3 to 3
- fc2_weight: bfloat16 [3072, 768], P('tensor'), may hold values from -0.109375 to 0.109375
- fc2_bias: float32 [768], replicated, may hold values from -1.75 to 1.75
- cotangent: bfloat16 [8, 1024, 768], P('batch'), may hold values from -6 to 6
Outputs:
- result: bfloat16 [8, 1024, 768], P('batch')
- grad_tokens: bfloat16 [8, 1024, 768], P('batch')
- grad_qkv_weight: float32 [768, 3, 768], P('batch', None, 'tensor')
- grad_qkv_bias: float32 [2, 12, 64], P(None, 'tensor', 'batch')
- grad_out_weight: float32 [768, 768], P('tensor', 'batch')
- grad_out_bias: float32 [768], P('batch')
- grad_ln1_gain: float32 [768], P('batch')
- grad_ln1_bias: float32 [768], P('batch')
- grad_ln2_gain: float32 [768], P('batch')
- grad_ln2_bias: float32 [768], P('batch')
- grad_fc1_weight: float32 [768, 3072], P('batch', 'tensor')
- grad_fc1_bias: float32 [48, 64], P('tensor', 'batch')
- grad_fc2_weight: float32 [3072, 768], P('tensor', 'batch')
- grad_fc2_bias: float32 [768], P('batch')
The draws below stay inside these ranges and needn't reach their ends.
All inputs are finite; a program needn't handle non-finite values.
Results may differ from the reference program's by a relative error of at most 0.012.
The reference program's roundings to bfloat16 on the way count: a program that leaves them out, or rounds other values in their place, can miss the bound.
Values sent between devices are 32-bit elements; how exact they have to be, the bound alone decides.
No kernel may reach another device: no remote copies, remote signals or barrier semaphores. Data moves between devices by JAX's collectives and lax.ppermute only.
A program may use at most 128 MiB of HBM per device.

```python
import math
import jax
import jax.numpy as jnp
from jax import lax

HEADS = 12
HD = 64
D = 768
FF = 3072
SEQ = 1024
CLIPS = 8


def spiked(values, stream_key, source, target, shards_of, factor):
    def block_of(axis_at):
        return (jnp.arange(values.shape[axis_at]) // (values.shape[axis_at] // shards_of)).reshape((-1,) + (1,) * (values.ndim - 1 - axis_at))

    one_side = jax.random.permutation(stream_key, shards_of)[block_of(target)]
    other_side = (block_of(target) + shards_of // 2) % shards_of
    return jnp.where((block_of(source) == one_side) | (block_of(source) == other_side), factor * values, values)


def block_levels(key, shape, pieces, low, largest):
    factor_of = 1.0
    for position, shards_of in pieces:
        steps = jax.random.uniform(jax.random.fold_in(jax.random.fold_in(key, 6), position), (shards_of,), jnp.float32, low / len(pieces), largest / len(pieces))
        factor_of = factor_of * jnp.repeat(jnp.exp(steps), shape[position] // shards_of).reshape((-1,) + (1,) * (len(shape) - 1 - position))
    return factor_of


def bell_draw(key, extent, scale, limit, split=(), dtype=jnp.bfloat16):
    drawn = scale * jax.random.normal(key, extent, jnp.float32)
    if split:
        drawn = drawn * block_levels(key, extent, split, -0.22, 0.18)
    return jnp.clip(drawn, -limit, limit).astype(dtype)


def noise_with(rng, dims, width, reach, shards, heavy, held_as=jnp.bfloat16):
    drawn = width * jax.random.normal(rng, dims, jnp.float32)
    if shards:
        drawn = drawn * block_levels(rng, dims, shards, -0.22, 0.18)
    return jnp.clip(spiked(drawn, jax.random.fold_in(rng, 3), *heavy), -reach, reach).astype(held_as)


def setup_inputs(seed: int = 0) -> dict:
    streams_of = jax.random.split(jax.random.key(seed), 15)
    return {
        "tokens": noise_with(streams_of[0], (CLIPS, SEQ, D), 1.0, 6.0, ((0, 8),), (0, 2, 8, 2.0)),
        "ln1_gain": jnp.clip(1.0 + 0.1 * jax.random.normal(streams_of[1], (D,), jnp.float32), 0.5, 1.5),
        "ln1_bias": bell_draw(streams_of[2], (D,), 0.3, 1.75, (), jnp.float32),
        "qkv_weight": bell_draw(streams_of[3], (D, 3, D), (D // 2) ** -0.5, 0.3125, ((2, 4),)),
        "qkv_bias": bell_draw(streams_of[4], (2, HEADS, HD), 0.5, 3.0, ((1, 4),), jnp.float32),
        "out_weight": bell_draw(streams_of[5], (D, D), (D // 8) ** -0.5, 0.625, ((0, 4),)),
        "out_bias": bell_draw(streams_of[6], (D,), 0.3, 1.75, (), jnp.float32),
        "ln2_gain": jnp.clip(1.0 + 0.1 * jax.random.normal(streams_of[7], (D,), jnp.float32), 0.5, 1.5),
        "ln2_bias": bell_draw(streams_of[8], (D,), 0.3, 1.75, (), jnp.float32),
        "fc1_weight": bell_draw(streams_of[9], (D, FF), D ** -0.5, 0.21875, ((1, 4),)),
        "fc1_bias": bell_draw(streams_of[10], (FF // HD, HD), 0.5, 3.0, ((0, 4),), jnp.float32),
        "fc2_weight": bell_draw(streams_of[11], (FF, D), FF ** -0.5, 0.109375, ((0, 4),)),
        "fc2_bias": bell_draw(streams_of[12], (D,), 0.3, 1.75, (), jnp.float32),
        "cotangent": noise_with(streams_of[13], (CLIPS, SEQ, D), 1.0, 6.0, ((0, 8),), (0, 2, 8, 2.0)),
    }


@jax.custom_vjp
def low(v):
    return lax.optimization_barrier(v.astype(jnp.bfloat16)).astype(jnp.float32)

@jax.custom_vjp
def low_back(v):
    return v

def low_keep(v):
    return (low(v), None)

def low_pass(kept, grad):
    return (grad,)

def back_keep(v):
    return (v, None)

def back_low(kept, grad):
    return (low(grad),)
low.defvjp(low_keep, low_pass)
low_back.defvjp(back_keep, back_low)
norm_epsilon = 1e-06
highest = lax.Precision.HIGHEST

def layer_norm(values, scale_gain, offset_bias):
    average = lax.optimization_barrier(jnp.mean(values, axis=-1, keepdims=True))
    centered = values - average
    spread = lax.optimization_barrier(jnp.mean(centered * centered, axis=-1, keepdims=True))
    return centered * lax.rsqrt(spread + norm_epsilon) * scale_gain + offset_bias

def attend_clip(packed_clip):
    queries = packed_clip[:, 0]
    all_keys = packed_clip[:, 1]
    values = packed_clip[:, 2]
    scaling = 1.0 / math.sqrt(HD)
    scores = jnp.einsum('qhe,khe->hqk', queries, all_keys, precision=highest) * scaling
    scores = low_back(scores)
    softmax_rows = low(jax.nn.softmax(scores, axis=-1))
    return jnp.einsum('hqk,khe->qhe', softmax_rows, values, precision=highest)

def forward(token_rows, ln1_gain, ln1_bias, qkv_weight, qkv_bias, out_weight, out_bias, ln2_gain, ln2_bias, fc1_weight, fc1_bias, fc2_weight, fc2_bias):
    first_left = low(layer_norm(token_rows, ln1_gain, ln1_bias))
    packed = jnp.einsum('nd,dte->nte', first_left, qkv_weight, precision=highest)
    bias_full = jnp.stack([qkv_bias[0].reshape(D), jnp.zeros((D,), jnp.float32), qkv_bias[1].reshape(D)])
    packed = low_back(low(packed + bias_full))
    attended = lax.map(jax.checkpoint(attend_clip), packed.reshape(CLIPS, SEQ, 3, HEADS, HD))
    attended = low_back(low(attended.reshape(CLIPS * SEQ, D)))
    branch = low_back(jnp.dot(attended, out_weight, precision=highest) + out_bias)
    middle = token_rows + branch
    second_left = low(layer_norm(middle, ln2_gain, ln2_bias))
    hidden_pre = low_back(jnp.dot(second_left, fc1_weight, precision=highest) + fc1_bias.reshape(FF))
    hidden_low = low(jax.nn.gelu(hidden_pre, approximate=False))
    return middle + jnp.dot(hidden_low, fc2_weight, precision=highest) + fc2_bias

def reference(tokens, ln1_gain, ln1_bias, qkv_weight, qkv_bias, out_weight, out_bias, ln2_gain, ln2_bias, fc1_weight, fc1_bias, fc2_weight, fc2_bias, cotangent):
    float_args = tuple((item.astype(jnp.float32) for item in (tokens.reshape(CLIPS * SEQ, D), ln1_gain, ln1_bias, qkv_weight, qkv_bias, out_weight, out_bias, ln2_gain, ln2_bias, fc1_weight, fc1_bias, fc2_weight, fc2_bias)))
    output, pullback = jax.vjp(forward, *float_args)
    gradients = pullback(cotangent.astype(jnp.float32).reshape(CLIPS * SEQ, D))
    result = output.reshape(CLIPS, SEQ, D).astype(jnp.bfloat16)
    grad_tokens = gradients[0].reshape(CLIPS, SEQ, D).astype(jnp.bfloat16)
    return (result, grad_tokens, gradients[3], gradients[4], gradients[5], gradients[6], gradients[1], gradients[2], gradients[7], gradients[8], gradients[9], gradients[10], gradients[11], gradients[12])
```

```python
import functools
import math

import jax
import jax.numpy as jnp
from jax import lax
from jax.experimental import pallas as pl
from jax.experimental.pallas import tpu as pltpu
from jax.sharding import PartitionSpec as P

HD = 64
BLOCK = 256
EPSILON = 1e-06
F32 = jnp.float32
BF16 = jnp.bfloat16
VMEM_LIMIT = 56 * 1024 * 1024


def nn(a, b):
    return lax.dot_general(a, b, (((1,), (0,)), ((), ())), preferred_element_type=F32)


def nt(a, b):
    return lax.dot_general(a, b, (((1,), (1,)), ((), ())), preferred_element_type=F32)


def tn(a, b):
    return lax.dot_general(a, b, (((0,), (0,)), ((), ())), preferred_element_type=F32)


def whole(shape):
    return pl.BlockSpec(shape, lambda *_: (0,) * len(shape))


def call(kernel, name, grid, in_specs, out_specs, out_shape, flops, scalars=0, scratch=()):
    moved = sum(math.prod(s.shape) * s.dtype.itemsize for s in out_shape)
    return pl.pallas_call(
        kernel,
        grid_spec=pltpu.PrefetchScalarGridSpec(
            num_scalar_prefetch=scalars,
            grid=grid,
            in_specs=in_specs,
            out_specs=out_specs,
            scratch_shapes=list(scratch),
        ),
        out_shape=out_shape,
        compiler_params=pltpu.CompilerParams(vmem_limit_bytes=VMEM_LIMIT),
        cost_estimate=pl.CostEstimate(flops=flops, bytes_accessed=2 * moved, transcendentals=0),
        name=name,
    )


def shape_of(shape, dtype):
    return jax.ShapeDtypeStruct(shape, dtype)


def normalize(values):
    average = jnp.mean(values, axis=-1, keepdims=True)
    centered = values - average
    spread = jnp.mean(centered * centered, axis=-1, keepdims=True)
    factor = lax.rsqrt(spread + EPSILON)
    return centered * factor, factor


def project_kernel(x_ref, gain_ref, bias_ref, w_ref, wb_ref, left_ref, q_ref, k_ref, v_ref):
    normal, _ = normalize(x_ref[...].astype(F32))
    left = (normal * gain_ref[...] + bias_ref[...]).astype(BF16)
    left_ref[...] = left
    width = q_ref.shape[1]
    for part, ref in enumerate((q_ref, k_ref, v_ref)):
        ref[...] = (
            nt(left, w_ref[part]) + wb_ref[:, part * width : (part + 1) * width]
        ).astype(BF16)


def project(x, gain, bias, weight, weight_bias):
    rows, model = x.shape
    width = weight.shape[1]
    out = pl.BlockSpec((BLOCK, width), lambda i: (i, 0))
    return call(
        project_kernel,
        "project",
        (rows // BLOCK,),
        [
            pl.BlockSpec((BLOCK, model), lambda i: (i, 0)),
            whole((1, model)),
            whole((1, model)),
            whole(weight.shape),
            whole((1, 3 * width)),
        ],
        [pl.BlockSpec((BLOCK, model), lambda i: (i, 0)), out, out, out],
        [shape_of((rows, model), BF16)] + [shape_of((rows, width), BF16)] * 3,
        2 * rows * model * 3 * width,
    )(x, gain, bias, weight, weight_bias)


def project_again_kernel(left_ref, w_ref, wb_ref, q_ref, k_ref, v_ref):
    width = q_ref.shape[1]
    for part, ref in enumerate((q_ref, k_ref, v_ref)):
        ref[...] = (
            nt(left_ref[...], w_ref[part]) + wb_ref[:, part * width : (part + 1) * width]
        ).astype(BF16)


def project_again(left, weight, weight_bias):
    rows, model = left.shape
    width = weight.shape[1]
    out = pl.BlockSpec((BLOCK, width), lambda i: (i, 0))
    return call(
        project_again_kernel,
        "project_again",
        (rows // BLOCK,),
        [
            pl.BlockSpec((BLOCK, model), lambda i: (i, 0)),
            whole(weight.shape),
            whole((1, 3 * width)),
        ],
        [out, out, out],
        [shape_of((rows, width), BF16)] * 3,
        2 * rows * model * 3 * width,
    )(left, weight, weight_bias)


def attend_kernel(q_ref, k_ref, v_ref, out_ref, total_ref):
    heads = q_ref.shape[1] // HD
    scale = 1.0 / math.sqrt(HD)
    parts = []
    logs = []
    for head in range(heads):
        at = slice(head * HD, (head + 1) * HD)
        scores = nt(k_ref[:, at], q_ref[:, at] * jnp.asarray(scale, BF16))
        peak = jnp.max(scores, axis=0, keepdims=True)
        powers = jnp.exp(scores - peak)
        totals = jnp.sum(powers, axis=0, keepdims=True)
        mixed = tn(v_ref[:, at], powers.astype(BF16))
        parts.append(mixed / totals)
        logs.append(peak + jnp.log(totals))
    out_ref[...] = jnp.transpose(jnp.concatenate(parts, axis=0)).astype(BF16).astype(F32)
    logs.append(jnp.zeros((total_ref.shape[0] - heads, total_ref.shape[1]), F32))
    total_ref[...] = jnp.concatenate(logs, axis=0)


def attend(queries, keys, values, chunk, chunk_rows):
    rows, width = keys.shape
    blocks = chunk_rows // BLOCK
    return call(
        attend_kernel,
        "attend",
        (blocks,),
        [
            pl.BlockSpec((BLOCK, width), lambda i: (chunk * blocks + i, 0)),
            whole((rows, width)),
            whole((rows, width)),
        ],
        [
            pl.BlockSpec((BLOCK, width), lambda i: (i, 0)),
            pl.BlockSpec((8, BLOCK), lambda i: (0, i)),
        ],
        [shape_of((chunk_rows, width), F32), shape_of((8, chunk_rows), F32)],
        2 * chunk_rows * rows * 256 * 6,
    )(queries, keys, values)


ERF = (0.254829592, -0.284496736, 1.421413741, -1.453152027, 1.061405429)


def gelu_pair(values):
    size = jnp.abs(values) * (1.0 / math.sqrt(2.0))
    step = 1.0 / (1.0 + 0.3275911 * size)
    bell = jnp.exp(-(size * size))
    series = ERF[4]
    for factor in (ERF[3], ERF[2], ERF[1], ERF[0]):
        series = series * step + factor
    tail = (0.5 * step) * series * bell
    below = jnp.where(values >= 0, 1.0 - tail, tail)
    return values * below, below + values * (bell * (1.0 / math.sqrt(2.0 * math.pi)))


def feed_kernel(
    core_ref,
    x_ref,
    dy_ref,
    a0_ref,
    a1_ref,
    a2_ref,
    a3_ref,
    w0_ref,
    w1_ref,
    w2_ref,
    w3_ref,
    out_bias_ref,
    gain_ref,
    bias_ref,
    fc1_ref,
    fc1_bias_ref,
    fc2_ref,
    middle_ref,
    left_ref,
    hidden_ref,
    pre_ref,
    send_res_ref,
    keep_res_ref,
    send_ref,
    keep_ref,
    sums_ref,
):
    step = pl.program_id(0)

    def share(a_ref, w_ref):
        return nn(a_ref[...].astype(BF16), w_ref[...].astype(BF16))

    branch = (share(a0_ref, w0_ref) + share(a1_ref, w1_ref)) + (
        share(a2_ref, w2_ref) + share(a3_ref, w3_ref)
    )
    middle = x_ref[...].astype(F32) + (branch + out_bias_ref[...])
    middle_ref[...] = middle
    normal, _ = normalize(middle)
    left = (normal * gain_ref[...] + bias_ref[...]).astype(BF16)
    left_ref[...] = left
    hidden, slope = gelu_pair(nn(left, fc1_ref[...]) + fc1_bias_ref[...])
    hidden = hidden.astype(BF16)
    hidden_ref[...] = hidden
    dy = dy_ref[...]
    pre = (nt(dy, fc2_ref[...]) * slope).astype(BF16)
    pre_ref[...] = pre
    second = nt(pre, fc1_ref[...])
    fed = nn(hidden, fc2_ref[...])
    pre_sum = jnp.sum(pre.astype(F32), axis=0, keepdims=True)

    @pl.when(step == 0)
    def _():
        send_ref[...] = second
        send_res_ref[...] = fed
        sums_ref[0:1, :] = pre_sum

    @pl.when(step == 1)
    def _():
        keep_ref[...] = second
        keep_res_ref[...] = fed
        sums_ref[0:1, :] = sums_ref[0:1, :] + pre_sum
        sums_ref[1:2, :] = jnp.sum(dy.astype(F32), axis=0, keepdims=True)


def feed(core, chunk, x, dy, attended, out_weights, out_bias, gain, bias, fc1, fc1_bias, fc2):
    model = x.shape[1]
    width = attended[0].shape[1]
    hidden = fc1.shape[1]

    def half(i, core):
        return jnp.where(i == 0, 1 - core[0], core[0])

    def in_all(i, core):
        return (chunk * 2 + half(i, core), 0)

    def in_chunk(i, core):
        return (half(i, core), 0)

    once = pl.BlockSpec((BLOCK, model), lambda i, core: (0, 0))
    kept = shape_of((BLOCK, model), F32)
    return call(
        feed_kernel,
        "feed",
        (2,),
        [pl.BlockSpec((BLOCK, model), in_all)] * 2
        + [pl.BlockSpec((BLOCK, width), in_chunk)] * 4
        + [whole((width, model))] * 4
        + [whole((1, model))] * 3
        + [whole((model, hidden)), whole((1, hidden)), whole((hidden, model))],
        [
            once,
            pl.BlockSpec((BLOCK, model), in_chunk),
            pl.BlockSpec((BLOCK, hidden), in_chunk),
            pl.BlockSpec((BLOCK, hidden), in_chunk),
            once,
            once,
            once,
            once,
            whole((8, model)),
        ],
        [
            kept,
            shape_of((2 * BLOCK, model), BF16),
            shape_of((2 * BLOCK, hidden), BF16),
            shape_of((2 * BLOCK, hidden), BF16),
            kept,
            kept,
            kept,
            kept,
            shape_of((8, model), F32),
        ],
        2 * 2 * BLOCK * model * (4 * width + 4 * hidden),
        scalars=1,
    )(core, x, dy, *attended, *out_weights, out_bias, gain, bias, fc1, fc1_bias, fc2)


def norm_back(grad, normal, factor, gain):
    scaled = grad * gain
    first = jnp.mean(scaled, axis=-1, keepdims=True)
    second = jnp.mean(scaled * normal, axis=-1, keepdims=True)
    return factor * (scaled - first - normal * second)


def second_back_kernel(core_ref, ours_ref, theirs_ref, middle_ref, dy_ref, gain_ref, grad_ref, low_ref, sums_ref):
    grad = ours_ref[...] + theirs_ref[...]
    normal, factor = normalize(middle_ref[...])
    total = dy_ref[...].astype(F32) + norm_back(grad, normal, factor, gain_ref[...])
    grad_ref[...] = total
    low = total.astype(BF16).astype(F32)
    low_ref[...] = low
    sums_ref[0:1, :] = jnp.sum(grad * normal, axis=0, keepdims=True)
    sums_ref[1:2, :] = jnp.sum(grad, axis=0, keepdims=True)
    sums_ref[2:3, :] = jnp.sum(low, axis=0, keepdims=True)


def second_back(core, chunk, ours, theirs, middle, dy, gain):
    model = ours.shape[1]
    block = pl.BlockSpec((BLOCK, model), lambda i, core: (0, 0))
    return call(
        second_back_kernel,
        "second_back",
        (1,),
        [
            block,
            block,
            block,
            pl.BlockSpec((BLOCK, model), lambda i, core: (chunk * 2 + core[0], 0)),
            whole((1, model)),
        ],
        [block, block, whole((8, model))],
        [shape_of((BLOCK, model), F32)] * 2 + [shape_of((8, model), F32)],
        BLOCK * model * 20,
        scalars=1,
    )(core, ours, theirs, middle, dy, gain)


def attend_back_kernel(
    core_ref, ours_ref, theirs_ref, w_ref, q_ref, k_ref, v_ref, total_ref, dk_in_ref, dv_in_ref,
    dq_ref, dk_ref, dv_ref, low_ref, grad_ref, *, first,
):
    step = pl.program_id(0)
    width = q_ref.shape[1]
    heads = width // HD

    @pl.when(step == 0)
    def _():
        grad_ref[...] = ours_ref[...].astype(BF16)
        if first:
            dk_ref[...] = jnp.zeros_like(dk_ref)
            dv_ref[...] = jnp.zeros_like(dv_ref)
        else:
            dk_ref[...] = dk_in_ref[...]
            dv_ref[...] = dv_in_ref[...]

    @pl.when(step == 1)
    def _():
        grad_ref[...] = theirs_ref[...].astype(BF16)

    grad = grad_ref[...]
    low_ref[...] = grad
    outer = nt(grad, w_ref[...].astype(BF16)).astype(BF16)
    scale = jnp.asarray(1.0 / math.sqrt(HD), BF16)
    dqs = []
    dks = []
    dvs = []
    for head in range(heads):
        at = slice(head * HD, (head + 1) * HD)
        queries = q_ref[:, at] * scale
        keys = k_ref[:, at]
        outer_here = outer[:, at]
        probs = jnp.exp(nt(keys, queries) - total_ref[head : head + 1, :])
        grad_probs = nt(v_ref[:, at], outer_here)
        inner = jnp.sum(probs * grad_probs, axis=0, keepdims=True)
        grad_scores = (probs * (grad_probs - inner)).astype(BF16)
        dvs.append(nn(probs.astype(BF16), outer_here))
        dks.append(nn(grad_scores, queries))
        dqs.append(tn(keys, grad_scores))
    dq_ref[...] = jnp.transpose(jnp.concatenate(dqs, axis=0) * (1.0 / math.sqrt(HD))).astype(BF16)
    dk_ref[...] = dk_ref[...] + jnp.concatenate(dks, axis=1)
    dv_ref[...] = dv_ref[...] + jnp.concatenate(dvs, axis=1)


def attend_back(core, chunk, ours, theirs, weight, queries, keys, values, totals, sums):
    rows, width = keys.shape
    model = ours.shape[1]
    first = sums is None
    if first:
        sums = [jnp.zeros((8, 128), F32)] * 2

    def half(i, core):
        return jnp.where(i == 0, core[0], 1 - core[0])

    block = pl.BlockSpec((BLOCK, model), lambda i, core: (0, 0))
    return call(
        functools.partial(attend_back_kernel, first=first),
        "attend_back",
        (2,),
        [
            block,
            block,
            whole((width, model)),
            pl.BlockSpec((BLOCK, width), lambda i, core: (chunk * 2 + half(i, core), 0)),
            whole((rows, width)),
            whole((rows, width)),
            pl.BlockSpec((8, BLOCK), lambda i, core: (0, half(i, core))),
            whole(sums[0].shape),
            whole(sums[1].shape),
        ],
        [
            pl.BlockSpec((BLOCK, width), lambda i, core: (half(i, core), 0)),
            whole((rows, width)),
            whole((rows, width)),
            pl.BlockSpec((BLOCK, model), lambda i, core: (half(i, core), 0)),
        ],
        [
            shape_of((2 * BLOCK, width), BF16),
            shape_of((rows, width), F32),
            shape_of((rows, width), F32),
            shape_of((2 * BLOCK, model), BF16),
        ],
        2 * 2 * BLOCK * rows * 256 * 5 * (width // HD),
        scalars=1,
        scratch=[pltpu.VMEM((BLOCK, model), BF16)],
    )(core, ours, theirs, weight, queries, keys, values, totals, *sums)


def first_grad_kernel(core_ref, *refs):
    step = pl.program_id(0)
    parts, weights, (send_ref, keep_ref) = refs[:6], refs[6:8], refs[8:]
    shares = []
    for group in range(2):
        share = None
        for part in range(3):
            term = nn(parts[3 * group + part][...].astype(BF16), weights[group][part].astype(BF16))
            share = term if share is None else share + term
        shares.append(share)
    total = shares[0] + shares[1]

    @pl.when(step < 2)
    def _():
        send_ref[...] = total

    @pl.when(step >= 2)
    def _():
        keep_ref[...] = total


def first_grad(core, groups, weights):
    rows, width = groups[0][1].shape
    model = weights[0].shape[2]

    def place(i, core):
        return ((i % 2) * 2 + jnp.where(i < 2, 1 - core[0], core[0]), 0)

    part = pl.BlockSpec((BLOCK, width), place)
    return call(
        first_grad_kernel,
        "first_grad",
        (4,),
        [part] * 6 + [whole(weights[0].shape)] * 2,
        [
            pl.BlockSpec((BLOCK, model), lambda i, core: (jnp.minimum(i, 1), 0)),
            pl.BlockSpec((BLOCK, model), lambda i, core: (jnp.maximum(i - 2, 0), 0)),
        ],
        [shape_of((rows // 2, model), F32)] * 2,
        2 * rows * width * 6 * model,
        scalars=1,
    )(core, *groups[0], *groups[1], *weights)


def first_back_kernel(core_ref, ours_ref, theirs_ref, x_ref, middle0_ref, middle1_ref, gain_ref, out_ref, sums_ref):
    step = pl.program_id(0)
    grad = ours_ref[...] + theirs_ref[...]
    normal, factor = normalize(x_ref[...].astype(F32))
    before = jnp.where(step == 0, middle0_ref[...], middle1_ref[...])
    total = before + norm_back(grad, normal, factor, gain_ref[...])
    out_ref[...] = total.astype(BF16).astype(F32)

    @pl.when(step == 0)
    def _():
        sums_ref[...] = jnp.zeros_like(sums_ref)

    sums_ref[0:1, :] = sums_ref[0:1, :] + jnp.sum(grad * normal, axis=0, keepdims=True)
    sums_ref[1:2, :] = sums_ref[1:2, :] + jnp.sum(grad, axis=0, keepdims=True)


def first_back(core, ours, theirs, x, middles, gain):
    rows, model = ours.shape
    block = pl.BlockSpec((BLOCK, model), lambda i, core: (i, 0))
    fixed = pl.BlockSpec((BLOCK, model), lambda i, core: (0, 0))
    return call(
        first_back_kernel,
        "first_back",
        (2,),
        [
            block,
            block,
            pl.BlockSpec((BLOCK, model), lambda i, core: (i * 2 + core[0], 0)),
            fixed,
            fixed,
            whole((1, model)),
        ],
        [block, whole((8, model))],
        [shape_of((rows, model), F32), shape_of((8, model), F32)],
        rows * model * 20,
        scalars=1,
    )(core, ours, theirs, x, *middles, gain)


def finish_kernel(core_ref, ours_ref, theirs_ref, out_ref):
    ours = (pl.program_id(0) % 2) == core_ref[0]

    @pl.when(ours)
    def _():
        out_ref[...] = ours_ref[...].astype(BF16)

    @pl.when(jnp.logical_not(ours))
    def _():
        out_ref[...] = theirs_ref[...].astype(BF16)


def finish(core, ours, theirs):
    rows, model = ours.shape
    block = pl.BlockSpec((BLOCK, model), lambda i, core: (i // 2, 0))
    return call(
        finish_kernel,
        "finish",
        (2 * rows // BLOCK,),
        [block, block],
        [pl.BlockSpec((BLOCK, model), lambda i, core: (i, 0))],
        [shape_of((2 * rows, model), BF16)],
        rows * model,
        scalars=1,
    )(core, ours, theirs)[0]


def gather_kernel(order_ref, piece_ref, out_ref):
    out_ref[...] = piece_ref[...].astype(BF16)


def place_pieces(order, pieces):
    count, rows, model = pieces.shape
    return call(
        gather_kernel,
        "place_pieces",
        (count,),
        [pl.BlockSpec((1, rows, model), lambda i, order: (order[i], 0, 0))],
        [pl.BlockSpec((1, rows, model), lambda i, order: (i, 0, 0))],
        [shape_of((count, rows, model), BF16)],
        count * rows * model,
        scalars=1,
    )(order, pieces)[0]


def body(
    tokens,
    ln1_gain,
    ln1_bias,
    qkv_weight,
    qkv_bias,
    out_weight,
    out_bias,
    ln2_gain,
    ln2_bias,
    fc1_weight,
    fc1_bias,
    fc2_weight,
    fc2_bias,
    cotangent,
    *,
    batch_count,
    tensor_count,
):
    rows, model = tokens.shape[1:]
    width = qkv_weight.shape[2]
    hidden = fc1_weight.shape[1]
    bits = batch_count.bit_length() - 1
    batch_at = lax.axis_index("batch")
    core_at = lax.axis_index("tensor") % 2
    core = core_at.astype(jnp.int32).reshape(1)

    def core_swap(v):
        return lax.ppermute(v, "tensor", [(i, i ^ 1) for i in range(tensor_count)])

    def chip_swap(v):
        return lax.ppermute(v, "tensor", [(i, i ^ 2) for i in range(tensor_count)])

    def batch_swap(v, bit):
        return lax.ppermute(v, "batch", [(i, i ^ (1 << bit)) for i in range(batch_count)])

    def scatter(v, order):
        axes = list(range(bits - 1, -1, -1))
        v = v.reshape((2,) * bits + v.shape[1:])
        for bit in order:
            axis = axes.index(bit)
            axes.pop(axis)
            mine = (batch_at >> bit) & 1
            sent = lax.dynamic_index_in_dim(v, 1 - mine, axis, keepdims=False)
            kept = lax.dynamic_index_in_dim(v, mine, axis, keepdims=False)
            v = kept + batch_swap(sent, bit)
        return v

    row = lambda v: v.reshape(1, -1)
    x = tokens.reshape(rows, model)
    dy = cotangent.reshape(rows, model)
    heads_weight = jnp.transpose(qkv_weight, (1, 2, 0))
    heads_bias = jnp.concatenate(
        [qkv_bias[0].reshape(-1), jnp.zeros((width,), F32), qkv_bias[1].reshape(-1)]
    )

    out_weight_wide = jnp.concatenate(
        [
            out_weight.astype(F32),
            jnp.pad(heads_bias, (0, 8 * model - 3 * width)).reshape(8, model),
        ]
    )
    out_weight_far = chip_swap(out_weight_wide)
    heads_bias_far = out_weight_far[width:].reshape(-1)[: 3 * width]
    out_weight_far = out_weight_far[:width]
    out_weight_core = core_swap(out_weight.astype(F32))
    out_weight_both = core_swap(out_weight_far)
    piece_rows = 3 * width // batch_count
    pieces = lax.dynamic_slice_in_dim(
        heads_weight.reshape(3 * width, model), batch_at * piece_rows, piece_rows, 0
    )
    pieces = chip_swap(pieces.astype(F32))[None]
    for bit in range(bits - 1, -1, -1):
        pieces = jnp.concatenate([pieces, batch_swap(pieces, bit)])
    places = []
    for m in range(batch_count):
        source = sum(((m >> j) & 1) << (bits - 1 - j) for j in range(bits))
        places.append(source)
    inverse = [0] * batch_count
    for m, source in enumerate(places):
        inverse[source] = m
    order = jnp.take(jnp.asarray(inverse, jnp.int32), jnp.arange(batch_count) ^ batch_at)
    heads_weight_far = place_pieces(order, pieces).reshape(3, width, model)

    left, queries, keys, values = project(
        x, row(ln1_gain), row(ln1_bias), heads_weight, row(heads_bias)
    )
    chunk_rows = 2 * BLOCK
    chunks = range(rows // chunk_rows)
    attended, totals, totals_far = [], [], []
    for chunk in chunks:
        mixed, logs = attend(queries, keys, values, chunk, chunk_rows)
        mixed_far = chip_swap(mixed)
        attended.append((mixed, mixed_far, core_swap(mixed), core_swap(mixed_far)))
        totals.append(logs)
        totals_far.append(chip_swap(logs))
    out_weights = (out_weight, out_weight_far, out_weight_core, out_weight_both)

    fed = []
    for chunk in chunks:
        fed.append(
            feed(
                core, chunk, x, dy, attended[chunk], out_weights, row(out_bias),
                row(ln2_gain), row(ln2_bias), fc1_weight, row(fc1_bias), fc2_weight,
            )
        )
    grad_fc1 = sum(tn(f[1], f[3]) for f in fed)
    grad_fc2 = sum(tn(dy[c * chunk_rows : (c + 1) * chunk_rows], f[2]) for c, f in zip(chunks, fed))
    grad_feed = jnp.concatenate([grad_fc1, grad_fc2], axis=1).reshape(
        batch_count, model // batch_count, 2 * hidden
    )
    grad_feed = scatter(grad_feed, [0] + list(range(1, bits)))

    queries_far, keys_far, values_far = project_again(left, heads_weight_far, row(heads_bias_far))

    middles, grads_low, small_sums = [], [], []
    for chunk in chunks:
        send, keep = fed[chunk][6:8]
        ours = keep + core_swap(send)
        grad, low, sums = second_back(core, chunk, ours, chip_swap(ours), fed[chunk][0], dy, row(ln2_gain))
        middles.append(grad)
        grads_low.append((low, core_swap(low)))
        small_sums.append(sums)

    res = []
    for chunk in chunks:
        send, keep = fed[chunk][4:6]
        ours = keep + core_swap(send)
        res.append(ours)
    res = jnp.concatenate(res)
    res = (jnp.concatenate([f[0] for f in fed]) + (res + chip_swap(res) + fc2_bias)).astype(BF16).astype(F32)
    res_other = core_swap(res)

    def back(weight, q, k, v, logs):
        parts = []
        sums = None
        for chunk in chunks:
            dq, dk, dv, low = attend_back(core, chunk, *grads_low[chunk], weight, q, k, v, logs[chunk], sums)
            sums = [dk, dv]
            parts.append((dq, low))
        return (
            jnp.concatenate([p[0] for p in parts]),
            sums[0].astype(BF16),
            sums[1].astype(BF16),
            [p[1] for p in parts],
        )

    dq, dk, dv, lows = back(out_weight, queries, keys, values, totals)
    grad_out = sum(tn(low, a[0].astype(BF16)) for low, a in zip(lows, attended))
    grad_heads = [tn(left, dq), tn(left, dk), tn(left, dv), grad_out]
    grad_heads = jnp.concatenate(grad_heads, axis=1).reshape(batch_count, model // batch_count, 4 * width)
    grad_heads = scatter(grad_heads, ([1, 0] + list(range(2, bits))))
    dq_far, dk_far, dv_far, _ = back(out_weight_far, queries_far, keys_far, values_far, totals_far)

    send, keep = first_grad(
        core, ((dq, dk, dv), (dq_far, dk_far, dv_far)), (heads_weight, heads_weight_far)
    )
    grad_rows, sums1 = first_back(core, keep, core_swap(send), x, middles, row(ln1_gain))
    grad_rows_other = core_swap(grad_rows)

    sums2 = sum(small_sums)
    vectors = jnp.stack(
        [sums2[2], sum(f[8][1] for f in fed), sums2[0], sums2[1], sums1[0], sums1[1]]
    )
    vectors = vectors + core_swap(vectors)
    fc1_sums = sum(f[8][0] for f in fed)
    dq_sums = jnp.sum(dq.astype(F32), axis=0)
    dv_sums = jnp.sum(dv.astype(F32), axis=0)
    share = HD // batch_count
    small = jnp.concatenate(
        [
            vectors.reshape(6, batch_count, -1).transpose(1, 0, 2).reshape(batch_count, -1),
            fc1_sums.reshape(-1, batch_count, share).transpose(1, 0, 2).reshape(batch_count, -1),
            jnp.stack([dq_sums, dv_sums])
            .reshape(-1, batch_count, share)
            .transpose(1, 0, 2)
            .reshape(batch_count, -1),
        ],
        axis=1,
    )
    small = scatter(small, list(range(bits)))
    piece = model // batch_count
    vectors = small[: 6 * piece].reshape(6, piece)
    hidden_heads = hidden // HD
    grad_fc1_bias = small[6 * piece : 6 * piece + hidden_heads * share].reshape(hidden_heads, share)
    grad_qkv_bias = small[6 * piece + hidden_heads * share :].reshape(2, width // HD, share)

    return (
        finish(core, res, res_other).reshape(tokens.shape),
        finish(core, grad_rows, grad_rows_other).reshape(tokens.shape),
        grad_heads[:, : 3 * width].reshape(piece, 3, width),
        grad_qkv_bias,
        grad_heads[:, 3 * width :].T,
        vectors[0],
        vectors[4],
        vectors[5],
        vectors[2],
        vectors[3],
        grad_feed[:, :hidden],
        grad_fc1_bias,
        grad_feed[:, hidden:].T,
        vectors[1],
    )


def solution(mesh):
    placed = (
        P("batch", None, None),
        P(),
        P(),
        P(None, None, "tensor"),
        P(None, "tensor", None),
        P("tensor", None),
        P(),
        P(),
        P(),
        P(None, "tensor"),
        P("tensor", None),
        P("tensor", None),
        P(),
        P("batch", None, None),
    )
    return jax.shard_map(
        functools.partial(
            body, batch_count=mesh.shape["batch"], tensor_count=mesh.shape["tensor"]
        ),
        mesh=mesh,
        in_specs=placed,
        out_specs=(
            P("batch", None, None),
            P("batch", None, None),
            P("batch", None, "tensor"),
            P(None, "tensor", "batch"),
            P("tensor", "batch"),
            P("batch"),
            P("batch"),
            P("batch"),
            P("batch"),
            P("batch"),
            P("batch", "tensor"),
            P("tensor", "batch"),
            P("tensor", "batch"),
            P("batch"),
        ),
        check_vma=False,
    )
```

```python
import functools
import math

import jax
import jax.numpy as jnp
from jax import lax
from jax.experimental import pallas as pl
from jax.experimental.pallas import tpu as pltpu
from jax.sharding import PartitionSpec as P

HD = 64
LN1_GAIN, LN1_BIAS, HEADS_BIAS, OUT_BIAS, LN2_GAIN, LN2_BIAS, FC1_BIAS, FC2_BIAS = range(8)
BLOCK = 256
EPSILON = 1e-06
F32 = jnp.float32
BF16 = jnp.bfloat16
VMEM_LIMIT = 20 * 1024 * 1024


def nn(a, b):
    return lax.dot_general(a, b, (((1,), (0,)), ((), ())), preferred_element_type=F32)


def nt(a, b):
    return lax.dot_general(a, b, (((1,), (1,)), ((), ())), preferred_element_type=F32)


def tn(a, b):
    return lax.dot_general(a, b, (((0,), (0,)), ((), ())), preferred_element_type=F32)


def call(kernel, name, out_shape, scalars=0, scratch=(), after=()):

    def run(*args):
        given = len(args)

        def inner(*refs):
            kernel(*refs[:given], *refs[given + len(after) :])

        return pl.pallas_call(
            inner,
            in_specs=[pl.BlockSpec(memory_space=pltpu.SMEM)] * scalars
            + [pl.BlockSpec(memory_space=pltpu.VMEM)] * (given - scalars)
            + [pl.BlockSpec(memory_space=pl.ANY)] * len(after),
            out_specs=[pl.BlockSpec(memory_space=pltpu.VMEM)] * len(out_shape),
            scratch_shapes=list(scratch),
            out_shape=out_shape,
            compiler_params=pltpu.CompilerParams(vmem_limit_bytes=VMEM_LIMIT),
            name=name,
        )(*args, *after)

    return run


def shape_of(shape, dtype):
    return jax.ShapeDtypeStruct(shape, dtype)


def vector(ref, row, width=None):
    return ref[row : row + 1, : ref.shape[1] if width is None else width]


def normalize(values):
    average = jnp.mean(values, axis=-1, keepdims=True)
    centered = values - average
    spread = jnp.mean(centered * centered, axis=-1, keepdims=True)
    factor = lax.rsqrt(spread + EPSILON)
    return centered * factor, factor


def half_of(core_ref, ref, offset=0, rows=None):
    size = ref.shape[0] // 2
    rows = size if rows is None else rows
    return pl.ds(pl.multiple_of(core_ref[0] * size + offset, BLOCK), rows)


def project_kernel(core_ref, x_ref, vec_ref, w_ref, other_ref, all_ref, q_ref, k_ref, v_ref):
    width = w_ref.shape[1]
    for start in range(0, x_ref.shape[0], BLOCK):
        at = slice(start, start + BLOCK)
        normal, _ = normalize(x_ref[at, :].astype(F32))
        all_ref[at, :] = (normal * vector(vec_ref, LN1_GAIN) + vector(vec_ref, LN1_BIAS)).astype(BF16)
    left = all_ref[...]
    mine = all_ref[half_of(core_ref, all_ref), :]
    bias_row = 3 * width + HEADS_BIAS
    biases = (vector(vec_ref, HEADS_BIAS), other_ref[bias_row : bias_row + 1, :])
    for group in range(2):
        for part, (ref, rows) in enumerate(((q_ref, mine), (k_ref, left), (v_ref, left))):
            span = slice(part * width, (part + 1) * width)
            weight = w_ref[part] if group == 0 else other_ref[span, :].astype(BF16)
            ref[:, group * width : (group + 1) * width] = (
                nt(rows, weight) + biases[group][:, span]
            ).astype(BF16)


def project(core, x, vectors, weight, other, after=()):
    rows, model = x.shape
    width = weight.shape[1]
    both = 2 * width
    return call(
        project_kernel,
        "project",
        [
            shape_of((rows, model), BF16),
            shape_of((rows // 2, both), BF16),
            shape_of((rows, both), BF16),
            shape_of((rows, both), BF16),
        ],
        scalars=1,
        after=after,
    )(core, x, vectors, weight, other)


def attend_kernel(q_ref, k_ref, v_ref, out_ref, other_ref, total_ref):
    heads = q_ref.shape[1] // HD
    scale = jnp.asarray(1.0 / math.sqrt(HD), BF16)
    parts = []
    logs = []
    for head in range(heads):
        at = slice(head * HD, (head + 1) * HD)
        scores = nt(q_ref[:, at] * scale, k_ref[:, at])
        peak = jnp.max(scores, axis=1, keepdims=True)
        powers = jnp.exp(scores - peak)
        totals = jnp.sum(powers, axis=1, keepdims=True)
        parts.append(nn(powers.astype(BF16), v_ref[:, at]) / totals)
        logs.append(peak + jnp.log(totals))
    mixed = jnp.concatenate(parts, axis=1).astype(BF16).astype(F32)
    out_ref[...] = mixed
    other_ref[...] = mixed[:, mixed.shape[1] // 2 :]
    logs.append(jnp.zeros((q_ref.shape[0], total_ref.shape[1] - heads), F32))
    total_ref[...] = jnp.concatenate(logs, axis=1)


def attend(queries, keys, values, after=()):
    rows, width = queries.shape
    return call(
        attend_kernel,
        "attend",
        [shape_of((rows, width), F32), shape_of((rows, width // 2), F32), shape_of((rows, 8), F32)],
        after=after,
    )(queries, keys, values)


def convert_kernel(*refs):
    half = len(refs) // 2
    for ref, out_ref in zip(refs[:half], refs[half:]):
        out_ref[...] = ref[...].astype(out_ref.dtype)


def convert(arrays, dtype, after=()):
    shapes = [shape_of(array.shape, dtype) for array in arrays]
    return call(convert_kernel, "convert", shapes, after=after)(*arrays)


ERF = (0.254829592, -0.284496736, 1.421413741, -1.453152027, 1.061405429)


def gelu_pair(values):
    size = jnp.abs(values) * (1.0 / math.sqrt(2.0))
    step = 1.0 / (1.0 + 0.3275911 * size)
    bell = jnp.exp(-(size * size))
    series = ERF[4]
    for factor in (ERF[3], ERF[2], ERF[1], ERF[0]):
        series = series * step + factor
    tail = (0.5 * step) * series * bell
    below = jnp.where(values >= 0, 1.0 - tail, tail)
    return values * below, below + values * (bell * (1.0 / math.sqrt(2.0 * math.pi)))


def feed_kernel(
    core_ref,
    x_ref,
    dy_ref,
    near_ref,
    far_ref,
    w0_ref,
    w1_ref,
    w2_ref,
    w3_ref,
    vec_ref,
    other_vec_ref,
    fc1_ref,
    fc2_ref,
    other_fc1_ref,
    other_fc2_ref,
    before_ref,
    middle_ref,
    left_ref,
    hidden_ref,
    pre_ref,
    swap_ref,
    res_ref,
    grad_ref,
    sums_ref,
    *,
    chunk,
):
    rows = slice(chunk * BLOCK, (chunk + 1) * BLOCK)
    place = half_of(core_ref, x_ref, chunk * BLOCK, BLOCK)
    width = w0_ref.shape[0]
    units = fc1_ref.shape[1]

    def share(ref, part, w_ref):
        return nn(ref[rows, part * width : (part + 1) * width].astype(BF16), w_ref[...].astype(BF16))

    branch = (share(near_ref, 0, w0_ref) + share(near_ref, 1, w1_ref)) + (
        share(far_ref, 0, w2_ref) + share(far_ref, 1, w3_ref)
    )
    middle = x_ref[place, :].astype(F32) + (branch + vector(vec_ref, OUT_BIAS))
    middle_ref[...] = middle
    normal, _ = normalize(middle)
    left = (normal * vector(vec_ref, LN2_GAIN) + vector(vec_ref, LN2_BIAS)).astype(BF16)
    left_ref[...] = left
    swap_ref[0:BLOCK, :] = left.astype(F32)
    dy = dy_ref[place, :]
    grad = res = None
    groups = ((vec_ref, FC1_BIAS, fc1_ref, fc2_ref), (other_vec_ref, 0, other_fc1_ref, other_fc2_ref))
    for group, (bias_ref, bias_row, in_ref, out_ref) in enumerate(groups):
        hidden, slope = gelu_pair(nn(left, in_ref[...]) + vector(bias_ref, bias_row, units))
        hidden = hidden.astype(BF16)
        pre = (nt(dy, out_ref[...]) * slope).astype(BF16)
        if group == 0:
            hidden_ref[...] = hidden
            pre_ref[...] = pre
        else:
            swap_ref[BLOCK : 2 * BLOCK, :] = pre.astype(F32)
            swap_ref[2 * BLOCK : 3 * BLOCK, :] = hidden.astype(F32)
        back = nt(pre, in_ref[...])
        fed = nn(hidden, out_ref[...])
        grad = back if grad is None else grad + back
        res = fed if res is None else res + fed
    if chunk == 0:
        grad_ref[...] = grad
    else:
        grad_ref[:BLOCK, :] = before_ref[...]
        grad_ref[BLOCK:, :] = grad
    res_ref[...] = res
    sums_ref[0:1, :] = jnp.sum(dy.astype(F32), axis=0, keepdims=True)


def feed(core, chunk, x, dy, near, far, out_weights, vectors, other_bias, fc1, fc2, other, before, after=()):
    model = x.shape[1]
    units = fc1.shape[1]
    rows = shape_of((BLOCK, model), F32)
    wide = shape_of((BLOCK, units), BF16)
    swap = shape_of((3 * BLOCK + (8 if chunk == 0 else 0), model), F32)
    grad = shape_of(((chunk + 1) * BLOCK, model), F32)
    return call(
        functools.partial(feed_kernel, chunk=chunk),
        "feed",
        [rows, shape_of((BLOCK, model), BF16), wide, wide, swap, rows, grad, shape_of((8, model), F32)],
        scalars=1,
        after=after,
    )(core, x, dy, near, far, *out_weights, vectors, other_bias, fc1, fc2, *other, before)


def cut_pieces(ref, send_ref, keep_ref, mine, count, axis_bits, axis):
    rows = ref.shape[0] // count
    stride = 1 << (axis_bits - 1 - axis)
    for value in range(2):

        @pl.when(mine == value)
        def _():
            for index in range(count):
                place = (index // (2 * stride)) * stride + index % stride
                out = keep_ref if (index // stride) % 2 == value else send_ref
                out[place * rows : (place + 1) * rows, :] = ref[index * rows : (index + 1) * rows, :]


def cut_spans(total_ref, refs, mine_ref, spans, count, axes):
    axis_bits = count.bit_length() - 1
    for index, (span, axis) in enumerate(zip(spans, axes)):
        cut_pieces(
            total_ref.at[:, span], refs[2 * index], refs[2 * index + 1], mine_ref[index], count,
            axis_bits, axis,
        )


def cut_shapes(rows, spans):
    shapes = []
    for span in spans:
        shapes += [shape_of((rows // 2, span.stop - span.start), F32)] * 2
    return shapes


def column_sum(values):
    return jnp.sum(values.astype(F32), axis=0, keepdims=True)


def fc2_grad_kernel(core_ref, mine_ref, dy_ref, *refs, spans, count, axes):
    hiddens, swaps, total_ref = refs[0:2], refs[2:4], refs[-1]
    total = None
    for chunk in range(2):
        for ref, half, at in (
            (hiddens[chunk], core_ref[0], 0),
            (swaps[chunk], 1 - core_ref[0], 2 * BLOCK),
        ):
            place = half * (dy_ref.shape[0] // 2) + chunk * BLOCK
            rows = dy_ref[pl.ds(pl.multiple_of(place, BLOCK), BLOCK), :]
            term = tn(rows, ref[at : at + BLOCK, :].astype(BF16))
            total = term if total is None else total + term
    total_ref[...] = total
    cut_spans(total_ref, refs[4:-1], mine_ref, spans, count, axes)


def fc1_grad_kernel(core_ref, mine_ref, *refs, spans, count, axes):
    lefts, pres, swaps, sums_ref, total_ref = refs[0:2], refs[2:4], refs[4:6], refs[-2], refs[-1]
    total = None
    sums = 0.0
    for chunk in range(2):
        theirs = swaps[chunk]
        for left, pre in (
            (lefts[chunk][...], pres[chunk][...]),
            (theirs[0:BLOCK, :].astype(BF16), theirs[BLOCK : 2 * BLOCK, :].astype(BF16)),
        ):
            term = tn(left, pre)
            total = term if total is None else total + term
            sums = sums + column_sum(pre)
    total_ref[...] = total
    sums_ref[0:1, :] = sums
    cut_spans(total_ref, refs[6:-2], mine_ref, spans, count, axes)


def heads_grad_kernel(
    core_ref, mine_ref, left_ref, ours_ref, theirs_ref, low_ref, low_other_ref, near_ref, near_other_ref,
    *refs, spans, count, axes,
):
    sums_ref, total_ref = refs[-2:]
    rows = left_ref.shape[0] // 2
    width = near_other_ref.shape[1]
    ours, theirs = ours_ref[...], theirs_ref[...].astype(BF16)
    left = left_ref[half_of(core_ref, left_ref), :]
    left_other = left_ref[pl.ds(pl.multiple_of((1 - core_ref[0]) * rows, BLOCK), rows), :]
    total_ref[:, : 3 * width] = tn(left, ours) + tn(left_other, theirs)
    total_ref[:, 3 * width :] = tn(low_ref[...], near_ref[:, :width].astype(BF16)) + tn(
        low_other_ref[...].astype(BF16), near_other_ref[...].astype(BF16)
    )
    sums_ref[...] = jnp.zeros_like(sums_ref)
    sums_ref[0:1, : 3 * width] = column_sum(ours) + column_sum(theirs)
    cut_spans(total_ref, refs[:-2], mine_ref, spans, count, axes)


def weight_grad(kernel, core, mine, operands, model, width, spans, count, axes, sums=True, after=()):
    return call(
        functools.partial(kernel, spans=spans, count=count, axes=axes),
        "weight_grad",
        cut_shapes(model, spans) + ([shape_of((8, model), F32)] if sums else []),
        scalars=2,
        scratch=[pltpu.VMEM((model, width), F32)],
        after=after,
    )(core, mine, *operands)


def hop_kernel(mine_ref, *refs, pairs, spans, count, axes):
    total_ref = refs[-1]
    at = 0
    for pair in range(pairs):
        ours, theirs = refs[2 * pair], refs[2 * pair + 1]
        total_ref[:, at : at + ours.shape[1]] = ours[...] + theirs[...]
        at += ours.shape[1]
    cut_spans(total_ref, refs[2 * pairs : -1], mine_ref, spans, count, axes)


def hop(mine, pairs, count, axis, after=()):
    operands = [array for pair in pairs for array in pair]
    rows = operands[0].shape[0]
    width = sum(pair[0].shape[1] for pair in pairs)
    spans = [slice(0, width)]
    return call(
        functools.partial(hop_kernel, pairs=len(pairs), spans=spans, count=count, axes=[axis]),
        "hop",
        cut_shapes(rows, spans),
        scalars=1,
        scratch=[pltpu.VMEM((rows, width), F32)],
        after=after,
    )(mine, *operands)


def norm_back(grad, normal, factor, gain):
    scaled = grad * gain
    first = jnp.mean(scaled, axis=-1, keepdims=True)
    second = jnp.mean(scaled * normal, axis=-1, keepdims=True)
    return factor * (scaled - first - normal * second)


def second_back_kernel(core_ref, *refs):
    ours_ref, theirs_ref, middles = refs[0], refs[1], refs[2:4]
    res_ref, dy_ref, vec_ref, grad_ref, low_ref, wide_ref, res_out_ref, sums_ref = refs[4:]
    res_out_ref[0 : res_ref.shape[0], :] = res_ref[...]
    all_sums = [0.0, 0.0, 0.0]
    for chunk in range(2):
        rows = slice(chunk * BLOCK, (chunk + 1) * BLOCK)
        grad = ours_ref[rows, :] + theirs_ref[rows, :]
        normal, factor = normalize(middles[chunk][...])
        dy = dy_ref[half_of(core_ref, dy_ref, chunk * BLOCK, BLOCK), :].astype(F32)
        total = dy + norm_back(grad, normal, factor, vector(vec_ref, LN2_GAIN))
        grad_ref[rows, :] = total
        low = total.astype(BF16)
        low_ref[rows, :] = low
        wide_ref[rows, :] = low.astype(F32)
        for index, term in enumerate((grad * normal, grad, low.astype(F32))):
            all_sums[index] = all_sums[index] + jnp.sum(term, axis=0, keepdims=True)
    for index, total in enumerate(all_sums):
        sums_ref[index : index + 1, :] = total


def second_back(core, ours, theirs, middles, res, dy, vectors, after=()):
    rows, model = ours.shape
    return call(
        second_back_kernel,
        "second_back",
        [
            shape_of((rows, model), F32),
            shape_of((rows, model), BF16),
            shape_of((rows, model), F32),
            shape_of((res.shape[0] + 8, model), F32),
            shape_of((8, model), F32),
        ],
        scalars=1,
        after=after,
    )(core, ours, theirs, *middles, res, dy, vectors)


def attend_back_kernel(
    core_ref, low_ref, w0_ref, w1_ref, q_ref, k_ref, v_ref, total_ref, dq_ref, dk_send_ref, dv_send_ref, dk_ref, dv_ref,
    scratch_ref,
):
    heads = q_ref.shape[1] // HD
    scale = jnp.asarray(1.0 / math.sqrt(HD), BF16)
    low = low_ref[...]
    outers = [nt(low, ref[...]).astype(BF16) for ref in (w0_ref, w1_ref)]
    outer = jnp.concatenate(outers, axis=1)
    dqs = []
    dks = []
    dvs = []
    for head in range(heads):
        at = slice(head * HD, (head + 1) * HD)
        queries = q_ref[:, at] * scale
        keys = k_ref[:, at]
        outer_here = outer[:, at]
        probs = jnp.exp(nt(queries, keys) - total_ref[:, head : head + 1])
        grad_probs = nt(outer_here, v_ref[:, at])
        inner = jnp.sum(probs * grad_probs, axis=1, keepdims=True)
        grad_scores = (probs * (grad_probs - inner)).astype(BF16)
        dvs.append(tn(outer_here, probs.astype(BF16)))
        dks.append(tn(queries, grad_scores))
        dqs.append(nn(grad_scores, keys))
    dq_ref[...] = (jnp.concatenate(dqs, axis=1) * (1.0 / math.sqrt(HD))).astype(BF16)
    for parts, send_ref, keep_ref in ((dks, dk_send_ref, dk_ref), (dvs, dv_send_ref, dv_ref)):
        scratch_ref[...] = jnp.transpose(jnp.concatenate(parts, axis=0))
        rows = scratch_ref.shape[0] // 2
        for ref, half in ((send_ref, 1 - core_ref[0]), (keep_ref, core_ref[0])):
            ref[...] = scratch_ref[pl.ds(pl.multiple_of(half * rows, BLOCK), rows), :]


def attend_back(core, low, out_weights, queries, keys, values, totals, after=()):
    rows, width = keys.shape
    half = shape_of((rows // 2, width), F32)
    return call(
        attend_back_kernel,
        "attend_back",
        [shape_of((rows // 2, width), BF16), half, half, half, half],
        scalars=1,
        scratch=[pltpu.VMEM((rows, width), F32)],
        after=after,
    )(core, low, *out_weights, queries, keys, values, totals)


def first_grad_kernel(dq_ref, dk_ref, dv_ref, dk_other_ref, dv_other_ref, w_ref, other_ref, out_ref, own_ref, send_ref):
    width = w_ref.shape[1]
    total = None
    for part in range(3):
        for group in range(2):
            if part == 0:
                values = dq_ref[:, group * width : (group + 1) * width]
            else:
                ours_ref, theirs_ref = ((dk_ref, dk_other_ref), (dv_ref, dv_other_ref))[part - 1]
                at, other = group * width, (1 - group) * width
                values = ours_ref[:, at : at + width] + theirs_ref[:, other : other + width]
                values = values.astype(BF16)
            span = slice(part * width, (part + 1) * width)
            if group == 0:
                own_ref[:, span] = values
                term = nn(values, w_ref[part])
            else:
                send_ref[:, span] = values.astype(F32)
                term = nn(values, other_ref[span, :].astype(BF16))
            total = term if total is None else total + term
    out_ref[...] = total


def first_grad(dq, ours, theirs, weight, other, after=()):
    rows = dq.shape[0]
    _, width, model = weight.shape
    return call(
        first_grad_kernel,
        "first_grad",
        [
            shape_of((rows, model), F32),
            shape_of((rows, 3 * width), BF16),
            shape_of((rows, 3 * width), F32),
        ],
        after=after,
    )(dq, *ours, *theirs, weight, other)


def first_back_kernel(
    core_ref, ours_ref, theirs_ref, x_ref, middle_ref, vec_ref, res_ref, out_ref, sums_ref, res_out_ref
):
    res_out_ref[...] = res_ref[...]
    gain_sum = bias_sum = 0.0
    for start in range(0, ours_ref.shape[0], BLOCK):
        at = slice(start, start + BLOCK)
        grad = ours_ref[at, :] + theirs_ref[at, :]
        normal, factor = normalize(x_ref[half_of(core_ref, x_ref, start, BLOCK), :].astype(F32))
        total = middle_ref[at, :] + norm_back(grad, normal, factor, vector(vec_ref, LN1_GAIN))
        out_ref[at, :] = total.astype(BF16).astype(F32)
        gain_sum = gain_sum + jnp.sum(grad * normal, axis=0, keepdims=True)
        bias_sum = bias_sum + jnp.sum(grad, axis=0, keepdims=True)
    sums_ref[0:1, :] = gain_sum
    sums_ref[1:2, :] = bias_sum


def first_back(core, ours, theirs, x, middle, vectors, res, after=()):
    rows, model = ours.shape
    return call(
        first_back_kernel,
        "first_back",
        [shape_of((rows, model), F32), shape_of((8, model), F32), shape_of(res.shape, F32)],
        scalars=1,
        after=after,
    )(core, ours, theirs, x, middle, vectors, res)


def result_kernel(ours_ref, theirs_ref, middle_ref, vec_ref, out_ref):
    rows = slice(0, middle_ref.shape[0])
    fed = ours_ref[rows, :] + theirs_ref[rows, :] + vector(vec_ref, FC2_BIAS)
    out_ref[...] = (middle_ref[...] + fed).astype(BF16).astype(F32)


def result_rows(ours, theirs, middle, vectors, after=()):
    return call(result_kernel, "result_rows", [shape_of(middle.shape, F32)], after=after)(
        ours, theirs, middle, vectors
    )[0]


def finish_kernel(core_ref, *refs):
    out_ref = refs[-1]
    for part, half in ((0, core_ref[0]), (1, 1 - core_ref[0])):
        at = 0
        for ref in refs[part:-1:2]:
            place = pl.multiple_of(half * (out_ref.shape[0] // 2) + at, BLOCK)
            out_ref[pl.ds(place, ref.shape[0]), :] = ref[...].astype(BF16)
            at += ref.shape[0]


def finish(core, pairs, after=()):
    operands = [array for pair in pairs for array in pair]
    shape = (sum(array.shape[0] for array in operands), operands[0].shape[1])
    return call(
        finish_kernel, "finish", [shape_of(shape, BF16)], scalars=1, after=after
    )(core, *operands)[0]


def feed_sum_kernel(ours_ref, theirs_ref, fc2_ref, fc1_ref):
    units = fc2_ref.shape[1]
    total = ours_ref[...] + theirs_ref[...]
    fc2_ref[...] = total[:, :units]
    fc1_ref[...] = total[:, units:]


def feed_sum(ours, theirs, after=()):
    half = shape_of((ours.shape[0], ours.shape[1] // 2), F32)
    return call(feed_sum_kernel, "feed_sum", [half, half], after=after)(ours, theirs)


def heads_sum_kernel(ours_ref, theirs_ref, heads_ref, out_ref):
    width = heads_ref.shape[2]
    total = ours_ref[...] + theirs_ref[...]
    for part in range(3):
        heads_ref[part] = total[:, part * width : (part + 1) * width]
    out_ref[...] = jnp.transpose(total[:, 3 * width :])


def heads_sum(ours, theirs, after=()):
    rows, width = ours.shape[0], ours.shape[1] // 4
    shapes = [shape_of((3, rows, width), F32), shape_of((width, rows), F32)]
    return call(heads_sum_kernel, "heads_sum", shapes, after=after)(ours, theirs)


def body(
    tokens,
    ln1_gain,
    ln1_bias,
    qkv_weight,
    qkv_bias,
    out_weight,
    out_bias,
    ln2_gain,
    ln2_bias,
    fc1_weight,
    fc1_bias,
    fc2_weight,
    fc2_bias,
    cotangent,
    *,
    batch_count,
    tensor_count,
):
    rows, model = tokens.shape[1:]
    width = qkv_weight.shape[2]
    units = fc1_weight.shape[1]
    bits = batch_count.bit_length() - 1
    batch_at = lax.axis_index("batch")
    core = (lax.axis_index("tensor") % 2).astype(jnp.int32).reshape(1)

    def core_swap(v):
        return lax.ppermute(v, "tensor", [(i, i ^ 1) for i in range(tensor_count)])

    def chip_swap(v):
        return lax.ppermute(v, "tensor", [(i, i ^ 2) for i in range(tensor_count)])

    def batch_swap(v, bit):
        return lax.ppermute(v, "batch", [(i, i ^ (1 << bit)) for i in range(batch_count)])

    last = []

    def then(made, *others):
        last[:] = [made[0], *others]
        return made

    orders = ([0, *range(1, bits)], [1, 0, *range(2, bits)])

    def mine_of(some):
        return jnp.stack([(batch_at >> bit) & 1 for bit in some]).astype(jnp.int32)

    class Scatter:
        def __init__(self, cut, order, left=range(bits - 1, -1, -1)):
            self.order = list(order)
            self.left = list(left)
            self.cross(cut)

        def cross(self, cut):
            send, self.keep = cut
            bit = self.order.pop(0)
            self.left.remove(bit)
            self.theirs = batch_swap(send, bit)

        def step(self, *others):
            bit = self.order[0]
            pairs = [(v.keep, v.theirs) for v in (self, *others)]
            self.cross(
                then(hop(mine_of([bit]), pairs, 1 << len(self.left), self.left.index(bit), after=last))
            )

        def end(self, summed):
            while self.order:
                self.step()
            return then(summed(self.keep, self.theirs, after=last))

    def weight_scatters(kernel, operands, width, orders, sums=True):
        span = width // len(orders)
        spans = [slice(i * span, (i + 1) * span) for i in range(len(orders))]
        firsts = [order[0] for order in orders]
        made = then(
            weight_grad(
                kernel, core, mine_of(firsts), operands, model, width, spans, batch_count,
                [bits - 1 - bit for bit in firsts], sums=sums, after=last,
            )
        )
        return [Scatter(made[2 * i : 2 * i + 2], order) for i, order in enumerate(orders)], made[-1]

    x = tokens.reshape(rows, model)
    dy = cotangent.reshape(rows, model)
    heads_weight = jnp.transpose(qkv_weight, (1, 2, 0))
    heads_bias = jnp.concatenate(
        [qkv_bias[0].reshape(-1), jnp.zeros((width,), F32), qkv_bias[1].reshape(-1)]
    )
    listed = (ln1_gain, ln1_bias, heads_bias, out_bias, ln2_gain, ln2_bias, fc1_bias, fc2_bias)
    vectors = jnp.concatenate(
        [jnp.pad(v.reshape(-1), (0, model - v.size)) for v in listed]
    ).reshape(8, model)

    heads_wide = jnp.concatenate([heads_weight.reshape(3 * width, model).astype(F32), vectors])
    heads_other = core_swap(heads_wide)
    out_weight_wide = out_weight.astype(F32)
    out_weight_far = chip_swap(out_weight_wide)
    others = then(
        convert([fc1_weight, fc2_weight, out_weight], F32, after=[heads_wide, out_weight_wide])
    )
    others = [core_swap(v) for v in others]
    other_bias = heads_other[3 * width + FC1_BIAS :]

    left, queries, keys, values = then(
        project(core, x, vectors, heads_weight, heads_other, after=last)
    )
    near, near_send, totals = then(attend(queries, keys, values, after=last))
    far = chip_swap(near)
    fc1_other, fc2_other, out_weight_other = then(convert(others, BF16, after=last))
    out_weight_both = core_swap(out_weight_far)
    out_weights = (out_weight, out_weight_other, out_weight_far, out_weight_both)
    near_other = core_swap(near_send)
    last.append(near_other)

    fed = []
    before = vectors
    for chunk in range(2):
        fed.append(
            then(
                feed(
                    core, chunk, x, dy, near, far, out_weights, vectors, other_bias, fc1_weight,
                    fc2_weight, (fc1_other, fc2_other), before, after=last,
                )
            )
        )
        before = fed[chunk][6]
    middles, lefts, hiddens, pres, swaps, res, grads, feed_sums = zip(*fed)
    grads = grads[1]
    grads_far = chip_swap(grads)
    swaps = [core_swap(v) for v in swaps]
    (fc2,), _ = weight_scatters(
        fc2_grad_kernel, [dy, *hiddens, *swaps], units, orders[1:], sums=False
    )
    (fc1,), fc1_sums = weight_scatters(
        fc1_grad_kernel, [*lefts, *pres, *swaps], units, orders[:1]
    )

    grad_middle, low, low_wide, res0, second_sums = then(
        second_back(core, grads, grads_far, middles, res[0], dy, vectors, after=last)
    )
    res0_far = chip_swap(res0)
    low_other = core_swap(low_wide)
    fc2.step()
    fc1.step()
    dq, dk_send, dv_send, dk, dv = then(
        attend_back(
            core, low, (out_weight, out_weight_other), queries, keys, values, totals, after=last
        )
    )
    theirs = core_swap(dk_send), core_swap(dv_send)
    grad_rows, heads_own, send = then(
        first_grad(
            dq, (dk, dv), theirs, heads_weight, heads_other, after=[*last, low_other, res0_far]
        )
    )
    grad_rows_far = chip_swap(grad_rows)
    heads_theirs = core_swap(send)
    heads, heads_sums = weight_scatters(
        heads_grad_kernel,
        [left, heads_own, heads_theirs, low, low_other, near, near_other],
        4 * width,
        orders,
    )
    result0 = then([result_rows(res0, res0_far, middles[0], vectors, after=last)])[0]
    result0_other = core_swap(result0)
    fc2.step(fc1)
    heads[0].step()
    heads[1].step()
    heads[0].step(heads[1])
    grad_fc2, grad_fc1 = fc2.end(feed_sum)
    grad_rows, norm_sums, res1 = then(
        first_back(core, grad_rows, grad_rows_far, x, grad_middle, vectors, res[1], after=last)
    )
    grad_rows_other = core_swap(grad_rows)
    res1_far = chip_swap(res1)
    grad_tokens = then([finish(core, [(grad_rows, grad_rows_other)], after=last)])[0]
    grad_heads, grad_out = heads[0].end(heads_sum)

    small = jnp.concatenate(
        [second_sums[2:3], feed_sums[0][:1] + feed_sums[1][:1], second_sums[:2], norm_sums[:2]]
    )
    small = jnp.concatenate([small + core_swap(small), fc1_sums[:1], heads_sums[:1]])
    for bit in range(bits):
        small = small + batch_swap(small, bit)
    last.append(small)
    result1 = then([result_rows(res1, res1_far, middles[1], vectors, after=last)])[0]
    result1_other = core_swap(result1)
    result = then(
        [finish(core, [(result0, result0_other), (result1, result1_other)], after=last)]
    )[0]
    share = HD // batch_count
    piece = model // batch_count
    shared = lax.dynamic_slice_in_dim(small[:6], batch_at * piece, piece, 1)
    own = lax.dynamic_slice_in_dim(
        small[6:].reshape(2, model // HD, HD), batch_at * share, share, 2
    )
    return (
        result.reshape(tokens.shape),
        grad_tokens.reshape(tokens.shape),
        jnp.transpose(grad_heads, (1, 0, 2)),
        own[1, : 3 * width // HD].reshape(3, width // HD, share)[::2],
        grad_out,
        shared[0],
        shared[4],
        shared[5],
        shared[2],
        shared[3],
        grad_fc1,
        own[0, : units // HD],
        grad_fc2.T,
        shared[1],
    )


def solution(mesh):
    placed = (
        P("batch", None, None),
        P(),
        P(),
        P(None, None, "tensor"),
        P(None, "tensor", None),
        P("tensor", None),
        P(),
        P(),
        P(),
        P(None, "tensor"),
        P("tensor", None),
        P("tensor", None),
        P(),
        P("batch", None, None),
    )
    return jax.shard_map(
        functools.partial(
            body, batch_count=mesh.shape["batch"], tensor_count=mesh.shape["tensor"]
        ),
        mesh=mesh,
        in_specs=placed,
        out_specs=(
            P("batch", None, None),
            P("batch", None, None),
            P("batch", None, "tensor"),
            P(None, "tensor", "batch"),
            P("tensor", "batch"),
            P("batch"),
            P("batch"),
            P("batch"),
            P("batch"),
            P("batch"),
            P("batch", "tensor"),
            P("tensor", "batch"),
            P("tensor", "batch"),
            P("batch"),
        ),
        check_vma=False,
    )
```

```python
import functools
import math

import jax
import jax.numpy as jnp
from jax import lax
from jax.experimental import pallas as pl
from jax.experimental.pallas import tpu as pltpu
from jax.sharding import PartitionSpec as P

HD = 64
LN1_GAIN, LN1_BIAS, HEADS_BIAS, OUT_BIAS, LN2_GAIN, LN2_BIAS, FC1_BIAS, FC2_BIAS = range(8)
BLOCK = 256
EPSILON = 1e-06
F32 = jnp.float32
BF16 = jnp.bfloat16


def nn(a, b):
    return lax.dot_general(a, b, (((1,), (0,)), ((), ())), preferred_element_type=F32)


def nt(a, b):
    return lax.dot_general(a, b, (((1,), (1,)), ((), ())), preferred_element_type=F32)


def tn(a, b):
    return lax.dot_general(a, b, (((0,), (0,)), ((), ())), preferred_element_type=F32)


def call(kernel, name, out_shape, scalars=0, scratch=(), after=(), far_in=(), far_out=(), vmem=20):

    def run(*args):
        given = len(args)
        ins = [scalars + index for index in far_in]
        outs = list(far_out)
        made = len(out_shape)

        def inner(*refs):
            first = given + len(after)
            operands, results = list(refs[:given]), list(refs[first : first + made])
            held = list(refs[first + made : first + made + len(scratch)])
            spare = list(refs[first + made + len(scratch) :])
            sems = spare.pop() if spare else None
            copies = []
            for count, index in enumerate(ins):
                copies.append(pltpu.make_async_copy(operands[index], spare[count], sems.at[count]))
                operands[index] = spare[count]
            for copy in copies:
                copy.start()
            far = [results[index] for index in outs]
            for count, index in enumerate(outs):
                results[index] = spare[len(ins) + count]
            for copy in copies:
                copy.wait()
            kernel(*operands, *results, *held)
            copies = []
            for count, ref in enumerate(far, len(ins)):
                copies.append(pltpu.make_async_copy(spare[count], ref, sems.at[count]))
            for copy in copies:
                copy.start()
            for copy in copies:
                copy.wait()

        def space(index, chosen):
            return pl.BlockSpec(memory_space=pltpu.HBM if index in chosen else pltpu.VMEM)

        moved = [args[index] for index in ins] + [out_shape[index] for index in outs]
        held = list(scratch) + [pltpu.VMEM(v.shape, v.dtype) for v in moved]
        if moved:
            held.append(pltpu.SemaphoreType.DMA((len(moved),)))
        return pl.pallas_call(
            inner,
            in_specs=[pl.BlockSpec(memory_space=pltpu.SMEM)] * scalars
            + [space(index, ins) for index in range(scalars, given)]
            + [pl.BlockSpec(memory_space=pl.ANY)] * len(after),
            out_specs=[space(index, outs) for index in range(made)],
            scratch_shapes=held,
            out_shape=out_shape,
            compiler_params=pltpu.CompilerParams(vmem_limit_bytes=vmem * 1024 * 1024),
            name=name,
        )(*args, *after)

    return run


def shape_of(shape, dtype):
    return jax.ShapeDtypeStruct(shape, dtype)


def vector(ref, row, width=None):
    return ref[row : row + 1, : ref.shape[1] if width is None else width]


def normalize(values):
    average = jnp.mean(values, axis=-1, keepdims=True)
    centered = values - average
    spread = jnp.mean(centered * centered, axis=-1, keepdims=True)
    factor = lax.rsqrt(spread + EPSILON)
    return centered * factor, factor


def half_of(core_ref, ref, offset=0, rows=None):
    size = ref.shape[0] // 2
    rows = size if rows is None else rows
    return pl.ds(pl.multiple_of(core_ref[0] * size + offset, 128), rows)


def pack_kernel(
    g1_ref, b1_ref, bias_ref, ob_ref, g2_ref, b2_ref, fc1_bias_ref, fb_ref, w_ref, out_w_ref,
    vec_ref, wide_ref, out_wide_ref,
):
    width = w_ref.shape[1]
    vec_ref[...] = jnp.zeros_like(vec_ref)
    for row, ref in (
        (LN1_GAIN, g1_ref),
        (LN1_BIAS, b1_ref),
        (OUT_BIAS, ob_ref),
        (LN2_GAIN, g2_ref),
        (LN2_BIAS, b2_ref),
        (FC2_BIAS, fb_ref),
    ):
        vec_ref[row : row + 1, :] = ref[...].reshape(1, -1)
    for head in range(bias_ref.shape[0]):
        for part, start in ((0, 0), (1, 2 * width)):
            at = start + head * HD
            vec_ref[HEADS_BIAS : HEADS_BIAS + 1, at : at + HD] = bias_ref[head, part : part + 1, :]
    for head in range(fc1_bias_ref.shape[0]):
        at = slice(head * HD, (head + 1) * HD)
        vec_ref[FC1_BIAS : FC1_BIAS + 1, at] = fc1_bias_ref[head : head + 1, :]
    for part in range(3):
        wide_ref[part * width : (part + 1) * width, :] = w_ref[part].astype(F32)
    wide_ref[3 * width :, :] = vec_ref[...]
    out_wide_ref[0:width, :] = out_w_ref[...].astype(F32)


def pack(listed, heads_weight, out_weight):
    width, model = out_weight.shape
    return call(
        pack_kernel,
        "pack",
        [
            shape_of((8, model), F32),
            shape_of((3 * width + 8, model), F32),
            shape_of((width + 8, model), F32),
        ],
        vmem=60,
    )(*listed, heads_weight, out_weight)


def project_kernel(core_ref, x_ref, vec_ref, w_ref, other_ref, all_ref, q_ref, k_ref, v_ref):
    width = w_ref.shape[1]
    for start in range(0, x_ref.shape[0], BLOCK):
        at = slice(start, start + BLOCK)
        normal, _ = normalize(x_ref[at, :].astype(F32))
        all_ref[at, :] = (normal * vector(vec_ref, LN1_GAIN) + vector(vec_ref, LN1_BIAS)).astype(BF16)
    left = all_ref[...]
    mine = all_ref[half_of(core_ref, all_ref), :]
    bias_row = 3 * width + HEADS_BIAS
    biases = (vector(vec_ref, HEADS_BIAS), other_ref[bias_row : bias_row + 1, :])
    for group in range(2):
        for part, (ref, rows) in enumerate(((q_ref, mine), (k_ref, left), (v_ref, left))):
            span = slice(part * width, (part + 1) * width)
            weight = w_ref[part] if group == 0 else other_ref[span, :].astype(BF16)
            ref[:, group * width : (group + 1) * width] = (
                nt(rows, weight) + biases[group][:, span]
            ).astype(BF16)


def project(core, x, vectors, weight, other, after=()):
    rows, model = x.shape
    width = weight.shape[1]
    both = 2 * width
    return call(
        project_kernel,
        "project",
        [
            shape_of((rows, model), BF16),
            shape_of((rows // 2, both), BF16),
            shape_of((rows, both), BF16),
            shape_of((rows, both), BF16),
        ],
        scalars=1,
        after=after,
    )(core, x, vectors, weight, other)


def attend_kernel(q_ref, k_ref, v_ref, out_ref, total_ref):
    heads = q_ref.shape[1] // HD
    scale = jnp.asarray(1.0 / math.sqrt(HD), BF16)
    parts = []
    logs = []
    for head in range(heads):
        at = slice(head * HD, (head + 1) * HD)
        scores = nt(q_ref[:, at] * scale, k_ref[:, at])
        peak = jnp.max(scores, axis=1, keepdims=True)
        powers = jnp.exp(scores - peak)
        totals = jnp.sum(powers, axis=1, keepdims=True)
        parts.append(nn(powers.astype(BF16), v_ref[:, at]) / totals)
        logs.append(peak + jnp.log(totals))
    mixed = jnp.concatenate(parts, axis=1).astype(BF16).astype(F32)
    out_ref[...] = mixed
    logs.append(jnp.zeros((q_ref.shape[0], total_ref.shape[1] - heads), F32))
    total_ref[...] = jnp.concatenate(logs, axis=1)


def attend(queries, keys, values, after=()):
    rows, width = queries.shape
    return call(
        attend_kernel,
        "attend",
        [shape_of((rows, width), F32), shape_of((rows, 8), F32)],
        after=after,
    )(queries, keys, values)


def convert_kernel(*refs):
    half = len(refs) // 2
    for ref, out_ref in zip(refs[:half], refs[half:]):
        out_ref[...] = ref[...].astype(out_ref.dtype)


def convert(arrays, dtype, vmem=20, after=()):
    shapes = [shape_of(array.shape, dtype) for array in arrays]
    return call(convert_kernel, "convert", shapes, after=after, vmem=vmem)(*arrays)


ERF = (0.254829592, -0.284496736, 1.421413741, -1.453152027, 1.061405429)


def gelu_pair(values):
    size = jnp.abs(values) * (1.0 / math.sqrt(2.0))
    step = 1.0 / (1.0 + 0.3275911 * size)
    bell = jnp.exp(-(size * size))
    series = ERF[4]
    for factor in (ERF[3], ERF[2], ERF[1], ERF[0]):
        series = series * step + factor
    tail = (0.5 * step) * series * bell
    below = jnp.where(values >= 0, 1.0 - tail, tail)
    return values * below, below + values * (bell * (1.0 / math.sqrt(2.0 * math.pi)))


def feed_kernel(
    core_ref,
    x_ref,
    dy_ref,
    near_ref,
    far_ref,
    w0_ref,
    w1_ref,
    w2_ref,
    w3_ref,
    vec_ref,
    other_vec_ref,
    fc1_ref,
    fc2_ref,
    other_fc1_ref,
    other_fc2_ref,
    *refs,
    start,
):
    kept_ref, own_ref, *swap_refs, grad_ref, sums_ref = refs
    count = grad_ref.shape[0]
    rows = slice(start, start + count)
    place = half_of(core_ref, x_ref, start, count)
    width = w0_ref.shape[0]
    units = fc1_ref.shape[1]

    def share(ref, part, w_ref):
        return nn(ref[rows, part * width : (part + 1) * width].astype(BF16), w_ref[0:width, :].astype(BF16))

    branch = (share(near_ref, 0, w0_ref) + share(near_ref, 1, w1_ref)) + (
        share(far_ref, 0, w2_ref) + share(far_ref, 1, w3_ref)
    )
    middle = x_ref[place, :].astype(F32) + (branch + vector(vec_ref, OUT_BIAS))
    kept_ref[0:count, :] = middle
    normal, _ = normalize(middle)
    left = (normal * vector(vec_ref, LN2_GAIN) + vector(vec_ref, LN2_BIAS)).astype(BF16)
    own_ref[0:count, :] = left
    dy = dy_ref[place, :]
    grad = res = None
    groups = ((vec_ref, FC1_BIAS, fc1_ref, fc2_ref), (other_vec_ref, 0, other_fc1_ref, other_fc2_ref))
    for group, (bias_ref, bias_row, in_ref, out_ref) in enumerate(groups):
        hidden, slope = gelu_pair(nn(left, in_ref[...]) + vector(bias_ref, bias_row, units))
        hidden = hidden.astype(BF16)
        pre = (nt(dy, out_ref[...]) * slope).astype(BF16)
        if group == 0:
            own_ref[count : 2 * count, :] = pre
            own_ref[2 * count :, :] = hidden
        else:
            at = 0
            wide = jnp.concatenate([left, pre, hidden], axis=0).astype(F32)
            for ref in swap_refs:
                size = 3 * count // len(swap_refs)
                ref[0:size, :] = wide[at : at + size]
                at += size
        back = nt(pre, in_ref[...])
        fed = nn(hidden, out_ref[...])
        grad = back if grad is None else grad + back
        res = fed if res is None else res + fed
    grad_ref[...] = grad
    kept_ref[count:, :] = res
    sums_ref[0:1, :] = jnp.sum(dy.astype(F32), axis=0, keepdims=True)


def feed(core, start, count, x, dy, near, far, out_weights, vectors, other_bias, fc1, fc2, other, after=()):
    model = x.shape[1]
    swaps = [3 * count + 8] if start == 0 else [3 * count // 2] * 2
    return call(
        functools.partial(feed_kernel, start=start),
        "feed",
        [shape_of((2 * count, model), F32), shape_of((3 * count, model), BF16)]
        + [shape_of((size, model), F32) for size in swaps]
        + [shape_of((count, model), F32), shape_of((8, model), F32)],
        scalars=1,
        after=after,
    )(core, x, dy, near, far, *out_weights, vectors, other_bias, fc1, fc2, *other)


def cut_pieces(ref, send_ref, keep_ref, mine, count, axis_bits, axis):
    rows = ref.shape[0] // count
    stride = 1 << (axis_bits - 1 - axis)
    for value in range(2):

        @pl.when(mine == value)
        def _():
            for index in range(count):
                place = (index // (2 * stride)) * stride + index % stride
                out = keep_ref if (index // stride) % 2 == value else send_ref
                out[place * rows : (place + 1) * rows, :] = ref[index * rows : (index + 1) * rows, :]


def cut_spans(total_ref, refs, mine_ref, spans, count, axes):
    axis_bits = count.bit_length() - 1
    for index, (span, axis) in enumerate(zip(spans, axes)):
        cut_pieces(
            total_ref.at[:, span], refs[2 * index], refs[2 * index + 1], mine_ref[index], count,
            axis_bits, axis,
        )


def cut_shapes(rows, spans):
    shapes = []
    for span in spans:
        shapes += [shape_of((rows // 2, span.stop - span.start), F32)] * 2
    return shapes


def column_sum(values):
    return jnp.sum(values.astype(F32), axis=0, keepdims=True)


def swapped(refs, part, count):
    size = 3 * count // len(refs)
    pieces = []
    at, end = part * count, (part + 1) * count
    while at < end:
        index = at // size
        stop = min(end, (index + 1) * size)
        pieces.append(refs[index][at - index * size : stop - index * size, :])
        at = stop
    return (pieces[0] if len(pieces) == 1 else jnp.concatenate(pieces, axis=0)).astype(BF16)


def chunks_of(refs):
    own0, own1, theirs0, theirs1, theirs2 = refs
    sizes = [own0.shape[0] // 3, own1.shape[0] // 3]
    return ((0, sizes[0], own0, [theirs0]), (sizes[0], sizes[1], own1, [theirs1, theirs2]))


def fc2_grad_kernel(core_ref, mine_ref, dy_ref, *refs, spans, count, axes):
    total_ref = refs[-1]
    total = None
    for start, size, own, theirs in chunks_of(refs[:5]):
        for half, hidden in (
            (core_ref[0], own[2 * size :, :]),
            (1 - core_ref[0], swapped(theirs, 2, size)),
        ):
            place = pl.multiple_of(half * (dy_ref.shape[0] // 2) + start, 128)
            term = tn(dy_ref[pl.ds(place, size), :], hidden)
            total = term if total is None else total + term
    total_ref[...] = total
    cut_spans(total_ref, refs[5:-1], mine_ref, spans, count, axes)


def fc1_grad_kernel(core_ref, mine_ref, *refs, spans, count, axes):
    sums_ref, total_ref = refs[-2:]
    total = None
    sums = 0.0
    for _, size, own, theirs in chunks_of(refs[:5]):
        for left, pre in (
            (own[0:size, :], own[size : 2 * size, :]),
            (swapped(theirs, 0, size), swapped(theirs, 1, size)),
        ):
            term = tn(left, pre)
            total = term if total is None else total + term
            sums = sums + column_sum(pre)
    total_ref[...] = total
    sums_ref[0:1, :] = sums
    cut_spans(total_ref, refs[5:-2], mine_ref, spans, count, axes)


def chunk_products(lows, near_ref, columns):
    at = 0
    total = None
    for low in lows:
        term = tn(low[...], near_ref[at : at + low.shape[0], columns].astype(BF16))
        total = term if total is None else total + term
        at += low.shape[0]
    return total


def heads_grad_kernel(
    core_ref, mine_ref, left_ref, ours_ref, theirs_ref, low0_ref, low1_ref, near_ref, out_w_ref,
    *refs, spans, count, axes,
):
    sums_ref, total_ref = refs[-2:]
    rows = left_ref.shape[0] // 2
    width = near_ref.shape[1] // 2
    ours = ours_ref[...]
    theirs = jnp.concatenate(
        [
            theirs_ref[0:rows, :],
            jnp.concatenate([theirs_ref[rows:, :width], theirs_ref[rows:, width:]], axis=0),
        ],
        axis=1,
    ).astype(BF16)
    left = left_ref[half_of(core_ref, left_ref), :]
    left_other = left_ref[pl.ds(pl.multiple_of((1 - core_ref[0]) * rows, BLOCK), rows), :]
    total_ref[:, : 3 * width] = tn(left, ours) + tn(left_other, theirs)
    out_w = jnp.concatenate([out_w_ref[:, :width], out_w_ref[:, width:]], axis=0)
    total_ref[:, 3 * width :] = out_w + chunk_products((low0_ref, low1_ref), near_ref, slice(0, width))
    sums_ref[...] = jnp.zeros_like(sums_ref)
    sums_ref[0:1, : 3 * width] = column_sum(ours) + column_sum(theirs)
    cut_spans(total_ref, refs[:-2], mine_ref, spans, count, axes)


def weight_grad(kernel, core, mine, operands, model, width, spans, count, axes, sums, far, after=()):
    return call(
        functools.partial(kernel, spans=spans, count=count, axes=axes),
        "weight_grad",
        cut_shapes(model, spans) + ([shape_of((8, model), F32)] if sums else []),
        scalars=2,
        scratch=[pltpu.VMEM((model, width), F32)],
        after=after,
        far_in=far,
    )(core, mine, *operands)


def hop_kernel(mine_ref, *refs, pairs, spans, count, axes):
    total_ref = refs[-1]
    at = 0
    for pair in range(pairs):
        ours, theirs = refs[2 * pair], refs[2 * pair + 1]
        total_ref[:, at : at + ours.shape[1]] = ours[...] + theirs[...]
        at += ours.shape[1]
    cut_spans(total_ref, refs[2 * pairs : -1], mine_ref, spans, count, axes)


def hop(mine, pairs, count, axis, after=()):
    operands = [array for pair in pairs for array in pair]
    rows = operands[0].shape[0]
    width = sum(pair[0].shape[1] for pair in pairs)
    spans = [slice(0, width)]
    return call(
        functools.partial(hop_kernel, pairs=len(pairs), spans=spans, count=count, axes=[axis]),
        "hop",
        cut_shapes(rows, spans),
        scalars=1,
        scratch=[pltpu.VMEM((rows, width), F32)],
        after=after,
    )(mine, *operands)


def norm_back(grad, normal, factor, gain):
    scaled = grad * gain
    first = jnp.mean(scaled, axis=-1, keepdims=True)
    second = jnp.mean(scaled * normal, axis=-1, keepdims=True)
    return factor * (scaled - first - normal * second)


def second_back_kernel(core_ref, ours_ref, theirs_ref, kept_ref, dy_ref, vec_ref, *refs, start):
    grad_ref, low_ref, sums_ref = refs[-5:-2] if start else refs
    count = ours_ref.shape[0]
    grad = ours_ref[...] + theirs_ref[...]
    normal, factor = normalize(kept_ref[0:count, :])
    dy = dy_ref[half_of(core_ref, dy_ref, start, count), :].astype(F32)
    total = dy + norm_back(grad, normal, factor, vector(vec_ref, LN2_GAIN))
    grad_ref[...] = total
    low = total.astype(BF16)
    low_ref[...] = low
    for index, term in enumerate((grad * normal, grad, low.astype(F32))):
        sums_ref[index : index + 1, :] = column_sum(term)
    if start:
        kept0_ref, low0_ref, near_ref = refs[:3]
        res_ref, out_w_ref = refs[-2:]
        rows = res_ref.shape[0] - 8
        res_ref[0:rows, :] = kept0_ref[start : start + rows, :]
        width = near_ref.shape[1] // 2
        product = chunk_products((low0_ref, low_ref), near_ref, slice(width, 2 * width))
        out_w_ref[:, :width] = product[: product.shape[0] // 2]
        out_w_ref[:, width:] = product[product.shape[0] // 2 :]


def second_back(core, start, ours, theirs, kept, dy, vectors, others=(), after=()):
    rows, model = ours.shape
    out_shape = [shape_of((rows, model), F32), shape_of((rows, model), BF16), shape_of((8, model), F32)]
    if others:
        out_shape += [shape_of((BLOCK + 8, model), F32), shape_of((model // 2, others[2].shape[1]), F32)]
    return call(
        functools.partial(second_back_kernel, start=start),
        "second_back",
        out_shape,
        scalars=1,
        after=after,
    )(core, ours, theirs, kept, dy, vectors, *others)


def attend_back_kernel(core_ref, low_ref, w0_ref, w1_ref, q_ref, k_ref, v_ref, total_ref, *refs, start):
    if start:
        dk0_ref, dv0_ref, dq_ref, dk_send_ref, dv_send_ref, dk_ref, dv_ref, scratch_ref = refs
    else:
        dq_ref, dk_ref, dv_ref = refs
    rows_here = slice(start, start + low_ref.shape[0])
    heads = q_ref.shape[1] // HD
    scale = jnp.asarray(1.0 / math.sqrt(HD), BF16)
    low = low_ref[...]
    outers = [nt(low, ref[...]).astype(BF16) for ref in (w0_ref, w1_ref)]
    outer = jnp.concatenate(outers, axis=1)
    dqs = []
    dks = []
    dvs = []
    for head in range(heads):
        at = slice(head * HD, (head + 1) * HD)
        queries = q_ref[rows_here, at] * scale
        keys = k_ref[:, at]
        outer_here = outer[:, at]
        probs = jnp.exp(nt(queries, keys) - total_ref[rows_here, head : head + 1])
        grad_probs = nt(outer_here, v_ref[:, at])
        inner = jnp.sum(probs * grad_probs, axis=1, keepdims=True)
        grad_scores = (probs * (grad_probs - inner)).astype(BF16)
        dvs.append(tn(outer_here, probs.astype(BF16)))
        dks.append(tn(queries, grad_scores))
        dqs.append(nn(grad_scores, keys))
    dq_ref[...] = (jnp.concatenate(dqs, axis=1) * (1.0 / math.sqrt(HD))).astype(BF16)
    if not start:
        dk_ref[...] = jnp.concatenate(dks, axis=0)
        dv_ref[...] = jnp.concatenate(dvs, axis=0)
        return
    for parts, before_ref, send_ref, keep_ref in (
        (dks, dk0_ref, dk_send_ref, dk_ref),
        (dvs, dv0_ref, dv_send_ref, dv_ref),
    ):
        scratch_ref[...] = jnp.transpose(before_ref[...] + jnp.concatenate(parts, axis=0))
        rows = scratch_ref.shape[0] // 2
        for ref, half in ((send_ref, 1 - core_ref[0]), (keep_ref, core_ref[0])):
            ref[...] = scratch_ref[pl.ds(pl.multiple_of(half * rows, BLOCK), rows), :]


def attend_back(core, start, low, out_weights, queries, keys, values, totals, before=(), after=()):
    rows, width = keys.shape
    sums = [shape_of((rows // 2, width), F32)] * 4 if before else [shape_of((width, rows), F32)] * 2
    return call(
        functools.partial(attend_back_kernel, start=start),
        "attend_back",
        [shape_of((low.shape[0], width), BF16)] + sums,
        scalars=1,
        scratch=[pltpu.VMEM((rows, width), F32)] if before else [],
        after=after,
    )(core, low, *out_weights, queries, keys, values, totals, *before)


def first_grad_kernel(
    dq0_ref, dq1_ref, dk_ref, dv_ref, dk_other_ref, dv_other_ref, w_ref, other_ref, out_ref, own_ref, send_ref
):
    width = w_ref.shape[1]
    total = None
    for part in range(3):
        for group in range(2):
            if part == 0:
                span = slice(group * width, (group + 1) * width)
                values = jnp.concatenate([dq0_ref[:, span], dq1_ref[:, span]], axis=0)
            else:
                ours_ref, theirs_ref = ((dk_ref, dk_other_ref), (dv_ref, dv_other_ref))[part - 1]
                at, other = group * width, (1 - group) * width
                values = ours_ref[:, at : at + width] + theirs_ref[:, other : other + width]
                values = values.astype(BF16)
            span = slice(part * width, (part + 1) * width)
            if group == 0:
                own_ref[:, span] = values
                term = nn(values, w_ref[part])
            else:
                rows = values.shape[0]
                if part < 2:
                    send_ref[0:rows, span] = values.astype(F32)
                else:
                    send_ref[rows:, :width] = values[: rows // 2].astype(F32)
                    send_ref[rows:, width:] = values[rows // 2 :].astype(F32)
                term = nn(values, other_ref[span, :].astype(BF16))
            total = term if total is None else total + term
    out_ref[...] = total


def first_grad(dqs, ours, theirs, weight, other, after=()):
    rows = ours[0].shape[0]
    _, width, model = weight.shape
    return call(
        first_grad_kernel,
        "first_grad",
        [
            shape_of((rows, model), F32),
            shape_of((rows, 3 * width), BF16),
            shape_of((rows + rows // 2, 2 * width), F32),
        ],
        after=after,
    )(*dqs, *ours, *theirs, weight, other)


def first_back_kernel(
    core_ref, ours_ref, theirs_ref, x_ref, middle0_ref, middle1_ref, vec_ref, kept0_ref, kept1_ref,
    out_ref, sums_ref, *res_refs,
):
    gain_sum = bias_sum = 0.0
    start = 0
    for middle_ref, kept_ref, res_ref in zip((middle0_ref, middle1_ref), (kept0_ref, kept1_ref), res_refs):
        res_ref[...] = kept_ref[kept_ref.shape[0] - res_ref.shape[0] :, :]
        count = middle_ref.shape[0]
        at = slice(start, start + count)
        grad = ours_ref[at, :] + theirs_ref[at, :]
        normal, factor = normalize(x_ref[half_of(core_ref, x_ref, start, count), :].astype(F32))
        total = middle_ref[...] + norm_back(grad, normal, factor, vector(vec_ref, LN1_GAIN))
        out_ref[at, :] = total.astype(BF16).astype(F32)
        gain_sum = gain_sum + column_sum(grad * normal)
        bias_sum = bias_sum + column_sum(grad)
        start += count
    sums_ref[0:1, :] = gain_sum
    sums_ref[1:2, :] = bias_sum


def first_back(core, ours, theirs, x, middles, vectors, kepts, counts, after=()):
    rows, model = ours.shape
    return call(
        first_back_kernel,
        "first_back",
        [shape_of((rows, model), F32), shape_of((8, model), F32)]
        + [shape_of((count, model), F32) for count in counts],
        scalars=1,
        after=after,
    )(core, ours, theirs, x, *middles, vectors, *kepts)


def result_kernel(*refs, starts, placed):
    vec_ref, out_ref = refs[3 * len(starts)], refs[-1]
    at = 0
    if placed:
        done_ref = refs[3 * len(starts) + 1]
        at = done_ref.shape[0]
        out_ref[0:at, :] = done_ref[...]
    for part, (start, rows) in enumerate(starts):
        ours_ref, theirs_ref, kept_ref = refs[3 * part : 3 * part + 3]
        fed = ours_ref[0:rows, :] + theirs_ref[0:rows, :] + vector(vec_ref, FC2_BIAS)
        total = kept_ref[start : start + rows, :] + fed
        out_ref[at : at + rows, :] = total.astype(BF16).astype(F32)
        at += rows


def result_rows(parts, vectors, done=(), after=()):
    operands = [array for part in parts for array in part[:3]]
    rows = sum(part[4] for part in parts) + sum(array.shape[0] for array in done)
    return call(
        functools.partial(
            result_kernel, starts=[part[3:] for part in parts], placed=bool(done)
        ),
        "result_rows",
        [shape_of((rows, vectors.shape[1]), F32)],
        after=after,
    )(*operands, vectors, *done)[0]


def finish_kernel(core_ref, *refs):
    out_ref = refs[-1]
    for part, half in ((0, core_ref[0]), (1, 1 - core_ref[0])):
        at = 0
        for ref in refs[part:-1:2]:
            place = pl.multiple_of(half * (out_ref.shape[0] // 2) + at, BLOCK)
            out_ref[pl.ds(place, ref.shape[0]), :] = ref[...].astype(BF16)
            at += ref.shape[0]


def finish(core, pairs, after=()):
    operands = [array for pair in pairs for array in pair]
    shape = (sum(array.shape[0] for array in operands), operands[0].shape[1])
    return call(
        finish_kernel, "finish", [shape_of(shape, BF16)], scalars=1, after=after
    )(core, *operands)[0]


def feed_sum_kernel(ours_ref, theirs_ref, fc2_ref, fc1_ref):
    units = fc2_ref.shape[1]
    total = ours_ref[...] + theirs_ref[...]
    fc2_ref[...] = total[:, :units]
    fc1_ref[...] = total[:, units:]


def feed_sum(ours, theirs, after=()):
    half = shape_of((ours.shape[0], ours.shape[1] // 2), F32)
    return call(
        feed_sum_kernel, "feed_sum", [half, half], after=after
    )(ours, theirs)


def heads_sum_kernel(ours_ref, theirs_ref, heads_ref, out_ref):
    width = heads_ref.shape[2]
    total = ours_ref[...] + theirs_ref[...]
    for part in range(3):
        heads_ref[part] = total[:, part * width : (part + 1) * width]
    out_ref[...] = jnp.transpose(total[:, 3 * width :])


def heads_sum(ours, theirs, after=()):
    rows, width = ours.shape[0], ours.shape[1] // 4
    shapes = [shape_of((3, rows, width), F32), shape_of((width, rows), F32)]
    return call(
        heads_sum_kernel, "heads_sum", shapes, after=after
    )(ours, theirs)


def body(
    tokens,
    ln1_gain,
    ln1_bias,
    qkv_weight,
    qkv_bias,
    out_weight,
    out_bias,
    ln2_gain,
    ln2_bias,
    fc1_weight,
    fc1_bias,
    fc2_weight,
    fc2_bias,
    cotangent,
    *,
    batch_count,
    tensor_count,
):
    rows, model = tokens.shape[1:]
    width = qkv_weight.shape[2]
    units = fc1_weight.shape[1]
    bits = batch_count.bit_length() - 1
    batch_at = lax.axis_index("batch")
    core = (lax.axis_index("tensor") % 2).astype(jnp.int32).reshape(1)

    def core_swap(v):
        return lax.ppermute(v, "tensor", [(i, i ^ 1) for i in range(tensor_count)])

    def chip_swap(v):
        return lax.ppermute(v, "tensor", [(i, i ^ 2) for i in range(tensor_count)])

    def batch_swap(v, bit):
        return lax.ppermute(v, "batch", [(i, i ^ (1 << bit)) for i in range(batch_count)])

    last = []

    def then(made, *others):
        last[:] = [made[0], *others]
        return made

    orders = ([0, *range(1, bits)], [1, 0, *range(2, bits)])

    def mine_of(some):
        return jnp.stack([(batch_at >> bit) & 1 for bit in some]).astype(jnp.int32)

    class Scatter:
        def __init__(self, cut, order, left=range(bits - 1, -1, -1)):
            self.order = list(order)
            self.left = list(left)
            self.cross(cut)

        def cross(self, cut):
            send, self.keep = cut
            bit = self.order.pop(0)
            self.left.remove(bit)
            self.theirs = batch_swap(send, bit)

        def step(self, *others):
            bit = self.order[0]
            pairs = [(v.keep, v.theirs) for v in (self, *others)]
            self.cross(
                then(hop(mine_of([bit]), pairs, 1 << len(self.left), self.left.index(bit), after=last))
            )

        def end(self, summed):
            while self.order:
                self.step()
            return then(summed(self.keep, self.theirs, after=last))

    def weight_scatters(kernel, operands, width, orders, far, sums=True):
        span = width // len(orders)
        spans = [slice(i * span, (i + 1) * span) for i in range(len(orders))]
        firsts = [order[0] for order in orders]
        made = then(
            weight_grad(
                kernel, core, mine_of(firsts), operands, model, width, spans, batch_count,
                [bits - 1 - bit for bit in firsts], sums=sums, far=far, after=last,
            )
        )
        return [Scatter(made[2 * i : 2 * i + 2], order) for i, order in enumerate(orders)], made[-1]

    x = tokens.reshape(rows, model)
    dy = cotangent.reshape(rows, model)
    heads_weight = jnp.transpose(qkv_weight, (1, 2, 0))
    listed = (
        ln1_gain, ln1_bias, jnp.transpose(qkv_bias, (1, 0, 2)), out_bias, ln2_gain, ln2_bias, fc1_bias,
        fc2_bias,
    )
    vectors, heads_wide, out_weight_wide = pack(listed, heads_weight, out_weight)

    heads_other = core_swap(heads_wide)
    out_weight_far = chip_swap(out_weight_wide)
    others = then(
        convert([fc1_weight, fc2_weight, out_weight], F32, vmem=60, after=[heads_wide])
    )
    others = [core_swap(v) for v in others]
    other_bias = heads_other[3 * width + FC1_BIAS :]

    left, queries, keys, values = then(
        project(core, x, vectors, heads_weight, heads_other, after=last)
    )
    near, totals = then(attend(queries, keys, values, after=last))
    far = chip_swap(near)
    fc1_other, fc2_other, out_weight_other = then(convert(others, BF16, after=last))
    out_weight_both = core_swap(out_weight_far)
    out_weights = (out_weight, out_weight_other, out_weight_far, out_weight_both)

    half = rows // 2
    sizes = (3 * half // 4, half // 4)
    starts = (0, sizes[0])
    fed = []
    for start, size in zip(starts, sizes):
        fed.append(
            then(
                feed(
                    core, start, size, x, dy, near, far, out_weights, vectors, other_bias, fc1_weight,
                    fc2_weight, (fc1_other, fc2_other), after=last,
                )
            )
        )
    kepts, owns = [f[0] for f in fed], [f[1] for f in fed]
    grads, feed_sums = [f[-2] for f in fed], [f[-1] for f in fed]
    grads_far = [chip_swap(v) for v in grads]
    swaps = [core_swap(v) for f in fed for v in f[2:-2]]
    (fc2,), _ = weight_scatters(
        fc2_grad_kernel, [dy, *owns, *swaps], units, orders[1:], (), sums=False
    )
    (fc1,), fc1_sums = weight_scatters(fc1_grad_kernel, [*owns, *swaps], units, orders[:1], ())

    weights = (out_weight, out_weight_other)
    heads = (queries, keys, values, totals)
    middle0, low0, second_sums0 = then(
        second_back(core, 0, grads[0], grads_far[0], kepts[0], dy, vectors, after=last)
    )
    dq0, dk0, dv0 = then(attend_back(core, 0, low0, weights, *heads, after=last))
    middle1, low1, second_sums1, res0, out_w = then(
        second_back(
            core, starts[1], grads[1], grads_far[1], kepts[1], dy, vectors, (kepts[0], low0, near),
            after=last,
        )
    )
    res0_far = chip_swap(res0)
    out_w_other = core_swap(out_w)
    dq1, dk_send, dv_send, dk, dv = then(
        attend_back(core, starts[1], low1, weights, *heads, (dk0, dv0), after=last)
    )
    theirs = core_swap(dk_send), core_swap(dv_send)
    fc2.step()
    fc1.step()
    grad_rows, heads_own, send = then(
        first_grad(
            (dq0, dq1), (dk, dv), theirs, heads_weight, heads_other, after=[*last, res0_far]
        )
    )
    grad_rows_far = chip_swap(grad_rows)
    heads_theirs = core_swap(send)
    heads, heads_sums = weight_scatters(
        heads_grad_kernel,
        [left, heads_own, heads_theirs, low0, low1, near, out_w_other],
        4 * width,
        orders,
        (),
    )
    result0 = then([result_rows([(res0, res0_far, kepts[0], 0, BLOCK)], vectors, after=last)])[0]
    fc2.step(fc1)
    heads[0].step()
    heads[1].step()
    counts = (sizes[0] - BLOCK, sizes[1])
    grad_rows, norm_sums, *res1 = then(
        first_back(
            core, grad_rows, grad_rows_far, x, (middle0, middle1), vectors, kepts, counts, after=last
        )
    )
    grad_rows_other = core_swap(grad_rows)
    res1_far = [chip_swap(v) for v in res1]
    grad_fc2, grad_fc1 = fc2.end(feed_sum)
    heads[0].step(heads[1])
    grad_heads, grad_out = heads[0].end(heads_sum)

    second_sums = second_sums0 + second_sums1
    small = jnp.concatenate(
        [second_sums[2:3], feed_sums[0][:1] + feed_sums[1][:1], second_sums[:2], norm_sums[:2]]
    )
    small = jnp.concatenate([small + core_swap(small), fc1_sums[:1], heads_sums[:1]])
    for bit in range(bits):
        small = small + batch_swap(small, bit)
    last.append(small)
    parts = [
        (v, far, kept, start, count)
        for v, far, kept, start, count in zip(res1, res1_far, kepts, (BLOCK, 0), counts)
    ]
    result = then([result_rows(parts, vectors, [result0], after=last)])[0]
    result_other = core_swap(result)
    grad_tokens = then([finish(core, [(grad_rows, grad_rows_other)], after=last)])[0]
    result = then([finish(core, [(result, result_other)], after=last)])[0]
    share = HD // batch_count
    piece = model // batch_count
    shared = lax.dynamic_slice_in_dim(small[:6], batch_at * piece, piece, 1)
    own = lax.dynamic_slice_in_dim(
        small[6:].reshape(2, model // HD, HD), batch_at * share, share, 2
    )
    return (
        result.reshape(tokens.shape),
        grad_tokens.reshape(tokens.shape),
        jnp.transpose(grad_heads, (1, 0, 2)),
        own[1, : 3 * width // HD].reshape(3, width // HD, share)[::2],
        grad_out,
        shared[0],
        shared[4],
        shared[5],
        shared[2],
        shared[3],
        grad_fc1,
        own[0, : units // HD],
        grad_fc2.T,
        shared[1],
    )


def solution(mesh):
    placed = (
        P("batch", None, None),
        P(),
        P(),
        P(None, None, "tensor"),
        P(None, "tensor", None),
        P("tensor", None),
        P(),
        P(),
        P(),
        P(None, "tensor"),
        P("tensor", None),
        P("tensor", None),
        P(),
        P("batch", None, None),
    )
    return jax.shard_map(
        functools.partial(
            body, batch_count=mesh.shape["batch"], tensor_count=mesh.shape["tensor"]
        ),
        mesh=mesh,
        in_specs=placed,
        out_specs=(
            P("batch", None, None),
            P("batch", None, None),
            P("batch", None, "tensor"),
            P(None, "tensor", "batch"),
            P("tensor", "batch"),
            P("batch"),
            P("batch"),
            P("batch"),
            P("batch"),
            P("batch"),
            P("batch", "tensor"),
            P("tensor", "batch"),
            P("tensor", "batch"),
            P("batch"),
        ),
        check_vma=False,
    )
```

```python
import functools
import math

import jax
import jax.numpy as jnp
from jax import lax
from jax.experimental import pallas as pl
from jax.experimental.pallas import tpu as pltpu
from jax.sharding import PartitionSpec as P

HD = 64
LN1_GAIN, LN1_BIAS, HEADS_BIAS, OUT_BIAS, LN2_GAIN, LN2_BIAS, FC1_BIAS, FC2_BIAS = range(8)
BLOCK = 256
EPSILON = 1e-06
F32 = jnp.float32
BF16 = jnp.bfloat16


def nn(a, b):
    return lax.dot_general(a, b, (((1,), (0,)), ((), ())), preferred_element_type=F32)


def nt(a, b):
    return lax.dot_general(a, b, (((1,), (1,)), ((), ())), preferred_element_type=F32)


def tn(a, b):
    return lax.dot_general(a, b, (((0,), (0,)), ((), ())), preferred_element_type=F32)


def call(kernel, name, out_shape, scalars=0, scratch=(), after=(), far_in=(), far_out=(), vmem=20, raw_in=()):

    def run(*args):
        given = len(args)
        ins = [scalars + index for index in far_in]
        outs = list(far_out)
        made = len(out_shape)

        def inner(*refs):
            first = given + len(after)
            operands, results = list(refs[:given]), list(refs[first : first + made])
            held = list(refs[first + made : first + made + len(scratch)])
            spare = list(refs[first + made + len(scratch) :])
            sems = spare.pop() if spare else None
            copies = []
            for count, index in enumerate(ins):
                copies.append(pltpu.make_async_copy(operands[index], spare[count], sems.at[count]))
                operands[index] = spare[count]
            for copy in copies:
                copy.start()
            far = [results[index] for index in outs]
            for count, index in enumerate(outs):
                results[index] = spare[len(ins) + count]
            for copy in copies:
                copy.wait()
            kernel(*operands, *results, *held)
            copies = []
            for count, ref in enumerate(far, len(ins)):
                copies.append(pltpu.make_async_copy(spare[count], ref, sems.at[count]))
            for copy in copies:
                copy.start()
            for copy in copies:
                copy.wait()

        def space(index, chosen):
            return pl.BlockSpec(memory_space=pltpu.HBM if index in chosen else pltpu.VMEM)

        moved = [args[index] for index in ins] + [out_shape[index] for index in outs]
        held = list(scratch) + [pltpu.VMEM(v.shape, v.dtype) for v in moved]
        if moved:
            held.append(pltpu.SemaphoreType.DMA((len(moved),)))
        return pl.pallas_call(
            inner,
            in_specs=[pl.BlockSpec(memory_space=pltpu.SMEM)] * scalars
            + [space(index, [*ins, *(scalars + at for at in raw_in)]) for index in range(scalars, given)]
            + [pl.BlockSpec(memory_space=pl.ANY)] * len(after),
            out_specs=[space(index, outs) for index in range(made)],
            scratch_shapes=held,
            out_shape=out_shape,
            compiler_params=pltpu.CompilerParams(vmem_limit_bytes=vmem * 1024 * 1024),
            name=name,
        )(*args, *after)

    return run


def shape_of(shape, dtype):
    return jax.ShapeDtypeStruct(shape, dtype)


def vector(ref, row, width=None):
    return ref[row : row + 1, : ref.shape[1] if width is None else width]


def normalize(values):
    average = jnp.mean(values, axis=-1, keepdims=True)
    centered = values - average
    spread = jnp.mean(centered * centered, axis=-1, keepdims=True)
    factor = lax.rsqrt(spread + EPSILON)
    return centered * factor, factor


def half_of(core_ref, ref, offset=0, rows=None):
    size = ref.shape[0] // 2
    rows = size if rows is None else rows
    return pl.ds(pl.multiple_of(core_ref[0] * size + offset, 128), rows)


def pack_kernel(
    g1_ref, b1_ref, bias_ref, ob_ref, g2_ref, b2_ref, fc1_bias_ref, fb_ref, w_ref, out_w_ref,
    vec_ref, wide_ref, out_wide_ref,
):
    width = w_ref.shape[1]
    vec_ref[...] = jnp.zeros_like(vec_ref)
    for row, ref in (
        (LN1_GAIN, g1_ref),
        (LN1_BIAS, b1_ref),
        (OUT_BIAS, ob_ref),
        (LN2_GAIN, g2_ref),
        (LN2_BIAS, b2_ref),
        (FC2_BIAS, fb_ref),
    ):
        vec_ref[row : row + 1, :] = ref[...].reshape(1, -1)
    for head in range(bias_ref.shape[0]):
        for part, start in ((0, 0), (1, 2 * width)):
            at = start + head * HD
            vec_ref[HEADS_BIAS : HEADS_BIAS + 1, at : at + HD] = bias_ref[head, part : part + 1, :]
    for head in range(fc1_bias_ref.shape[0]):
        at = slice(head * HD, (head + 1) * HD)
        vec_ref[FC1_BIAS : FC1_BIAS + 1, at] = fc1_bias_ref[head : head + 1, :]
    for part in range(3):
        wide_ref[part * width : (part + 1) * width, :] = w_ref[part].astype(F32)
    wide_ref[3 * width :, :] = vec_ref[...]
    out_wide_ref[0:width, :] = out_w_ref[...].astype(F32)


def pack(listed, heads_weight, out_weight):
    width, model = out_weight.shape
    return call(
        pack_kernel,
        "pack",
        [
            shape_of((8, model), F32),
            shape_of((3 * width + 8, model), F32),
            shape_of((width + 8, model), F32),
        ],
        vmem=60,
    )(*listed, heads_weight, out_weight)


def project_kernel(core_ref, x_ref, vec_ref, w_ref, other_ref, all_ref, q_ref, k_ref, v_ref):
    width = w_ref.shape[1]
    for start in range(0, x_ref.shape[0], BLOCK):
        at = slice(start, start + BLOCK)
        normal, _ = normalize(x_ref[at, :].astype(F32))
        all_ref[at, :] = (normal * vector(vec_ref, LN1_GAIN) + vector(vec_ref, LN1_BIAS)).astype(BF16)
    left = all_ref[...]
    mine = all_ref[half_of(core_ref, all_ref), :]
    bias_row = 3 * width + HEADS_BIAS
    biases = (vector(vec_ref, HEADS_BIAS), other_ref[bias_row : bias_row + 1, :])
    for group in range(2):
        for part, (ref, rows) in enumerate(((q_ref, mine), (k_ref, left), (v_ref, left))):
            span = slice(part * width, (part + 1) * width)
            weight = w_ref[part] if group == 0 else other_ref[span, :].astype(BF16)
            ref[:, group * width : (group + 1) * width] = (
                nt(rows, weight) + biases[group][:, span]
            ).astype(BF16)


def project(core, x, vectors, weight, other, after=()):
    rows, model = x.shape
    width = weight.shape[1]
    both = 2 * width
    return call(
        project_kernel,
        "project",
        [
            shape_of((rows, model), BF16),
            shape_of((rows // 2, both), BF16),
            shape_of((rows, both), BF16),
            shape_of((rows, both), BF16),
        ],
        scalars=1,
        after=after,
    )(core, x, vectors, weight, other)


def attend_kernel(q_ref, k_ref, v_ref, out_ref, total_ref):
    heads = q_ref.shape[1] // HD
    scale = jnp.asarray(1.0 / math.sqrt(HD), BF16)
    parts = []
    logs = []
    for head in range(heads):
        at = slice(head * HD, (head + 1) * HD)
        scores = nt(q_ref[:, at] * scale, k_ref[:, at])
        peak = jnp.max(scores, axis=1, keepdims=True)
        powers = jnp.exp(scores - peak)
        totals = jnp.sum(powers, axis=1, keepdims=True)
        parts.append(nn(powers.astype(BF16), v_ref[:, at]) / totals)
        logs.append(peak + jnp.log(totals))
    mixed = jnp.concatenate(parts, axis=1).astype(BF16).astype(F32)
    out_ref[...] = mixed
    logs.append(jnp.zeros((q_ref.shape[0], total_ref.shape[1] - heads), F32))
    total_ref[...] = jnp.concatenate(logs, axis=1)


def attend(queries, keys, values, after=()):
    rows, width = queries.shape
    return call(
        attend_kernel,
        "attend",
        [shape_of((rows, width), F32), shape_of((rows, 8), F32)],
        after=after,
    )(queries, keys, values)


def convert_kernel(*refs):
    half = len(refs) // 2
    for ref, out_ref in zip(refs[:half], refs[half:]):
        out_ref[...] = ref[...].astype(out_ref.dtype)


def convert(arrays, dtype, vmem=20, after=()):
    shapes = [shape_of(array.shape, dtype) for array in arrays]
    return call(convert_kernel, "convert", shapes, after=after, vmem=vmem)(*arrays)


ERF = (0.254829592, -0.284496736, 1.421413741, -1.453152027, 1.061405429)


def gelu_pair(values):
    size = jnp.abs(values) * (1.0 / math.sqrt(2.0))
    step = 1.0 / (1.0 + 0.3275911 * size)
    bell = jnp.exp(-(size * size))
    series = ERF[4]
    for factor in (ERF[3], ERF[2], ERF[1], ERF[0]):
        series = series * step + factor
    tail = (0.5 * step) * series * bell
    below = jnp.where(values >= 0, 1.0 - tail, tail)
    return values * below, below + values * (bell * (1.0 / math.sqrt(2.0 * math.pi)))


def feed_kernel(
    core_ref,
    x_ref,
    dy_ref,
    near_ref,
    far_ref,
    w0_ref,
    w1_ref,
    w2_ref,
    w3_ref,
    vec_ref,
    other_vec_ref,
    fc1_ref,
    fc2_ref,
    other_fc1_ref,
    other_fc2_ref,
    *refs,
    start,
):
    kept_ref, own_ref, *swap_refs, grad_ref, sums_ref = refs
    count = grad_ref.shape[0]
    rows = slice(start, start + count)
    place = half_of(core_ref, x_ref, start, count)
    width = w0_ref.shape[0]
    units = fc1_ref.shape[1]

    def share(ref, part, w_ref):
        return nn(ref[rows, part * width : (part + 1) * width].astype(BF16), w_ref[0:width, :].astype(BF16))

    branch = (share(near_ref, 0, w0_ref) + share(near_ref, 1, w1_ref)) + (
        share(far_ref, 0, w2_ref) + share(far_ref, 1, w3_ref)
    )
    middle = x_ref[place, :].astype(F32) + (branch + vector(vec_ref, OUT_BIAS))
    kept_ref[0:count, :] = middle
    normal, _ = normalize(middle)
    left = (normal * vector(vec_ref, LN2_GAIN) + vector(vec_ref, LN2_BIAS)).astype(BF16)
    own_ref[0:count, :] = left
    dy = dy_ref[place, :]
    grad = res = None
    groups = ((vec_ref, FC1_BIAS, fc1_ref, fc2_ref), (other_vec_ref, 0, other_fc1_ref, other_fc2_ref))
    for group, (bias_ref, bias_row, in_ref, out_ref) in enumerate(groups):
        hidden, slope = gelu_pair(nn(left, in_ref[...]) + vector(bias_ref, bias_row, units))
        hidden = hidden.astype(BF16)
        pre = (nt(dy, out_ref[...]) * slope).astype(BF16)
        if group == 0:
            own_ref[count : 2 * count, :] = pre
            own_ref[2 * count :, :] = hidden
        else:
            at = 0
            wide = jnp.concatenate([left, pre, hidden], axis=0).astype(F32)
            for ref in swap_refs:
                size = 3 * count // len(swap_refs)
                ref[0:size, :] = wide[at : at + size]
                at += size
        back = nt(pre, in_ref[...])
        fed = nn(hidden, out_ref[...])
        grad = back if grad is None else grad + back
        res = fed if res is None else res + fed
    grad_ref[...] = grad
    kept_ref[count:, :] = res
    sums_ref[0:1, :] = jnp.sum(dy.astype(F32), axis=0, keepdims=True)


def feed(core, start, count, x, dy, near, far, out_weights, vectors, other_bias, fc1, fc2, other, after=()):
    model = x.shape[1]
    swaps = [3 * count + 8] if start == 0 else [3 * count // 2] * 2
    return call(
        functools.partial(feed_kernel, start=start),
        "feed",
        [shape_of((2 * count, model), F32), shape_of((3 * count, model), BF16)]
        + [shape_of((size, model), F32) for size in swaps]
        + [shape_of((count, model), F32), shape_of((8, model), F32)],
        scalars=1,
        after=after,
    )(core, x, dy, near, far, *out_weights, vectors, other_bias, fc1, fc2, *other)


def cut_pieces(ref, send_ref, keep_ref, mine, count, axis_bits, axis):
    rows = ref.shape[0] // count
    stride = 1 << (axis_bits - 1 - axis)
    for value in range(2):

        @pl.when(mine == value)
        def _():
            for index in range(count):
                place = (index // (2 * stride)) * stride + index % stride
                out = keep_ref if (index // stride) % 2 == value else send_ref
                out[place * rows : (place + 1) * rows, :] = ref[index * rows : (index + 1) * rows, :]


def cut_spans(total_ref, refs, mine_ref, spans, count, axes):
    axis_bits = count.bit_length() - 1
    for index, (span, axis) in enumerate(zip(spans, axes)):
        cut_pieces(
            total_ref.at[:, span], refs[2 * index], refs[2 * index + 1], mine_ref[index], count,
            axis_bits, axis,
        )


def cut_shapes(rows, spans):
    shapes = []
    for span in spans:
        shapes += [shape_of((rows // 2, span.stop - span.start), F32)] * 2
    return shapes


def column_sum(values):
    return jnp.sum(values.astype(F32), axis=0, keepdims=True)


def turn_kernel(ref, out_ref):
    out_ref[...] = jnp.transpose(ref[...])


def turn(array, after=()):
    return call(turn_kernel, "turn", [shape_of(array.shape[::-1], array.dtype)], after=after)(array)


def fetch(pairs, sem):
    copies = [
        pltpu.make_async_copy(source, target, sem.at[index])
        for index, (source, target) in enumerate(pairs)
    ]
    for copy in copies:
        copy.start()
    return copies


def fc2_grad_kernel(core_ref, mine_ref, dy_ref, own0, own1, swap0, swap1, swap2, *refs, spans, count, axes):
    cuts, (total_ref, dy_held, h0, h1, t0, t1, sem) = refs[:-7], refs[-7:]
    n0, n1 = h0.shape[0], h1.shape[0]
    copies = fetch(
        [
            (dy_ref, dy_held),
            (own0.at[pl.ds(2 * n0, n0), :], h0),
            (own1.at[pl.ds(2 * n1, n1), :], h1),
            (swap0.at[pl.ds(2 * n0, n0), :], t0),
            (swap2.at[pl.ds(n1 // 2, n1), :], t1),
        ],
        sem,
    )
    copies[0].wait()
    total = None
    for index, (held, start, half) in enumerate(
        ((h0, 0, core_ref[0]), (h1, n0, core_ref[0]), (t0, 0, 1 - core_ref[0]), (t1, n0, 1 - core_ref[0]))
    ):
        copies[index + 1].wait()
        place = pl.multiple_of(half * (dy_held.shape[1] // 2) + start, 128)
        term = nn(dy_held[:, pl.ds(place, held.shape[0])], held[...].astype(BF16))
        total = term if total is None else total + term
    total_ref[...] = total
    cut_spans(total_ref, cuts, mine_ref, spans, count, axes)


def fc1_grad_kernel(core_ref, mine_ref, own0, own1, swap0, swap1, swap2, *refs, spans, count, axes):
    cuts, (sums_ref, total_ref, h0, h1, t0, t1, sem) = refs[:-7], refs[-7:]
    n0, n1 = h0.shape[0] // 2, h1.shape[0] // 2
    copies = fetch(
        [
            (own0.at[pl.ds(0, 2 * n0), :], h0),
            (own1.at[pl.ds(0, 2 * n1), :], h1),
            (swap0.at[pl.ds(0, 2 * n0), :], t0),
            (swap1, t1.at[pl.ds(0, 3 * n1 // 2), :]),
            (swap2.at[pl.ds(0, n1 // 2), :], t1.at[pl.ds(3 * n1 // 2, n1 // 2), :]),
        ],
        sem,
    )
    total = None
    sums = 0.0
    for index, held in enumerate((h0, h1, t0, t1)):
        copies[index].wait()
        if index == 3:
            copies[4].wait()
        size = held.shape[0] // 2
        left, pre = held[0:size, :].astype(BF16), held[size:, :].astype(BF16)
        term = tn(left, pre)
        total = term if total is None else total + term
        sums = sums + column_sum(pre)
    total_ref[...] = total
    sums_ref[0:1, :] = sums
    cut_spans(total_ref, cuts, mine_ref, spans, count, axes)


def chunk_products(lows, near_ref, columns):
    at = 0
    total = None
    for low in lows:
        term = tn(low[...], near_ref[at : at + low.shape[0], columns].astype(BF16))
        total = term if total is None else total + term
        at += low.shape[0]
    return total


def heads_grad_kernel(
    core_ref, mine_ref, left_ref, ours_ref, theirs_ref, low0_ref, low1_ref, near_ref, out_w_ref,
    *refs, spans, count, axes,
):
    sums_ref, total_ref = refs[-2:]
    rows = left_ref.shape[0] // 2
    width = near_ref.shape[1] // 2
    ours = ours_ref[...]
    theirs = jnp.concatenate(
        [
            theirs_ref[0:rows, :],
            jnp.concatenate([theirs_ref[rows:, :width], theirs_ref[rows:, width:]], axis=0),
        ],
        axis=1,
    ).astype(BF16)
    left = left_ref[half_of(core_ref, left_ref), :]
    left_other = left_ref[pl.ds(pl.multiple_of((1 - core_ref[0]) * rows, BLOCK), rows), :]
    total_ref[:, : 3 * width] = tn(left, ours) + tn(left_other, theirs)
    out_w = jnp.concatenate([out_w_ref[:, :width], out_w_ref[:, width:]], axis=0)
    total_ref[:, 3 * width :] = out_w + chunk_products((low0_ref, low1_ref), near_ref, slice(0, width))
    sums_ref[...] = jnp.zeros_like(sums_ref)
    sums_ref[0:1, : 3 * width] = column_sum(ours) + column_sum(theirs)
    cut_spans(total_ref, refs[:-2], mine_ref, spans, count, axes)


def weight_grad(
    kernel, core, mine, operands, model, width, spans, count, axes, sums, far, held=(), after=()
):
    raw = tuple(range(len(operands))) if held else ()
    return call(
        functools.partial(kernel, spans=spans, count=count, axes=axes),
        "weight_grad",
        cut_shapes(model, spans) + ([shape_of((8, model), F32)] if sums else []),
        scalars=2,
        scratch=[pltpu.VMEM((model, width), F32), *held],
        after=after,
        raw_in=raw,
        vmem=60 if held else 20,
    )(core, mine, *operands)


def hop_kernel(mine_ref, *refs, pairs, spans, count, axes):
    total_ref = refs[-1]
    at = 0
    for pair in range(pairs):
        ours, theirs = refs[2 * pair], refs[2 * pair + 1]
        total_ref[:, at : at + ours.shape[1]] = ours[...] + theirs[...]
        at += ours.shape[1]
    cut_spans(total_ref, refs[2 * pairs : -1], mine_ref, spans, count, axes)


def hop(mine, pairs, count, axis, after=()):
    operands = [array for pair in pairs for array in pair]
    rows = operands[0].shape[0]
    width = sum(pair[0].shape[1] for pair in pairs)
    spans = [slice(0, width)]
    return call(
        functools.partial(hop_kernel, pairs=len(pairs), spans=spans, count=count, axes=[axis]),
        "hop",
        cut_shapes(rows, spans),
        scalars=1,
        scratch=[pltpu.VMEM((rows, width), F32)],
        after=after,
    )(mine, *operands)


def norm_back(grad, normal, factor, gain):
    scaled = grad * gain
    first = jnp.mean(scaled, axis=-1, keepdims=True)
    second = jnp.mean(scaled * normal, axis=-1, keepdims=True)
    return factor * (scaled - first - normal * second)


def second_back_kernel(core_ref, ours_ref, theirs_ref, kept_ref, dy_ref, vec_ref, *refs, start):
    grad_ref, low_ref, sums_ref, last_ref = refs[-4:]
    count = ours_ref.shape[0]
    grad = ours_ref[...] + theirs_ref[...]
    normal, factor = normalize(kept_ref[0:count, :])
    dy = dy_ref[half_of(core_ref, dy_ref, start, count), :].astype(F32)
    total = dy + norm_back(grad, normal, factor, vector(vec_ref, LN2_GAIN))
    grad_ref[...] = total
    low = total.astype(BF16)
    low_ref[...] = low
    for index, term in enumerate((grad * normal, grad, low.astype(F32))):
        sums_ref[index : index + 1, :] = column_sum(term)
    if start == 0:
        rows = last_ref.shape[0] - 8
        last_ref[0:rows, :] = kept_ref[count : count + rows, :]
    else:
        low0_ref, near_ref = refs[:2]
        width = near_ref.shape[1] // 2
        product = chunk_products((low0_ref, low_ref), near_ref, slice(width, 2 * width))
        last_ref[:, :width] = product[: product.shape[0] // 2]
        last_ref[:, width:] = product[product.shape[0] // 2 :]


def second_back(core, start, ours, theirs, kept, dy, vectors, others=(), after=()):
    rows, model = ours.shape
    out_shape = [shape_of((rows, model), F32), shape_of((rows, model), BF16), shape_of((8, model), F32)]
    if others:
        out_shape.append(shape_of((model // 2, others[1].shape[1]), F32))
    else:
        out_shape.append(shape_of((BLOCK + 8, model), F32))
    return call(
        functools.partial(second_back_kernel, start=start),
        "second_back",
        out_shape,
        scalars=1,
        after=after,
    )(core, ours, theirs, kept, dy, vectors, *others)


def attend_back_kernel(core_ref, low_ref, w0_ref, w1_ref, q_ref, k_ref, v_ref, total_ref, *refs, start):
    if start:
        dk0_ref, dv0_ref, dq_ref, dk_send_ref, dv_send_ref, dk_ref, dv_ref, scratch_ref = refs
    else:
        dq_ref, dk_ref, dv_ref = refs
    rows_here = slice(start, start + low_ref.shape[0])
    heads = q_ref.shape[1] // HD
    scale = jnp.asarray(1.0 / math.sqrt(HD), BF16)
    low = low_ref[...]
    outers = [nt(low, ref[...]).astype(BF16) for ref in (w0_ref, w1_ref)]
    outer = jnp.concatenate(outers, axis=1)
    dqs = []
    dks = []
    dvs = []
    for head in range(heads):
        at = slice(head * HD, (head + 1) * HD)
        queries = q_ref[rows_here, at] * scale
        keys = k_ref[:, at]
        outer_here = outer[:, at]
        probs = jnp.exp(nt(queries, keys) - total_ref[rows_here, head : head + 1])
        grad_probs = nt(outer_here, v_ref[:, at])
        inner = jnp.sum(probs * grad_probs, axis=1, keepdims=True)
        grad_scores = (probs * (grad_probs - inner)).astype(BF16)
        dvs.append(tn(outer_here, probs.astype(BF16)))
        dks.append(tn(queries, grad_scores))
        dqs.append(nn(grad_scores, keys))
    dq_ref[...] = (jnp.concatenate(dqs, axis=1) * (1.0 / math.sqrt(HD))).astype(BF16)
    if not start:
        dk_ref[...] = jnp.concatenate(dks, axis=0)
        dv_ref[...] = jnp.concatenate(dvs, axis=0)
        return
    for parts, before_ref, send_ref, keep_ref in (
        (dks, dk0_ref, dk_send_ref, dk_ref),
        (dvs, dv0_ref, dv_send_ref, dv_ref),
    ):
        scratch_ref[...] = jnp.transpose(before_ref[...] + jnp.concatenate(parts, axis=0))
        rows = scratch_ref.shape[0] // 2
        for ref, half in ((send_ref, 1 - core_ref[0]), (keep_ref, core_ref[0])):
            ref[...] = scratch_ref[pl.ds(pl.multiple_of(half * rows, BLOCK), rows), :]


def attend_back(core, start, low, out_weights, queries, keys, values, totals, before=(), after=()):
    rows, width = keys.shape
    sums = [shape_of((rows // 2, width), F32)] * 4 if before else [shape_of((width, rows), F32)] * 2
    return call(
        functools.partial(attend_back_kernel, start=start),
        "attend_back",
        [shape_of((low.shape[0], width), BF16)] + sums,
        scalars=1,
        scratch=[pltpu.VMEM((rows, width), F32)] if before else [],
        after=after,
    )(core, low, *out_weights, queries, keys, values, totals, *before)


def first_grad_kernel(
    dq0_ref, dq1_ref, dk_ref, dv_ref, dk_other_ref, dv_other_ref, w_ref, other_ref, out_ref, own_ref, send_ref
):
    width = w_ref.shape[1]
    total = None
    for part in range(3):
        for group in range(2):
            if part == 0:
                span = slice(group * width, (group + 1) * width)
                values = jnp.concatenate([dq0_ref[:, span], dq1_ref[:, span]], axis=0)
            else:
                ours_ref, theirs_ref = ((dk_ref, dk_other_ref), (dv_ref, dv_other_ref))[part - 1]
                at, other = group * width, (1 - group) * width
                values = ours_ref[:, at : at + width] + theirs_ref[:, other : other + width]
                values = values.astype(BF16)
            span = slice(part * width, (part + 1) * width)
            if group == 0:
                own_ref[:, span] = values
                term = nn(values, w_ref[part])
            else:
                rows = values.shape[0]
                if part < 2:
                    send_ref[0:rows, span] = values.astype(F32)
                else:
                    send_ref[rows:, :width] = values[: rows // 2].astype(F32)
                    send_ref[rows:, width:] = values[rows // 2 :].astype(F32)
                term = nn(values, other_ref[span, :])
            total = term if total is None else total + term
    out_ref[...] = total


def first_grad(dqs, ours, theirs, weight, other, after=()):
    rows = ours[0].shape[0]
    _, width, model = weight.shape
    return call(
        first_grad_kernel,
        "first_grad",
        [
            shape_of((rows, model), F32),
            shape_of((rows, 3 * width), BF16),
            shape_of((rows + rows // 2, 2 * width), F32),
        ],
        after=after,
    )(*dqs, *ours, *theirs, weight, other)


def first_back_kernel(
    core_ref, ours_ref, theirs_ref, x_ref, middle0_ref, middle1_ref, vec_ref, kept0_ref, kept1_ref,
    out_ref, sums_ref, *res_refs,
):
    gain_sum = bias_sum = 0.0
    start = 0
    for middle_ref, kept_ref, res_ref in zip((middle0_ref, middle1_ref), (kept0_ref, kept1_ref), res_refs):
        res_ref[...] = kept_ref[kept_ref.shape[0] - res_ref.shape[0] :, :]
        count = middle_ref.shape[0]
        at = slice(start, start + count)
        grad = ours_ref[at, :] + theirs_ref[at, :]
        normal, factor = normalize(x_ref[half_of(core_ref, x_ref, start, count), :].astype(F32))
        total = middle_ref[...] + norm_back(grad, normal, factor, vector(vec_ref, LN1_GAIN))
        out_ref[at, :] = total.astype(BF16).astype(F32)
        gain_sum = gain_sum + column_sum(grad * normal)
        bias_sum = bias_sum + column_sum(grad)
        start += count
    sums_ref[0:1, :] = gain_sum
    sums_ref[1:2, :] = bias_sum


def first_back(core, ours, theirs, x, middles, vectors, kepts, counts, after=()):
    rows, model = ours.shape
    return call(
        first_back_kernel,
        "first_back",
        [shape_of((rows, model), F32), shape_of((8, model), F32)]
        + [shape_of((count, model), F32) for count in counts],
        scalars=1,
        after=after,
    )(core, ours, theirs, x, *middles, vectors, *kepts)


def result_kernel(*refs, starts, placed):
    vec_ref, out_ref = refs[3 * len(starts)], refs[-1]
    at = 0
    if placed:
        done_ref = refs[3 * len(starts) + 1]
        at = done_ref.shape[0]
        out_ref[0:at, :] = done_ref[...]
    for part, (start, rows) in enumerate(starts):
        ours_ref, theirs_ref, kept_ref = refs[3 * part : 3 * part + 3]
        fed = ours_ref[0:rows, :] + theirs_ref[0:rows, :] + vector(vec_ref, FC2_BIAS)
        total = kept_ref[start : start + rows, :] + fed
        out_ref[at : at + rows, :] = total.astype(BF16).astype(F32)
        at += rows


def result_rows(parts, vectors, done=(), after=()):
    operands = [array for part in parts for array in part[:3]]
    rows = sum(part[4] for part in parts) + sum(array.shape[0] for array in done)
    return call(
        functools.partial(
            result_kernel, starts=[part[3:] for part in parts], placed=bool(done)
        ),
        "result_rows",
        [shape_of((rows, vectors.shape[1]), F32)],
        after=after,
    )(*operands, vectors, *done)[0]


def finish_kernel(core_ref, ours_ref, theirs_ref, out_ref, in_ref, low_ref, in_sem, out_sem):
    count = in_ref.shape[0] // 2
    rows = in_ref.shape[1]
    reads, writes = [], []
    for index in range(2 * count):
        ref = ours_ref if index < count else theirs_ref
        at = (index % count) * rows
        read = pltpu.make_async_copy(ref.at[pl.ds(at, rows), :], in_ref.at[index], in_sem.at[index])
        read.start()
        reads.append(read)
    for index, read in enumerate(reads):
        half = core_ref[0] if index < count else 1 - core_ref[0]
        place = pl.multiple_of(half * count * rows + (index % count) * rows, 128)
        read.wait()
        low_ref[index] = in_ref[index].astype(BF16)
        write = pltpu.make_async_copy(
            low_ref.at[index], out_ref.at[pl.ds(place, rows), :], out_sem.at[index]
        )
        write.start()
        writes.append(write)
    for write in writes:
        write.wait()


def finish(core, pairs, after=()):
    ((ours, theirs),) = pairs
    rows, model = ours.shape
    pieces = 4
    held = [pltpu.VMEM((2 * pieces, rows // pieces, model), dtype) for dtype in (F32, BF16)]

    def run(*refs):
        finish_kernel(*refs[:3], *refs[3 + len(after) :])

    return pl.pallas_call(
        run,
        in_specs=[pl.BlockSpec(memory_space=pltpu.SMEM)]
        + [pl.BlockSpec(memory_space=pltpu.HBM)] * 2
        + [pl.BlockSpec(memory_space=pl.ANY)] * len(after),
        out_specs=pl.BlockSpec(memory_space=pltpu.HBM),
        scratch_shapes=[*held, pltpu.SemaphoreType.DMA((8,)), pltpu.SemaphoreType.DMA((8,))],
        out_shape=shape_of((2 * rows, model), BF16),
        compiler_params=pltpu.CompilerParams(vmem_limit_bytes=60 * 1024 * 1024),
        name="finish",
    )(core, ours, theirs, *after)


def gather_sums_kernel(second0, second1, feed0, feed1, norm, fc1, heads, partial_ref, whole_ref):
    partial_ref[...] = jnp.zeros_like(partial_ref)
    whole_ref[...] = jnp.zeros_like(whole_ref)
    partial_ref[0:1, :] = second0[2:3, :] + second1[2:3, :]
    partial_ref[1:2, :] = feed0[0:1, :] + feed1[0:1, :]
    partial_ref[2:4, :] = second0[0:2, :] + second1[0:2, :]
    partial_ref[4:6, :] = norm[0:2, :]
    whole_ref[6:7, :] = fc1[0:1, :]
    whole_ref[7:8, :] = heads[0:1, :]


def gather_sums(arrays, after=()):
    shape = shape_of(arrays[0].shape, F32)
    return call(gather_sums_kernel, "gather_sums", [shape, shape], after=after)(*arrays)


def feed_sum_kernel(ours_ref, theirs_ref, fc2_ref, fc1_ref):
    units = fc2_ref.shape[1]
    total = ours_ref[...] + theirs_ref[...]
    fc2_ref[...] = total[:, :units]
    fc1_ref[...] = total[:, units:]


def feed_sum(ours, theirs, after=()):
    half = shape_of((ours.shape[0], ours.shape[1] // 2), F32)
    return call(
        feed_sum_kernel, "feed_sum", [half, half], after=after
    )(ours, theirs)


def heads_sum_kernel(ours_ref, theirs_ref, heads_ref, out_ref):
    width = heads_ref.shape[2]
    total = ours_ref[...] + theirs_ref[...]
    for part in range(3):
        heads_ref[part] = total[:, part * width : (part + 1) * width]
    out_ref[...] = jnp.transpose(total[:, 3 * width :])


def heads_sum(ours, theirs, after=()):
    rows, width = ours.shape[0], ours.shape[1] // 4
    shapes = [shape_of((3, rows, width), F32), shape_of((width, rows), F32)]
    return call(
        heads_sum_kernel, "heads_sum", shapes, after=after
    )(ours, theirs)


def body(
    tokens,
    ln1_gain,
    ln1_bias,
    qkv_weight,
    qkv_bias,
    out_weight,
    out_bias,
    ln2_gain,
    ln2_bias,
    fc1_weight,
    fc1_bias,
    fc2_weight,
    fc2_bias,
    cotangent,
    *,
    batch_count,
    tensor_count,
):
    rows, model = tokens.shape[1:]
    width = qkv_weight.shape[2]
    units = fc1_weight.shape[1]
    bits = batch_count.bit_length() - 1
    batch_at = lax.axis_index("batch")
    core = (lax.axis_index("tensor") % 2).astype(jnp.int32).reshape(1)

    def core_swap(v):
        return lax.ppermute(v, "tensor", [(i, i ^ 1) for i in range(tensor_count)])

    def chip_swap(v):
        return lax.ppermute(v, "tensor", [(i, i ^ 2) for i in range(tensor_count)])

    def batch_swap(v, bit):
        return lax.ppermute(v, "batch", [(i, i ^ (1 << bit)) for i in range(batch_count)])

    last = []

    def then(made, *others):
        last[:] = [made[0], *others]
        return made

    orders = ([0, *range(1, bits)], [1, 0, *range(2, bits)])

    def mine_of(some):
        return jnp.stack([(batch_at >> bit) & 1 for bit in some]).astype(jnp.int32)

    class Scatter:
        def __init__(self, cut, order, left=range(bits - 1, -1, -1)):
            self.order = list(order)
            self.left = list(left)
            self.cross(cut)

        def cross(self, cut):
            send, self.keep = cut
            bit = self.order.pop(0)
            self.left.remove(bit)
            self.theirs = batch_swap(send, bit)

        def step(self, *others):
            bit = self.order[0]
            pairs = [(v.keep, v.theirs) for v in (self, *others)]
            self.cross(
                then(hop(mine_of([bit]), pairs, 1 << len(self.left), self.left.index(bit), after=last))
            )

        def end(self, summed):
            while self.order:
                self.step()
            return then(summed(self.keep, self.theirs, after=last))

    def weight_scatters(kernel, operands, widths, orders, held, sums=True):
        width = sum(widths)
        spans = [slice(sum(widths[:i]), sum(widths[: i + 1])) for i in range(len(widths))]
        firsts = [order[0] for order in orders]
        made = then(
            weight_grad(
                kernel, core, mine_of(firsts), operands, model, width, spans, batch_count,
                [bits - 1 - bit for bit in firsts], sums=sums, far=(), held=held, after=last,
            )
        )
        return [Scatter(made[2 * i : 2 * i + 2], order) for i, order in enumerate(orders)], made[-1]

    x = tokens.reshape(rows, model)
    dy = cotangent.reshape(rows, model)
    heads_weight = jnp.transpose(qkv_weight, (1, 2, 0))
    listed = (
        ln1_gain, ln1_bias, jnp.transpose(qkv_bias, (1, 0, 2)), out_bias, ln2_gain, ln2_bias, fc1_bias,
        fc2_bias,
    )
    vectors, heads_wide, out_weight_wide = pack(listed, heads_weight, out_weight)

    heads_other = core_swap(heads_wide)
    out_weight_far = chip_swap(out_weight_wide)
    others = then(
        convert([fc1_weight, fc2_weight, out_weight], F32, vmem=60, after=[heads_wide])
    )
    others = [core_swap(v) for v in others]
    other_bias = heads_other[3 * width + FC1_BIAS :]

    left, queries, keys, values = then(
        project(core, x, vectors, heads_weight, heads_other, after=last)
    )
    near, totals = then(attend(queries, keys, values, after=last))
    far = chip_swap(near)
    fc1_other, fc2_other, out_weight_other, heads_other_low = then(
        convert([*others, heads_other], BF16, after=last)
    )
    dy_turned = then(turn(dy, after=last))[0]
    out_weight_both = core_swap(out_weight_far)
    out_weights = (out_weight, out_weight_other, out_weight_far, out_weight_both)

    half = rows // 2
    sizes = (3 * half // 4, half // 4)
    starts = (0, sizes[0])
    fed = []
    for start, size in zip(starts, sizes):
        fed.append(
            then(
                feed(
                    core, start, size, x, dy, near, far, out_weights, vectors, other_bias, fc1_weight,
                    fc2_weight, (fc1_other, fc2_other), after=last,
                )
            )
        )
    kepts, owns = [f[0] for f in fed], [f[1] for f in fed]
    grads, feed_sums = [f[-2] for f in fed], [f[-1] for f in fed]
    grads_far = [chip_swap(v) for v in grads]
    swaps = [core_swap(v) for f in fed for v in f[2:-2]]
    (fc2,), _ = weight_scatters(
        fc2_grad_kernel, [dy_turned, *owns, *swaps], [units], orders[1:],
        [
            pltpu.VMEM((model, rows), BF16),
            *(pltpu.VMEM((size, units), dtype) for dtype in (BF16, F32) for size in sizes),
            pltpu.SemaphoreType.DMA((5,)),
        ],
        sums=False
    )
    (fc1,), fc1_sums = weight_scatters(fc1_grad_kernel, [*owns, *swaps], [units], orders[:1],
        [
            *(pltpu.VMEM((2 * size, units), dtype) for dtype in (BF16, F32) for size in sizes),
            pltpu.SemaphoreType.DMA((5,)),
        ],
    )

    weights = (out_weight, out_weight_other)
    heads = (queries, keys, values, totals)
    middle0, low0, second_sums0, res0 = then(
        second_back(core, 0, grads[0], grads_far[0], kepts[0], dy, vectors, after=last)
    )
    res0_far = chip_swap(res0)
    dq0, dk0, dv0 = then(attend_back(core, 0, low0, weights, *heads, after=last))
    middle1, low1, second_sums1, out_w = then(
        second_back(
            core, starts[1], grads[1], grads_far[1], kepts[1], dy, vectors, (low0, near),
            after=last,
        )
    )
    out_w_other = core_swap(out_w)
    dq1, dk_send, dv_send, dk, dv = then(
        attend_back(core, starts[1], low1, weights, *heads, (dk0, dv0), after=last)
    )
    theirs = core_swap(dk_send), core_swap(dv_send)
    fc2.step()
    fc1.step()
    grad_rows, heads_own, send = then(
        first_grad(
            (dq0, dq1), (dk, dv), theirs, heads_weight, heads_other_low, after=[*last, res0_far]
        )
    )
    grad_rows_far = chip_swap(grad_rows)
    heads_theirs = core_swap(send)
    heads, heads_sums = weight_scatters(
        heads_grad_kernel,
        [left, heads_own, heads_theirs, low0, low1, near, out_w_other],
        [8 * width // 3, 4 * width // 3],
        orders,
        (),
    )
    result0 = then([result_rows([(res0, res0_far, kepts[0], 0, BLOCK)], vectors, after=last)])[0]
    fc2.step(fc1)
    heads[1].step()
    heads[0].step()
    counts = (sizes[0] - BLOCK, sizes[1])
    grad_rows, norm_sums, *res1 = then(
        first_back(
            core, grad_rows, grad_rows_far, x, (middle0, middle1), vectors, kepts, counts, after=last
        )
    )
    grad_rows_other = core_swap(grad_rows)
    res1_far = [chip_swap(v) for v in res1]
    grad_fc2, grad_fc1 = fc2.end(feed_sum)
    heads[0].step(heads[1])
    partial, whole = then(
        gather_sums(
            (second_sums0, second_sums1, *feed_sums, norm_sums, fc1_sums, heads_sums), after=last
        )
    )
    small = partial + core_swap(partial) + whole
    for bit in range(bits):
        small = small + batch_swap(small, bit)
    grad_heads, grad_out = heads[0].end(heads_sum)
    last.append(small)
    parts = [
        (v, far, kept, start, count)
        for v, far, kept, start, count in zip(res1, res1_far, kepts, (BLOCK, 0), counts)
    ]
    result = then([result_rows(parts, vectors, [result0], after=last)])[0]
    result_other = core_swap(result)
    grad_tokens = then([finish(core, [(grad_rows, grad_rows_other)], after=last)])[0]
    result = then([finish(core, [(result, result_other)], after=last)])[0]
    share = HD // batch_count
    piece = model // batch_count
    shared = lax.dynamic_slice_in_dim(small[:6], batch_at * piece, piece, 1)
    own = lax.dynamic_slice_in_dim(
        small[6:].reshape(2, model // HD, HD), batch_at * share, share, 2
    )
    return (
        result.reshape(tokens.shape),
        grad_tokens.reshape(tokens.shape),
        jnp.transpose(grad_heads, (1, 0, 2)),
        own[1, : 3 * width // HD].reshape(3, width // HD, share)[::2],
        grad_out,
        shared[0],
        shared[4],
        shared[5],
        shared[2],
        shared[3],
        grad_fc1,
        own[0, : units // HD],
        grad_fc2.T,
        shared[1],
    )


def solution(mesh):
    placed = (
        P("batch", None, None),
        P(),
        P(),
        P(None, None, "tensor"),
        P(None, "tensor", None),
        P("tensor", None),
        P(),
        P(),
        P(),
        P(None, "tensor"),
        P("tensor", None),
        P("tensor", None),
        P(),
        P("batch", None, None),
    )
    return jax.shard_map(
        functools.partial(
            body, batch_count=mesh.shape["batch"], tensor_count=mesh.shape["tensor"]
        ),
        mesh=mesh,
        in_specs=placed,
        out_specs=(
            P("batch", None, None),
            P("batch", None, None),
            P("batch", None, "tensor"),
            P(None, "tensor", "batch"),
            P("tensor", "batch"),
            P("batch"),
            P("batch"),
            P("batch"),
            P("batch"),
            P("batch"),
            P("batch", "tensor"),
            P("tensor", "batch"),
            P("tensor", "batch"),
            P("batch"),
        ),
        check_vma=False,
    )
```

```python
import functools
import math

import jax
import jax.numpy as jnp
from jax import lax
from jax.experimental import pallas as pl
from jax.experimental.pallas import tpu as pltpu
from jax.sharding import PartitionSpec as P

HD = 64
LN1_GAIN, LN1_BIAS, HEADS_BIAS, OUT_BIAS, LN2_GAIN, LN2_BIAS, FC1_BIAS, FC2_BIAS = range(8)
BLOCK = 256
EPSILON = 1e-06
F32 = jnp.float32
BF16 = jnp.bfloat16


def nn(a, b):
    return lax.dot_general(a, b, (((1,), (0,)), ((), ())), preferred_element_type=F32)


def nt(a, b):
    return lax.dot_general(a, b, (((1,), (1,)), ((), ())), preferred_element_type=F32)


def tn(a, b):
    return lax.dot_general(a, b, (((0,), (0,)), ((), ())), preferred_element_type=F32)


def call(kernel, name, out_shape, scalars=0, scratch=(), after=(), far_in=(), far_out=(), vmem=20, raw_in=(), raw_out=()):

    def run(*args):
        given = len(args)
        ins = [scalars + index for index in far_in]
        outs = list(far_out)
        made = len(out_shape)

        def inner(*refs):
            first = given + len(after)
            operands, results = list(refs[:given]), list(refs[first : first + made])
            held = list(refs[first + made : first + made + len(scratch)])
            spare = list(refs[first + made + len(scratch) :])
            sems = spare.pop() if spare else None
            copies = []
            for count, index in enumerate(ins):
                copies.append(pltpu.make_async_copy(operands[index], spare[count], sems.at[count]))
                operands[index] = spare[count]
            for copy in copies:
                copy.start()
            far = [results[index] for index in outs]
            for count, index in enumerate(outs):
                results[index] = spare[len(ins) + count]
            for copy in copies:
                copy.wait()
            kernel(*operands, *results, *held)
            copies = []
            for count, ref in enumerate(far, len(ins)):
                copies.append(pltpu.make_async_copy(spare[count], ref, sems.at[count]))
            for copy in copies:
                copy.start()
            for copy in copies:
                copy.wait()

        def space(index, chosen):
            return pl.BlockSpec(memory_space=pltpu.HBM if index in chosen else pltpu.VMEM)

        moved = [args[index] for index in ins] + [out_shape[index] for index in outs]
        held = list(scratch) + [pltpu.VMEM(v.shape, v.dtype) for v in moved]
        if moved:
            held.append(pltpu.SemaphoreType.DMA((len(moved),)))
        return pl.pallas_call(
            inner,
            in_specs=[pl.BlockSpec(memory_space=pltpu.SMEM)] * scalars
            + [space(index, [*ins, *(scalars + at for at in raw_in)]) for index in range(scalars, given)]
            + [pl.BlockSpec(memory_space=pl.ANY)] * len(after),
            out_specs=[space(index, [*outs, *raw_out]) for index in range(made)],
            scratch_shapes=held,
            out_shape=out_shape,
            compiler_params=pltpu.CompilerParams(vmem_limit_bytes=vmem * 1024 * 1024),
            name=name,
        )(*args, *after)

    return run


def shape_of(shape, dtype):
    return jax.ShapeDtypeStruct(shape, dtype)


def vector(ref, row, width=None):
    return ref[row : row + 1, : ref.shape[1] if width is None else width]


def normalize(values):
    average = jnp.mean(values, axis=-1, keepdims=True)
    centered = values - average
    spread = jnp.mean(centered * centered, axis=-1, keepdims=True)
    factor = lax.rsqrt(spread + EPSILON)
    return centered * factor, factor


def half_of(core_ref, ref, offset=0, rows=None):
    size = ref.shape[0] // 2
    rows = size if rows is None else rows
    return pl.ds(pl.multiple_of(core_ref[0] * size + offset, 128), rows)


def pack_kernel(
    g1_ref, b1_ref, bias_ref, ob_ref, g2_ref, b2_ref, fc1_bias_ref, fb_ref, w_ref, out_w_ref,
    vec_ref, wide_ref, out_wide_ref,
):
    width = w_ref.shape[1]
    vec_ref[...] = jnp.zeros_like(vec_ref)
    for row, ref in (
        (LN1_GAIN, g1_ref),
        (LN1_BIAS, b1_ref),
        (OUT_BIAS, ob_ref),
        (LN2_GAIN, g2_ref),
        (LN2_BIAS, b2_ref),
        (FC2_BIAS, fb_ref),
    ):
        vec_ref[row : row + 1, :] = ref[...].reshape(1, -1)
    for head in range(bias_ref.shape[0]):
        for part, start in ((0, 0), (1, 2 * width)):
            at = start + head * HD
            vec_ref[HEADS_BIAS : HEADS_BIAS + 1, at : at + HD] = bias_ref[head, part : part + 1, :]
    for head in range(fc1_bias_ref.shape[0]):
        at = slice(head * HD, (head + 1) * HD)
        vec_ref[FC1_BIAS : FC1_BIAS + 1, at] = fc1_bias_ref[head : head + 1, :]
    for part in range(3):
        wide_ref[part * width : (part + 1) * width, :] = w_ref[part].astype(F32)
    wide_ref[3 * width :, :] = vec_ref[...]
    out_wide_ref[0:width, :] = out_w_ref[...].astype(F32)


def pack(listed, heads_weight, out_weight):
    width, model = out_weight.shape
    return call(
        pack_kernel,
        "pack",
        [
            shape_of((8, model), F32),
            shape_of((3 * width + 8, model), F32),
            shape_of((width + 8, model), F32),
        ],
        vmem=60,
    )(*listed, heads_weight, out_weight)


def project_kernel(
    core_ref, x_ref, vec_ref, w_ref, far_other_ref, all_ref, q_ref, k_ref, v_ref, other_ref, sem
):
    width = w_ref.shape[1]
    copy = pltpu.make_async_copy(far_other_ref, other_ref, sem)
    copy.start()
    for start in range(0, x_ref.shape[0], BLOCK):
        at = slice(start, start + BLOCK)
        normal, _ = normalize(x_ref[at, :].astype(F32))
        all_ref[at, :] = (normal * vector(vec_ref, LN1_GAIN) + vector(vec_ref, LN1_BIAS)).astype(BF16)
    left = all_ref[...]
    mine = all_ref[half_of(core_ref, all_ref), :]
    bias_row = 3 * width + HEADS_BIAS
    for group in range(2):
        if group == 1:
            copy.wait()
        bias = vector(vec_ref, HEADS_BIAS) if group == 0 else other_ref[bias_row : bias_row + 1, :]
        for part, (ref, rows) in enumerate(((q_ref, mine), (k_ref, left), (v_ref, left))):
            span = slice(part * width, (part + 1) * width)
            weight = w_ref[part] if group == 0 else other_ref[span, :].astype(BF16)
            ref[:, group * width : (group + 1) * width] = (
                nt(rows, weight) + bias[:, span]
            ).astype(BF16)


def project(core, x, vectors, weight, other, after=()):
    rows, model = x.shape
    width = weight.shape[1]
    both = 2 * width
    return call(
        project_kernel,
        "project",
        [
            shape_of((rows, model), BF16),
            shape_of((rows // 2, both), BF16),
            shape_of((rows, both), BF16),
            shape_of((rows, both), BF16),
        ],
        scalars=1,
        scratch=[pltpu.VMEM(other.shape, F32), pltpu.SemaphoreType.DMA],
        raw_in=(3,),
        after=after,
    )(core, x, vectors, weight, other)


def attend_kernel(q_ref, k_ref, v_ref, out_ref, total_ref):
    heads = q_ref.shape[1] // HD
    scale = jnp.asarray(1.0 / math.sqrt(HD), BF16)
    parts = []
    logs = []
    for head in range(heads):
        at = slice(head * HD, (head + 1) * HD)
        scores = nt(q_ref[:, at] * scale, k_ref[:, at])
        peak = jnp.max(scores, axis=1, keepdims=True)
        powers = jnp.exp(scores - peak)
        totals = jnp.sum(powers, axis=1, keepdims=True)
        parts.append(nn(powers.astype(BF16), v_ref[:, at]) / totals)
        logs.append(peak + jnp.log(totals))
    mixed = jnp.concatenate(parts, axis=1).astype(BF16).astype(F32)
    out_ref[...] = mixed
    logs.append(jnp.zeros((q_ref.shape[0], total_ref.shape[1] - heads), F32))
    total_ref[...] = jnp.concatenate(logs, axis=1)


def attend(queries, keys, values, after=()):
    rows, width = queries.shape
    return call(
        attend_kernel,
        "attend",
        [shape_of((rows, width), F32), shape_of((rows, 8), F32)],
        after=after,
    )(queries, keys, values)


def convert_kernel(*refs):
    half = len(refs) // 2
    for ref, out_ref in zip(refs[:half], refs[half:]):
        out_ref[...] = ref[...].astype(out_ref.dtype)


def widen_kernel(*refs, parts, given):
    ins, outs, (read_ref, wide_ref, in_sem, out_sem) = refs[:given], refs[given : 2 * given], refs[2 * given :]
    rows = read_ref.shape[1]
    reads, writes = [], []
    for index, (array, at) in enumerate(parts):
        read = pltpu.make_async_copy(
            ins[array].at[pl.ds(at, rows), :], read_ref.at[index], in_sem.at[index]
        )
        read.start()
        reads.append(read)
    for index, (array, at) in enumerate(parts):
        reads[index].wait()
        wide_ref[index] = read_ref[index].astype(F32)
        write = pltpu.make_async_copy(
            wide_ref.at[index], outs[array].at[pl.ds(at, rows), :], out_sem.at[index]
        )
        write.start()
        writes.append(write)
    for write in writes:
        write.wait()


def widen(arrays, after=()):
    model = arrays[0].shape[1]
    rows = min(array.shape[0] for array in arrays)
    parts = [(index, at) for index, v in enumerate(arrays) for at in range(0, v.shape[0], rows)]
    count = len(parts)
    indices = tuple(range(len(arrays)))
    return call(
        functools.partial(widen_kernel, parts=parts, given=len(arrays)),
        "widen",
        [shape_of(array.shape, F32) for array in arrays],
        scratch=[
            pltpu.VMEM((count, rows, model), BF16),
            pltpu.VMEM((count, rows, model), F32),
            pltpu.SemaphoreType.DMA((count,)),
            pltpu.SemaphoreType.DMA((count,)),
        ],
        after=after,
        raw_in=indices,
        raw_out=indices,
        vmem=60,
    )(*arrays)


def convert(arrays, dtype, vmem=20, after=()):
    shapes = [shape_of(array.shape, dtype) for array in arrays]
    return call(convert_kernel, "convert", shapes, after=after, vmem=vmem)(*arrays)


ERF = (0.254829592, -0.284496736, 1.421413741, -1.453152027, 1.061405429)


def gelu_pair(values):
    size = jnp.abs(values) * (1.0 / math.sqrt(2.0))
    step = 1.0 / (1.0 + 0.3275911 * size)
    bell = jnp.exp(-(size * size))
    series = ERF[4]
    for factor in (ERF[3], ERF[2], ERF[1], ERF[0]):
        series = series * step + factor
    tail = (0.5 * step) * series * bell
    below = jnp.where(values >= 0, 1.0 - tail, tail)
    return values * below, below + values * (bell * (1.0 / math.sqrt(2.0 * math.pi)))


def feed_kernel(
    core_ref,
    x_ref,
    dy_ref,
    near_ref,
    far_ref,
    w0_ref,
    w1_ref,
    w2_ref,
    w3_ref,
    vec_ref,
    other_vec_ref,
    fc1_ref,
    fc2_ref,
    other_fc1_ref,
    other_fc2_ref,
    *refs,
    start,
):
    kept_ref, own_ref, *swap_refs, grad_ref, sums_ref = refs
    count = grad_ref.shape[0]
    rows = slice(start, start + count)
    place = half_of(core_ref, x_ref, start, count)
    width = w0_ref.shape[0]
    units = fc1_ref.shape[1]

    def share(ref, part, w_ref):
        return nn(ref[rows, part * width : (part + 1) * width].astype(BF16), w_ref[0:width, :].astype(BF16))

    branch = (share(near_ref, 0, w0_ref) + share(near_ref, 1, w1_ref)) + (
        share(far_ref, 0, w2_ref) + share(far_ref, 1, w3_ref)
    )
    middle = x_ref[place, :].astype(F32) + (branch + vector(vec_ref, OUT_BIAS))
    kept_ref[0:count, :] = middle
    normal, _ = normalize(middle)
    left = (normal * vector(vec_ref, LN2_GAIN) + vector(vec_ref, LN2_BIAS)).astype(BF16)
    own_ref[0:count, :] = left
    dy = dy_ref[place, :]
    grad = res = None
    groups = ((vec_ref, FC1_BIAS, fc1_ref, fc2_ref), (other_vec_ref, 0, other_fc1_ref, other_fc2_ref))
    for group, (bias_ref, bias_row, in_ref, out_ref) in enumerate(groups):
        hidden, slope = gelu_pair(nn(left, in_ref[...]) + vector(bias_ref, bias_row, units))
        hidden = hidden.astype(BF16)
        pre = (nt(dy, out_ref[...]) * slope).astype(BF16)
        if group == 0:
            own_ref[count : 2 * count, :] = pre
            own_ref[2 * count :, :] = hidden
        else:
            at = 0
            wide = jnp.concatenate([left, pre, hidden], axis=0).astype(F32)
            for ref in swap_refs:
                size = 3 * count // len(swap_refs)
                ref[0:size, :] = wide[at : at + size]
                at += size
        back = nt(pre, in_ref[...])
        fed = nn(hidden, out_ref[...])
        grad = back if grad is None else grad + back
        res = fed if res is None else res + fed
    grad_ref[...] = grad
    kept_ref[count:, :] = res
    sums_ref[0:1, :] = jnp.sum(dy.astype(F32), axis=0, keepdims=True)


def feed(core, start, count, x, dy, near, far, out_weights, vectors, other_bias, fc1, fc2, other, after=()):
    model = x.shape[1]
    swaps = [3 * count + 8] if start == 0 else [3 * count // 2] * 2
    return call(
        functools.partial(feed_kernel, start=start),
        "feed",
        [shape_of((2 * count, model), F32), shape_of((3 * count, model), BF16)]
        + [shape_of((size, model), F32) for size in swaps]
        + [shape_of((count, model), F32), shape_of((8, model), F32)],
        scalars=1,
        after=after,
    )(core, x, dy, near, far, *out_weights, vectors, other_bias, fc1, fc2, *other)


def cut_pieces(ref, send_ref, keep_ref, mine, count, axis_bits, axis):
    rows = ref.shape[0] // count
    stride = 1 << (axis_bits - 1 - axis)
    for value in range(2):

        @pl.when(mine == value)
        def _():
            for index in range(count):
                place = (index // (2 * stride)) * stride + index % stride
                out = keep_ref if (index // stride) % 2 == value else send_ref
                out[place * rows : (place + 1) * rows, :] = ref[index * rows : (index + 1) * rows, :]


def cut_spans(total_ref, refs, mine_ref, spans, count, axes):
    axis_bits = count.bit_length() - 1
    for index, (span, axis) in enumerate(zip(spans, axes)):
        cut_pieces(
            total_ref.at[:, span], refs[2 * index], refs[2 * index + 1], mine_ref[index], count,
            axis_bits, axis,
        )


def cut_shapes(rows, spans):
    shapes = []
    for span in spans:
        shapes += [shape_of((rows // 2, span.stop - span.start), F32)] * 2
    return shapes


def column_sum(values):
    return jnp.sum(values.astype(F32), axis=0, keepdims=True)


def turn_kernel(ref, out_ref):
    out_ref[...] = jnp.transpose(ref[...])


def turn(array, after=()):
    return call(turn_kernel, "turn", [shape_of(array.shape[::-1], array.dtype)], after=after)(array)


def fetch(pairs, sem):
    copies = [
        pltpu.make_async_copy(source, target, sem.at[index])
        for index, (source, target) in enumerate(pairs)
    ]
    for copy in copies:
        copy.start()
    return copies


def fc2_grad_kernel(core_ref, mine_ref, dy_ref, own0, own1, swap0, swap1, swap2, *refs, spans, count, axes):
    cuts, (total_ref, dy_held, h0, h1, t0, t1, sem) = refs[:-7], refs[-7:]
    n0, n1 = h0.shape[0], h1.shape[0]
    copies = fetch(
        [
            (dy_ref, dy_held),
            (own0.at[pl.ds(2 * n0, n0), :], h0),
            (own1.at[pl.ds(2 * n1, n1), :], h1),
            (swap0.at[pl.ds(2 * n0, n0), :], t0),
            (swap2.at[pl.ds(n1 // 2, n1), :], t1),
        ],
        sem,
    )
    copies[0].wait()
    total = None
    for index, (held, start, half) in enumerate(
        ((h0, 0, core_ref[0]), (h1, n0, core_ref[0]), (t0, 0, 1 - core_ref[0]), (t1, n0, 1 - core_ref[0]))
    ):
        copies[index + 1].wait()
        place = pl.multiple_of(half * (dy_held.shape[1] // 2) + start, 128)
        term = nn(dy_held[:, pl.ds(place, held.shape[0])], held[...].astype(BF16))
        total = term if total is None else total + term
    total_ref[...] = total
    cut_spans(total_ref, cuts, mine_ref, spans, count, axes)


def fc1_grad_kernel(core_ref, mine_ref, own0, own1, swap0, swap1, swap2, *refs, spans, count, axes):
    cuts, (sums_ref, total_ref, h0, h1, t0, t1, sem) = refs[:-7], refs[-7:]
    n0, n1 = h0.shape[0] // 2, h1.shape[0] // 2
    copies = fetch(
        [
            (own0.at[pl.ds(0, 2 * n0), :], h0),
            (own1.at[pl.ds(0, 2 * n1), :], h1),
            (swap0.at[pl.ds(0, 2 * n0), :], t0),
            (swap1, t1.at[pl.ds(0, 3 * n1 // 2), :]),
            (swap2.at[pl.ds(0, n1 // 2), :], t1.at[pl.ds(3 * n1 // 2, n1 // 2), :]),
        ],
        sem,
    )
    total = None
    sums = 0.0
    for index, held in enumerate((h0, h1, t0, t1)):
        copies[index].wait()
        if index == 3:
            copies[4].wait()
        size = held.shape[0] // 2
        left, pre = held[0:size, :].astype(BF16), held[size:, :].astype(BF16)
        term = tn(left, pre)
        total = term if total is None else total + term
        sums = sums + column_sum(pre)
    total_ref[...] = total
    sums_ref[0:1, :] = sums
    cut_spans(total_ref, cuts, mine_ref, spans, count, axes)


def chunk_products(lows, near_ref, columns):
    at = 0
    total = None
    for low in lows:
        term = tn(low[...], near_ref[at : at + low.shape[0], columns].astype(BF16))
        total = term if total is None else total + term
        at += low.shape[0]
    return total


def heads_grad_kernel(
    core_ref, mine_ref, left_ref, ours_ref, theirs_ref, low0_ref, low1_ref, near_ref, out_w_ref,
    *refs, spans, count, axes,
):
    sums_ref, total_ref = refs[-2:]
    rows = left_ref.shape[0] // 2
    width = near_ref.shape[1] // 2
    ours = ours_ref[...]
    theirs = jnp.concatenate(
        [
            theirs_ref[0:rows, :],
            jnp.concatenate([theirs_ref[rows:, :width], theirs_ref[rows:, width:]], axis=0),
        ],
        axis=1,
    ).astype(BF16)
    left = left_ref[half_of(core_ref, left_ref), :]
    left_other = left_ref[pl.ds(pl.multiple_of((1 - core_ref[0]) * rows, BLOCK), rows), :]
    total_ref[:, : 3 * width] = tn(left, ours) + tn(left_other, theirs)
    out_w = jnp.concatenate([out_w_ref[:, :width], out_w_ref[:, width:]], axis=0)
    total_ref[:, 3 * width :] = out_w + chunk_products((low0_ref, low1_ref), near_ref, slice(0, width))
    sums_ref[...] = jnp.zeros_like(sums_ref)
    sums_ref[0:1, : 3 * width] = column_sum(ours) + column_sum(theirs)
    cut_spans(total_ref, refs[:-2], mine_ref, spans, count, axes)


def weight_grad(
    kernel, core, mine, operands, model, width, spans, count, axes, sums, far, held=(), after=()
):
    raw = tuple(range(len(operands))) if held else ()
    return call(
        functools.partial(kernel, spans=spans, count=count, axes=axes),
        "weight_grad",
        cut_shapes(model, spans) + ([shape_of((8, model), F32)] if sums else []),
        scalars=2,
        scratch=[pltpu.VMEM((model, width), F32), *held],
        after=after,
        raw_in=raw,
        vmem=60 if held else 20,
    )(core, mine, *operands)


def hop_kernel(mine_ref, *refs, pairs, spans, count, axes):
    total_ref = refs[-1]
    at = 0
    for pair in range(pairs):
        ours, theirs = refs[2 * pair], refs[2 * pair + 1]
        total_ref[:, at : at + ours.shape[1]] = ours[...] + theirs[...]
        at += ours.shape[1]
    cut_spans(total_ref, refs[2 * pairs : -1], mine_ref, spans, count, axes)


def hop(mine, pairs, count, axis, after=()):
    operands = [array for pair in pairs for array in pair]
    rows = operands[0].shape[0]
    width = sum(pair[0].shape[1] for pair in pairs)
    spans = [slice(0, width)]
    return call(
        functools.partial(hop_kernel, pairs=len(pairs), spans=spans, count=count, axes=[axis]),
        "hop",
        cut_shapes(rows, spans),
        scalars=1,
        scratch=[pltpu.VMEM((rows, width), F32)],
        after=after,
    )(mine, *operands)


def norm_back(grad, normal, factor, gain):
    scaled = grad * gain
    first = jnp.mean(scaled, axis=-1, keepdims=True)
    second = jnp.mean(scaled * normal, axis=-1, keepdims=True)
    return factor * (scaled - first - normal * second)


def second_back_kernel(core_ref, ours_ref, theirs_ref, kept_ref, dy_ref, vec_ref, *refs, start):
    grad_ref, low_ref, sums_ref, last_ref = refs[-4:]
    count = ours_ref.shape[0]
    grad = ours_ref[...] + theirs_ref[...]
    normal, factor = normalize(kept_ref[0:count, :])
    dy = dy_ref[half_of(core_ref, dy_ref, start, count), :].astype(F32)
    total = dy + norm_back(grad, normal, factor, vector(vec_ref, LN2_GAIN))
    grad_ref[...] = total
    low = total.astype(BF16)
    low_ref[...] = low
    for index, term in enumerate((grad * normal, grad, low.astype(F32))):
        sums_ref[index : index + 1, :] = column_sum(term)
    if start == 0:
        rows = last_ref.shape[0] - 8
        last_ref[0:rows, :] = kept_ref[count : count + rows, :]
    else:
        low0_ref, near_ref = refs[:2]
        width = near_ref.shape[1] // 2
        product = chunk_products((low0_ref, low_ref), near_ref, slice(width, 2 * width))
        last_ref[:, :width] = product[: product.shape[0] // 2]
        last_ref[:, width:] = product[product.shape[0] // 2 :]


def second_back(core, start, ours, theirs, kept, dy, vectors, others=(), after=()):
    rows, model = ours.shape
    out_shape = [shape_of((rows, model), F32), shape_of((rows, model), BF16), shape_of((8, model), F32)]
    if others:
        out_shape.append(shape_of((model // 2, others[1].shape[1]), F32))
    else:
        out_shape.append(shape_of((BLOCK + 8, model), F32))
    return call(
        functools.partial(second_back_kernel, start=start),
        "second_back",
        out_shape,
        scalars=1,
        after=after,
    )(core, ours, theirs, kept, dy, vectors, *others)


def attend_back_kernel(core_ref, low_ref, w0_ref, w1_ref, q_ref, k_ref, v_ref, total_ref, *refs, start):
    if start:
        dk0_ref, dv0_ref, dq_ref, dk_send_ref, dv_send_ref, dk_ref, dv_ref, scratch_ref = refs
    else:
        dq_ref, dk_ref, dv_ref = refs
    rows_here = slice(start, start + low_ref.shape[0])
    heads = q_ref.shape[1] // HD
    scale = jnp.asarray(1.0 / math.sqrt(HD), BF16)
    low = low_ref[...]
    outers = [nt(low, ref[...]).astype(BF16) for ref in (w0_ref, w1_ref)]
    outer = jnp.concatenate(outers, axis=1)
    dqs = []
    dks = []
    dvs = []
    for head in range(heads):
        at = slice(head * HD, (head + 1) * HD)
        queries = q_ref[rows_here, at] * scale
        keys = k_ref[:, at]
        outer_here = outer[:, at]
        probs = jnp.exp(nt(queries, keys) - total_ref[rows_here, head : head + 1])
        grad_probs = nt(outer_here, v_ref[:, at])
        inner = jnp.sum(probs * grad_probs, axis=1, keepdims=True)
        grad_scores = (probs * (grad_probs - inner)).astype(BF16)
        dvs.append(tn(outer_here, probs.astype(BF16)))
        dks.append(tn(queries, grad_scores))
        dqs.append(nn(grad_scores, keys))
    dq_ref[...] = (jnp.concatenate(dqs, axis=1) * (1.0 / math.sqrt(HD))).astype(BF16)
    if not start:
        dk_ref[...] = jnp.concatenate(dks, axis=0)
        dv_ref[...] = jnp.concatenate(dvs, axis=0)
        return
    for parts, before_ref, send_ref, keep_ref in (
        (dks, dk0_ref, dk_send_ref, dk_ref),
        (dvs, dv0_ref, dv_send_ref, dv_ref),
    ):
        scratch_ref[...] = jnp.transpose(before_ref[...] + jnp.concatenate(parts, axis=0))
        rows = scratch_ref.shape[0] // 2
        for ref, half in ((send_ref, 1 - core_ref[0]), (keep_ref, core_ref[0])):
            ref[...] = scratch_ref[pl.ds(pl.multiple_of(half * rows, BLOCK), rows), :]


def attend_back(core, start, low, out_weights, queries, keys, values, totals, before=(), after=()):
    rows, width = keys.shape
    sums = [shape_of((rows // 2, width), F32)] * 4 if before else [shape_of((width, rows), F32)] * 2
    return call(
        functools.partial(attend_back_kernel, start=start),
        "attend_back",
        [shape_of((low.shape[0], width), BF16)] + sums,
        scalars=1,
        scratch=[pltpu.VMEM((rows, width), F32)] if before else [],
        after=after,
    )(core, low, *out_weights, queries, keys, values, totals, *before)


def first_grad_kernel(
    dq0_ref, dq1_ref, dk_ref, dv_ref, dk_other_ref, dv_other_ref, w_ref, other_ref, out_ref, own_ref, send_ref
):
    width = w_ref.shape[1]
    total = None
    for part in range(3):
        for group in range(2):
            if part == 0:
                span = slice(group * width, (group + 1) * width)
                values = jnp.concatenate([dq0_ref[:, span], dq1_ref[:, span]], axis=0)
            else:
                ours_ref, theirs_ref = ((dk_ref, dk_other_ref), (dv_ref, dv_other_ref))[part - 1]
                at, other = group * width, (1 - group) * width
                values = ours_ref[:, at : at + width] + theirs_ref[:, other : other + width]
                values = values.astype(BF16)
            span = slice(part * width, (part + 1) * width)
            if group == 0:
                own_ref[:, span] = values
                term = nn(values, w_ref[part])
            else:
                rows = values.shape[0]
                if part < 2:
                    send_ref[0:rows, span] = values.astype(F32)
                else:
                    send_ref[rows:, :width] = values[: rows // 2].astype(F32)
                    send_ref[rows:, width:] = values[rows // 2 :].astype(F32)
                term = nn(values, other_ref[span, :])
            total = term if total is None else total + term
    out_ref[...] = total


def first_grad(dqs, ours, theirs, weight, other, after=()):
    rows = ours[0].shape[0]
    _, width, model = weight.shape
    return call(
        first_grad_kernel,
        "first_grad",
        [
            shape_of((rows, model), F32),
            shape_of((rows, 3 * width), BF16),
            shape_of((rows + rows // 2, 2 * width), F32),
        ],
        after=after,
    )(*dqs, *ours, *theirs, weight, other)


def first_back_kernel(
    core_ref, ours_ref, theirs_ref, x_ref, middle0_ref, middle1_ref, vec_ref, kept0_ref, kept1_ref,
    out_ref, sums_ref, *res_refs,
):
    gain_sum = bias_sum = 0.0
    start = 0
    for middle_ref, kept_ref, res_ref in zip((middle0_ref, middle1_ref), (kept0_ref, kept1_ref), res_refs):
        res_ref[...] = kept_ref[kept_ref.shape[0] - res_ref.shape[0] :, :]
        count = middle_ref.shape[0]
        at = slice(start, start + count)
        grad = ours_ref[at, :] + theirs_ref[at, :]
        normal, factor = normalize(x_ref[half_of(core_ref, x_ref, start, count), :].astype(F32))
        total = middle_ref[...] + norm_back(grad, normal, factor, vector(vec_ref, LN1_GAIN))
        out_ref[at, :] = total.astype(BF16).astype(F32)
        gain_sum = gain_sum + column_sum(grad * normal)
        bias_sum = bias_sum + column_sum(grad)
        start += count
    sums_ref[0:1, :] = gain_sum
    sums_ref[1:2, :] = bias_sum


def first_back(core, ours, theirs, x, middles, vectors, kepts, counts, after=()):
    rows, model = ours.shape
    return call(
        first_back_kernel,
        "first_back",
        [shape_of((rows, model), F32), shape_of((8, model), F32)]
        + [shape_of((count, model), F32) for count in counts],
        scalars=1,
        after=after,
    )(core, ours, theirs, x, *middles, vectors, *kepts)


def result_kernel(*refs, starts, placed):
    vec_ref, out_ref = refs[3 * len(starts)], refs[-1]
    at = 0
    if placed:
        done_ref = refs[3 * len(starts) + 1]
        at = done_ref.shape[0]
        out_ref[0:at, :] = done_ref[...]
    for part, (start, rows) in enumerate(starts):
        ours_ref, theirs_ref, kept_ref = refs[3 * part : 3 * part + 3]
        fed = ours_ref[0:rows, :] + theirs_ref[0:rows, :] + vector(vec_ref, FC2_BIAS)
        total = kept_ref[start : start + rows, :] + fed
        out_ref[at : at + rows, :] = total.astype(BF16).astype(F32)
        at += rows


def result_rows(parts, vectors, done=(), after=()):
    operands = [array for part in parts for array in part[:3]]
    rows = sum(part[4] for part in parts) + sum(array.shape[0] for array in done)
    return call(
        functools.partial(
            result_kernel, starts=[part[3:] for part in parts], placed=bool(done)
        ),
        "result_rows",
        [shape_of((rows, vectors.shape[1]), F32)],
        after=after,
    )(*operands, vectors, *done)[0]


def finish_kernel(core_ref, ours_ref, theirs_ref, out_ref, in_ref, low_ref, in_sem, out_sem):
    count = in_ref.shape[0] // 2
    rows = in_ref.shape[1]
    reads, writes = [], []
    for index in range(2 * count):
        ref = ours_ref if index < count else theirs_ref
        at = (index % count) * rows
        read = pltpu.make_async_copy(ref.at[pl.ds(at, rows), :], in_ref.at[index], in_sem.at[index])
        read.start()
        reads.append(read)
    for index, read in enumerate(reads):
        half = core_ref[0] if index < count else 1 - core_ref[0]
        place = pl.multiple_of(half * count * rows + (index % count) * rows, 128)
        read.wait()
        low_ref[index] = in_ref[index].astype(BF16)
        write = pltpu.make_async_copy(
            low_ref.at[index], out_ref.at[pl.ds(place, rows), :], out_sem.at[index]
        )
        write.start()
        writes.append(write)
    for write in writes:
        write.wait()


def finish(core, pairs, after=()):
    ((ours, theirs),) = pairs
    rows, model = ours.shape
    pieces = 4
    held = [pltpu.VMEM((2 * pieces, rows // pieces, model), dtype) for dtype in (F32, BF16)]

    def run(*refs):
        finish_kernel(*refs[:3], *refs[3 + len(after) :])

    return pl.pallas_call(
        run,
        in_specs=[pl.BlockSpec(memory_space=pltpu.SMEM)]
        + [pl.BlockSpec(memory_space=pltpu.HBM)] * 2
        + [pl.BlockSpec(memory_space=pl.ANY)] * len(after),
        out_specs=pl.BlockSpec(memory_space=pltpu.HBM),
        scratch_shapes=[*held, pltpu.SemaphoreType.DMA((8,)), pltpu.SemaphoreType.DMA((8,))],
        out_shape=shape_of((2 * rows, model), BF16),
        compiler_params=pltpu.CompilerParams(vmem_limit_bytes=60 * 1024 * 1024),
        name="finish",
    )(core, ours, theirs, *after)


def gather_sums_kernel(second0, second1, feed0, feed1, norm, fc1, heads, partial_ref, whole_ref):
    partial_ref[...] = jnp.zeros_like(partial_ref)
    whole_ref[...] = jnp.zeros_like(whole_ref)
    partial_ref[0:1, :] = second0[2:3, :] + second1[2:3, :]
    partial_ref[1:2, :] = feed0[0:1, :] + feed1[0:1, :]
    partial_ref[2:4, :] = second0[0:2, :] + second1[0:2, :]
    partial_ref[4:6, :] = norm[0:2, :]
    whole_ref[6:7, :] = fc1[0:1, :]
    whole_ref[7:8, :] = heads[0:1, :]


def gather_sums(arrays, after=()):
    shape = shape_of(arrays[0].shape, F32)
    return call(gather_sums_kernel, "gather_sums", [shape, shape], after=after)(*arrays)


def feed_sum_kernel(ours_ref, theirs_ref, fc2_ref, fc1_ref):
    units = fc2_ref.shape[1]
    total = ours_ref[...] + theirs_ref[...]
    fc2_ref[...] = total[:, :units]
    fc1_ref[...] = total[:, units:]


def feed_sum(ours, theirs, after=()):
    half = shape_of((ours.shape[0], ours.shape[1] // 2), F32)
    return call(
        feed_sum_kernel, "feed_sum", [half, half], after=after
    )(ours, theirs)


def heads_sum_kernel(ours_ref, theirs_ref, heads_ref, out_ref):
    width = heads_ref.shape[2]
    total = ours_ref[...] + theirs_ref[...]
    for part in range(3):
        heads_ref[part] = total[:, part * width : (part + 1) * width]
    out_ref[...] = jnp.transpose(total[:, 3 * width :])


def heads_sum(ours, theirs, after=()):
    rows, width = ours.shape[0], ours.shape[1] // 4
    shapes = [shape_of((3, rows, width), F32), shape_of((width, rows), F32)]
    return call(
        heads_sum_kernel, "heads_sum", shapes, after=after
    )(ours, theirs)


def body(
    tokens,
    ln1_gain,
    ln1_bias,
    qkv_weight,
    qkv_bias,
    out_weight,
    out_bias,
    ln2_gain,
    ln2_bias,
    fc1_weight,
    fc1_bias,
    fc2_weight,
    fc2_bias,
    cotangent,
    *,
    batch_count,
    tensor_count,
):
    rows, model = tokens.shape[1:]
    width = qkv_weight.shape[2]
    units = fc1_weight.shape[1]
    bits = batch_count.bit_length() - 1
    batch_at = lax.axis_index("batch")
    core = (lax.axis_index("tensor") % 2).astype(jnp.int32).reshape(1)

    def core_swap(v):
        return lax.ppermute(v, "tensor", [(i, i ^ 1) for i in range(tensor_count)])

    def chip_swap(v):
        return lax.ppermute(v, "tensor", [(i, i ^ 2) for i in range(tensor_count)])

    def batch_swap(v, bit):
        return lax.ppermute(v, "batch", [(i, i ^ (1 << bit)) for i in range(batch_count)])

    last = []

    def then(made, *others):
        last[:] = [made[0], *others]
        return made

    orders = ([0, *range(1, bits)], [1, 0, *range(2, bits)])

    def mine_of(some):
        return jnp.stack([(batch_at >> bit) & 1 for bit in some]).astype(jnp.int32)

    class Scatter:
        def __init__(self, cut, order, left=range(bits - 1, -1, -1)):
            self.order = list(order)
            self.left = list(left)
            self.cross(cut)

        def cross(self, cut):
            send, self.keep = cut
            bit = self.order.pop(0)
            self.left.remove(bit)
            self.theirs = batch_swap(send, bit)

        def step(self, *others):
            bit = self.order[0]
            pairs = [(v.keep, v.theirs) for v in (self, *others)]
            self.cross(
                then(hop(mine_of([bit]), pairs, 1 << len(self.left), self.left.index(bit), after=last))
            )

        def end(self, summed):
            while self.order:
                self.step()
            return then(summed(self.keep, self.theirs, after=last))

    def weight_scatters(kernel, operands, widths, orders, held, sums=True):
        width = sum(widths)
        spans = [slice(sum(widths[:i]), sum(widths[: i + 1])) for i in range(len(widths))]
        firsts = [order[0] for order in orders]
        made = then(
            weight_grad(
                kernel, core, mine_of(firsts), operands, model, width, spans, batch_count,
                [bits - 1 - bit for bit in firsts], sums=sums, far=(), held=held, after=last,
            )
        )
        return [Scatter(made[2 * i : 2 * i + 2], order) for i, order in enumerate(orders)], made[-1]

    x = tokens.reshape(rows, model)
    dy = cotangent.reshape(rows, model)
    heads_weight = jnp.transpose(qkv_weight, (1, 2, 0))
    listed = (
        ln1_gain, ln1_bias, jnp.transpose(qkv_bias, (1, 0, 2)), out_bias, ln2_gain, ln2_bias, fc1_bias,
        fc2_bias,
    )
    vectors, heads_wide, out_weight_wide = pack(listed, heads_weight, out_weight)

    heads_other = core_swap(heads_wide)
    out_weight_far = chip_swap(out_weight_wide)
    others = then(
        widen([fc1_weight, fc2_weight, out_weight], after=[heads_wide])
    )
    others = [core_swap(v) for v in others]
    other_bias = heads_other[3 * width + FC1_BIAS :]

    left, queries, keys, values = then(
        project(core, x, vectors, heads_weight, heads_other, after=last)
    )
    near, totals = then(attend(queries, keys, values, after=last))
    far = chip_swap(near)
    fc1_other, fc2_other, out_weight_other, heads_other_low = then(
        convert([*others, heads_other], BF16, after=last)
    )
    dy_turned = then(turn(dy, after=last))[0]
    out_weight_both = core_swap(out_weight_far)
    out_weights = (out_weight, out_weight_other, out_weight_far, out_weight_both)

    half = rows // 2
    sizes = (3 * half // 4, half // 4)
    starts = (0, sizes[0])
    fed = []
    for start, size in zip(starts, sizes):
        fed.append(
            then(
                feed(
                    core, start, size, x, dy, near, far, out_weights, vectors, other_bias, fc1_weight,
                    fc2_weight, (fc1_other, fc2_other), after=last,
                )
            )
        )
    kepts, owns = [f[0] for f in fed], [f[1] for f in fed]
    grads, feed_sums = [f[-2] for f in fed], [f[-1] for f in fed]
    grads_far = [chip_swap(v) for v in grads]
    swaps = [core_swap(v) for f in fed for v in f[2:-2]]
    (fc2,), _ = weight_scatters(
        fc2_grad_kernel, [dy_turned, *owns, *swaps], [units], orders[1:],
        [
            pltpu.VMEM((model, rows), BF16),
            *(pltpu.VMEM((size, units), dtype) for dtype in (BF16, F32) for size in sizes),
            pltpu.SemaphoreType.DMA((5,)),
        ],
        sums=False
    )
    (fc1,), fc1_sums = weight_scatters(fc1_grad_kernel, [*owns, *swaps], [units], orders[:1],
        [
            *(pltpu.VMEM((2 * size, units), dtype) for dtype in (BF16, F32) for size in sizes),
            pltpu.SemaphoreType.DMA((5,)),
        ],
    )

    weights = (out_weight, out_weight_other)
    heads = (queries, keys, values, totals)
    middle0, low0, second_sums0, res0 = then(
        second_back(core, 0, grads[0], grads_far[0], kepts[0], dy, vectors, after=last)
    )
    res0_far = chip_swap(res0)
    dq0, dk0, dv0 = then(attend_back(core, 0, low0, weights, *heads, after=last))
    middle1, low1, second_sums1, out_w = then(
        second_back(
            core, starts[1], grads[1], grads_far[1], kepts[1], dy, vectors, (low0, near),
            after=last,
        )
    )
    out_w_other = core_swap(out_w)
    dq1, dk_send, dv_send, dk, dv = then(
        attend_back(core, starts[1], low1, weights, *heads, (dk0, dv0), after=last)
    )
    theirs = core_swap(dk_send), core_swap(dv_send)
    fc2.step()
    fc1.step()
    grad_rows, heads_own, send = then(
        first_grad(
            (dq0, dq1), (dk, dv), theirs, heads_weight, heads_other_low, after=[*last, res0_far]
        )
    )
    grad_rows_far = chip_swap(grad_rows)
    heads_theirs = core_swap(send)
    heads, heads_sums = weight_scatters(
        heads_grad_kernel,
        [left, heads_own, heads_theirs, low0, low1, near, out_w_other],
        [8 * width // 3, 4 * width // 3],
        orders,
        (),
    )
    result0 = then([result_rows([(res0, res0_far, kepts[0], 0, BLOCK)], vectors, after=last)])[0]
    fc2.step(fc1)
    heads[1].step()
    heads[0].step()
    counts = (sizes[0] - BLOCK, sizes[1])
    grad_rows, norm_sums, *res1 = then(
        first_back(
            core, grad_rows, grad_rows_far, x, (middle0, middle1), vectors, kepts, counts, after=last
        )
    )
    grad_rows_other = core_swap(grad_rows)
    res1_far = [chip_swap(v) for v in res1]
    grad_fc2, grad_fc1 = fc2.end(feed_sum)
    heads[0].step(heads[1])
    partial, whole = then(
        gather_sums(
            (second_sums0, second_sums1, *feed_sums, norm_sums, fc1_sums, heads_sums), after=last
        )
    )
    small = partial + core_swap(partial) + whole
    for bit in range(bits):
        small = small + batch_swap(small, bit)
    grad_heads, grad_out = heads[0].end(heads_sum)
    last.append(small)
    parts = [
        (v, far, kept, start, count)
        for v, far, kept, start, count in zip(res1, res1_far, kepts, (BLOCK, 0), counts)
    ]
    result = then([result_rows(parts, vectors, [result0], after=last)])[0]
    result_other = core_swap(result)
    grad_tokens = then([finish(core, [(grad_rows, grad_rows_other)], after=last)])[0]
    result = then([finish(core, [(result, result_other)], after=last)])[0]
    share = HD // batch_count
    piece = model // batch_count
    shared = lax.dynamic_slice_in_dim(small[:6], batch_at * piece, piece, 1)
    own = lax.dynamic_slice_in_dim(
        small[6:].reshape(2, model // HD, HD), batch_at * share, share, 2
    )
    return (
        result.reshape(tokens.shape),
        grad_tokens.reshape(tokens.shape),
        jnp.transpose(grad_heads, (1, 0, 2)),
        own[1, : 3 * width // HD].reshape(3, width // HD, share)[::2],
        grad_out,
        shared[0],
        shared[4],
        shared[5],
        shared[2],
        shared[3],
        grad_fc1,
        own[0, : units // HD],
        grad_fc2.T,
        shared[1],
    )


def solution(mesh):
    placed = (
        P("batch", None, None),
        P(),
        P(),
        P(None, None, "tensor"),
        P(None, "tensor", None),
        P("tensor", None),
        P(),
        P(),
        P(),
        P(None, "tensor"),
        P("tensor", None),
        P("tensor", None),
        P(),
        P("batch", None, None),
    )
    return jax.shard_map(
        functools.partial(
            body, batch_count=mesh.shape["batch"], tensor_count=mesh.shape["tensor"]
        ),
        mesh=mesh,
        in_specs=placed,
        out_specs=(
            P("batch", None, None),
            P("batch", None, None),
            P("batch", None, "tensor"),
            P(None, "tensor", "batch"),
            P("tensor", "batch"),
            P("batch"),
            P("batch"),
            P("batch"),
            P("batch"),
            P("batch"),
            P("batch", "tensor"),
            P("tensor", "batch"),
            P("tensor", "batch"),
            P("batch"),
        ),
        check_vma=False,
    )
```

```python
import functools
import math

import jax
import jax.numpy as jnp
from jax import lax
from jax.experimental import pallas as pl
from jax.experimental.pallas import tpu as pltpu
from jax.sharding import PartitionSpec as P

HD = 64
LN1_GAIN, LN1_BIAS, HEADS_BIAS, OUT_BIAS, LN2_GAIN, LN2_BIAS, FC1_BIAS, FC2_BIAS = range(8)
BLOCK = 256
EPSILON = 1e-06
F32 = jnp.float32
BF16 = jnp.bfloat16


def nn(a, b):
    return lax.dot_general(a, b, (((1,), (0,)), ((), ())), preferred_element_type=F32)


def nt(a, b):
    return lax.dot_general(a, b, (((1,), (1,)), ((), ())), preferred_element_type=F32)


def tn(a, b):
    return lax.dot_general(a, b, (((0,), (0,)), ((), ())), preferred_element_type=F32)


def call(kernel, name, out_shape, scalars=0, scratch=(), after=(), far_in=(), far_out=(), vmem=20, raw_in=(), raw_out=()):

    def run(*args):
        given = len(args)
        ins = [scalars + index for index in far_in]
        outs = list(far_out)
        made = len(out_shape)

        def inner(*refs):
            first = given + len(after)
            operands, results = list(refs[:given]), list(refs[first : first + made])
            held = list(refs[first + made : first + made + len(scratch)])
            spare = list(refs[first + made + len(scratch) :])
            sems = spare.pop() if spare else None
            copies = []
            for count, index in enumerate(ins):
                copies.append(pltpu.make_async_copy(operands[index], spare[count], sems.at[count]))
                operands[index] = spare[count]
            for copy in copies:
                copy.start()
            far = [results[index] for index in outs]
            for count, index in enumerate(outs):
                results[index] = spare[len(ins) + count]
            for copy in copies:
                copy.wait()
            kernel(*operands, *results, *held)
            copies = []
            for count, ref in enumerate(far, len(ins)):
                copies.append(pltpu.make_async_copy(spare[count], ref, sems.at[count]))
            for copy in copies:
                copy.start()
            for copy in copies:
                copy.wait()

        def space(index, chosen):
            return pl.BlockSpec(memory_space=pltpu.HBM if index in chosen else pltpu.VMEM)

        moved = [args[index] for index in ins] + [out_shape[index] for index in outs]
        held = list(scratch) + [pltpu.VMEM(v.shape, v.dtype) for v in moved]
        if moved:
            held.append(pltpu.SemaphoreType.DMA((len(moved),)))
        return pl.pallas_call(
            inner,
            in_specs=[pl.BlockSpec(memory_space=pltpu.SMEM)] * scalars
            + [space(index, [*ins, *(scalars + at for at in raw_in)]) for index in range(scalars, given)]
            + [pl.BlockSpec(memory_space=pl.ANY)] * len(after),
            out_specs=[space(index, [*outs, *raw_out]) for index in range(made)],
            scratch_shapes=held,
            out_shape=out_shape,
            compiler_params=pltpu.CompilerParams(vmem_limit_bytes=vmem * 1024 * 1024),
            name=name,
        )(*args, *after)

    return run


def shape_of(shape, dtype):
    return jax.ShapeDtypeStruct(shape, dtype)


def vector(ref, row, width=None):
    return ref[row : row + 1, : ref.shape[1] if width is None else width]


def normalize(values):
    average = jnp.mean(values, axis=-1, keepdims=True)
    centered = values - average
    spread = jnp.mean(centered * centered, axis=-1, keepdims=True)
    factor = lax.rsqrt(spread + EPSILON)
    return centered * factor, factor


def half_of(core_ref, ref, offset=0, rows=None):
    size = ref.shape[0] // 2
    rows = size if rows is None else rows
    return pl.ds(pl.multiple_of(core_ref[0] * size + offset, 128), rows)


def pack_kernel(
    g1_ref, b1_ref, bias_ref, ob_ref, g2_ref, b2_ref, fc1_bias_ref, fb_ref, w_ref, out_w_ref,
    vec_ref, wide_ref, out_wide_ref,
):
    width = w_ref.shape[1]
    vec_ref[...] = jnp.zeros_like(vec_ref)
    for row, ref in (
        (LN1_GAIN, g1_ref),
        (LN1_BIAS, b1_ref),
        (OUT_BIAS, ob_ref),
        (LN2_GAIN, g2_ref),
        (LN2_BIAS, b2_ref),
        (FC2_BIAS, fb_ref),
    ):
        vec_ref[row : row + 1, :] = ref[...].reshape(1, -1)
    for head in range(bias_ref.shape[0]):
        for part, start in ((0, 0), (1, 2 * width)):
            at = start + head * HD
            vec_ref[HEADS_BIAS : HEADS_BIAS + 1, at : at + HD] = bias_ref[head, part : part + 1, :]
    for head in range(fc1_bias_ref.shape[0]):
        at = slice(head * HD, (head + 1) * HD)
        vec_ref[FC1_BIAS : FC1_BIAS + 1, at] = fc1_bias_ref[head : head + 1, :]
    for part in range(3):
        wide_ref[part * width : (part + 1) * width, :] = w_ref[part].astype(F32)
    wide_ref[3 * width :, :] = vec_ref[...]
    out_wide_ref[0:width, :] = out_w_ref[...].astype(F32)


def pack(listed, heads_weight, out_weight):
    width, model = out_weight.shape
    return call(
        pack_kernel,
        "pack",
        [
            shape_of((8, model), F32),
            shape_of((3 * width + 8, model), F32),
            shape_of((width + 8, model), F32),
        ],
        vmem=60,
    )(*listed, heads_weight, out_weight)


def project_kernel(
    core_ref, x_ref, vec_ref, w_ref, far_other_ref, all_ref, q_ref, k_ref, v_ref, other_ref, sem
):
    width = w_ref.shape[1]
    copy = pltpu.make_async_copy(far_other_ref, other_ref, sem)
    copy.start()
    for start in range(0, x_ref.shape[0], BLOCK):
        at = slice(start, start + BLOCK)
        normal, _ = normalize(x_ref[at, :].astype(F32))
        all_ref[at, :] = (normal * vector(vec_ref, LN1_GAIN) + vector(vec_ref, LN1_BIAS)).astype(BF16)
    left = all_ref[...]
    mine = all_ref[half_of(core_ref, all_ref), :]
    bias_row = 3 * width + HEADS_BIAS
    for group in range(2):
        if group == 1:
            copy.wait()
        bias = vector(vec_ref, HEADS_BIAS) if group == 0 else other_ref[bias_row : bias_row + 1, :]
        for part, (ref, rows) in enumerate(((q_ref, mine), (k_ref, left), (v_ref, left))):
            span = slice(part * width, (part + 1) * width)
            weight = w_ref[part] if group == 0 else other_ref[span, :].astype(BF16)
            ref[:, group * width : (group + 1) * width] = (
                nt(rows, weight) + bias[:, span]
            ).astype(BF16)


def project(core, x, vectors, weight, other, after=()):
    rows, model = x.shape
    width = weight.shape[1]
    both = 2 * width
    return call(
        project_kernel,
        "project",
        [
            shape_of((rows, model), BF16),
            shape_of((rows // 2, both), BF16),
            shape_of((rows, both), BF16),
            shape_of((rows, both), BF16),
        ],
        scalars=1,
        scratch=[pltpu.VMEM(other.shape, F32), pltpu.SemaphoreType.DMA],
        raw_in=(3,),
        after=after,
    )(core, x, vectors, weight, other)


def attend_kernel(q_ref, k_ref, v_ref, out_ref, total_ref):
    heads = q_ref.shape[1] // HD
    scale = jnp.asarray(1.0 / math.sqrt(HD), BF16)
    parts = []
    logs = []
    for head in range(heads):
        at = slice(head * HD, (head + 1) * HD)
        scores = nt(q_ref[:, at] * scale, k_ref[:, at])
        peak = jnp.max(scores, axis=1, keepdims=True)
        powers = jnp.exp(scores - peak)
        totals = jnp.sum(powers, axis=1, keepdims=True)
        parts.append(nn(powers.astype(BF16), v_ref[:, at]) / totals)
        logs.append(peak + jnp.log(totals))
    mixed = jnp.concatenate(parts, axis=1).astype(BF16).astype(F32)
    out_ref[...] = mixed
    logs.append(jnp.zeros((q_ref.shape[0], total_ref.shape[1] - heads), F32))
    total_ref[...] = jnp.concatenate(logs, axis=1)


def attend(queries, keys, values, after=()):
    rows, width = queries.shape
    return call(
        attend_kernel,
        "attend",
        [shape_of((rows, width), F32), shape_of((rows, 8), F32)],
        after=after,
    )(queries, keys, values)


def convert_kernel(*refs):
    half = len(refs) // 2
    for ref, out_ref in zip(refs[:half], refs[half:]):
        out_ref[...] = ref[...].astype(out_ref.dtype)


def widen_kernel(*refs, parts, given):
    ins, outs, (read_ref, wide_ref, in_sem, out_sem) = refs[:given], refs[given : 2 * given], refs[2 * given :]
    rows = read_ref.shape[1]
    reads, writes = [], []
    for index, (array, at) in enumerate(parts):
        read = pltpu.make_async_copy(
            ins[array].at[pl.ds(at, rows), :], read_ref.at[index], in_sem.at[index]
        )
        read.start()
        reads.append(read)
    for index, (array, at) in enumerate(parts):
        reads[index].wait()
        wide_ref[index] = read_ref[index].astype(F32)
        write = pltpu.make_async_copy(
            wide_ref.at[index], outs[array].at[pl.ds(at, rows), :], out_sem.at[index]
        )
        write.start()
        writes.append(write)
    for write in writes:
        write.wait()


def widen(arrays, after=()):
    model = arrays[0].shape[1]
    rows = min(array.shape[0] for array in arrays)
    parts = [(index, at) for index, v in enumerate(arrays) for at in range(0, v.shape[0], rows)]
    count = len(parts)
    indices = tuple(range(len(arrays)))
    return call(
        functools.partial(widen_kernel, parts=parts, given=len(arrays)),
        "widen",
        [shape_of(array.shape, F32) for array in arrays],
        scratch=[
            pltpu.VMEM((count, rows, model), BF16),
            pltpu.VMEM((count, rows, model), F32),
            pltpu.SemaphoreType.DMA((count,)),
            pltpu.SemaphoreType.DMA((count,)),
        ],
        after=after,
        raw_in=indices,
        raw_out=indices,
        vmem=60,
    )(*arrays)


def convert(arrays, dtype, vmem=20, after=()):
    shapes = [shape_of(array.shape, dtype) for array in arrays]
    return call(convert_kernel, "convert", shapes, after=after, vmem=vmem)(*arrays)


ERF = (0.254829592, -0.284496736, 1.421413741, -1.453152027, 1.061405429)


def gelu_pair(values):
    size = jnp.abs(values) * (1.0 / math.sqrt(2.0))
    step = 1.0 / (1.0 + 0.3275911 * size)
    bell = jnp.exp(-(size * size))
    series = ERF[4]
    for factor in (ERF[3], ERF[2], ERF[1], ERF[0]):
        series = series * step + factor
    tail = (0.5 * step) * series * bell
    below = jnp.where(values >= 0, 1.0 - tail, tail)
    return values * below, below + values * (bell * (1.0 / math.sqrt(2.0 * math.pi)))


def feed_kernel(
    core_ref,
    x_ref,
    dy_ref,
    near_ref,
    far_ref,
    w0_ref,
    w1_ref,
    w2_ref,
    w3_ref,
    vec_ref,
    other_vec_ref,
    fc1_ref,
    fc2_ref,
    other_fc1_ref,
    other_fc2_ref,
    *refs,
    start,
):
    kept_ref, own_ref, *swap_refs, grad_ref, sums_ref = refs
    count = grad_ref.shape[0]
    rows = slice(start, start + count)
    place = half_of(core_ref, x_ref, start, count)
    width = w0_ref.shape[0]
    units = fc1_ref.shape[1]

    def share(ref, part, w_ref):
        return nn(ref[rows, part * width : (part + 1) * width].astype(BF16), w_ref[0:width, :].astype(BF16))

    branch = (share(near_ref, 0, w0_ref) + share(near_ref, 1, w1_ref)) + (
        share(far_ref, 0, w2_ref) + share(far_ref, 1, w3_ref)
    )
    middle = x_ref[place, :].astype(F32) + (branch + vector(vec_ref, OUT_BIAS))
    kept_ref[0:count, :] = middle
    normal, _ = normalize(middle)
    left = (normal * vector(vec_ref, LN2_GAIN) + vector(vec_ref, LN2_BIAS)).astype(BF16)
    own_ref[0:count, :] = left
    dy = dy_ref[place, :]
    grad = res = None
    groups = ((vec_ref, FC1_BIAS, fc1_ref, fc2_ref), (other_vec_ref, 0, other_fc1_ref, other_fc2_ref))
    for group, (bias_ref, bias_row, in_ref, out_ref) in enumerate(groups):
        hidden, slope = gelu_pair(nn(left, in_ref[...]) + vector(bias_ref, bias_row, units))
        hidden = hidden.astype(BF16)
        pre = (nt(dy, out_ref[...]) * slope).astype(BF16)
        if group == 0:
            own_ref[count : 2 * count, :] = pre
            own_ref[2 * count :, :] = hidden
        else:
            at = 0
            wide = jnp.concatenate([left, pre, hidden], axis=0).astype(F32)
            for ref in swap_refs:
                size = 3 * count // len(swap_refs)
                ref[0:size, :] = wide[at : at + size]
                at += size
        back = nt(pre, in_ref[...])
        fed = nn(hidden, out_ref[...])
        grad = back if grad is None else grad + back
        res = fed if res is None else res + fed
    grad_ref[...] = grad
    kept_ref[count:, :] = res
    sums_ref[0:1, :] = jnp.sum(dy.astype(F32), axis=0, keepdims=True)


def feed(core, start, count, x, dy, near, far, out_weights, vectors, other_bias, fc1, fc2, other, after=()):
    model = x.shape[1]
    swaps = [3 * count + 8] if start == 0 else [3 * count // 2] * 2
    return call(
        functools.partial(feed_kernel, start=start),
        "feed",
        [shape_of((2 * count, model), F32), shape_of((3 * count, model), BF16)]
        + [shape_of((size, model), F32) for size in swaps]
        + [shape_of((count, model), F32), shape_of((8, model), F32)],
        scalars=1,
        after=after,
    )(core, x, dy, near, far, *out_weights, vectors, other_bias, fc1, fc2, *other)


def cut_pieces(ref, send_ref, keep_ref, mine, count, axis_bits, axis):
    rows = ref.shape[0] // count
    stride = 1 << (axis_bits - 1 - axis)
    for value in range(2):

        @pl.when(mine == value)
        def _():
            for index in range(count):
                place = (index // (2 * stride)) * stride + index % stride
                out = keep_ref if (index // stride) % 2 == value else send_ref
                out[place * rows : (place + 1) * rows, :] = ref[index * rows : (index + 1) * rows, :]


def cut_spans(total_ref, refs, mine_ref, spans, count, axes):
    axis_bits = count.bit_length() - 1
    for index, (span, axis) in enumerate(zip(spans, axes)):
        cut_pieces(
            total_ref.at[:, span], refs[2 * index], refs[2 * index + 1], mine_ref[index], count,
            axis_bits, axis,
        )


def cut_shapes(rows, spans):
    shapes = []
    for span in spans:
        shapes += [shape_of((rows // 2, span.stop - span.start), F32)] * 2
    return shapes


def column_sum(values):
    return jnp.sum(values.astype(F32), axis=0, keepdims=True)


def turn_kernel(ref, out_ref):
    out_ref[...] = jnp.transpose(ref[...])


def turn(array, after=()):
    return call(turn_kernel, "turn", [shape_of(array.shape[::-1], array.dtype)], after=after)(array)


def fetch(pairs, sem):
    copies = [
        pltpu.make_async_copy(source, target, sem.at[index])
        for index, (source, target) in enumerate(pairs)
    ]
    for copy in copies:
        copy.start()
    return copies


def fc2_grad_kernel(core_ref, mine_ref, dy_ref, own0, own1, swap0, swap1, swap2, *refs, spans, count, axes):
    cuts, (total_ref, dy_held, h0, h1, t0, t1, sem) = refs[:-7], refs[-7:]
    n0, n1 = h0.shape[0], h1.shape[0]
    copies = fetch(
        [
            (dy_ref, dy_held),
            (own0.at[pl.ds(2 * n0, n0), :], h0),
            (own1.at[pl.ds(2 * n1, n1), :], h1),
            (swap0.at[pl.ds(2 * n0, n0), :], t0),
            (swap2.at[pl.ds(n1 // 2, n1), :], t1),
        ],
        sem,
    )
    copies[0].wait()
    total = None
    for index, (held, start, half) in enumerate(
        ((h0, 0, core_ref[0]), (h1, n0, core_ref[0]), (t0, 0, 1 - core_ref[0]), (t1, n0, 1 - core_ref[0]))
    ):
        copies[index + 1].wait()
        place = pl.multiple_of(half * (dy_held.shape[1] // 2) + start, 128)
        term = nn(dy_held[:, pl.ds(place, held.shape[0])], held[...].astype(BF16))
        total = term if total is None else total + term
    total_ref[...] = total
    cut_spans(total_ref, cuts, mine_ref, spans, count, axes)


def fc1_grad_kernel(core_ref, mine_ref, own0, own1, swap0, swap1, swap2, *refs, spans, count, axes):
    cuts, (sums_ref, total_ref, h0, h1, t0, t1, sem) = refs[:-7], refs[-7:]
    n0, n1 = h0.shape[0] // 2, h1.shape[0] // 2
    copies = fetch(
        [
            (own0.at[pl.ds(0, 2 * n0), :], h0),
            (own1.at[pl.ds(0, 2 * n1), :], h1),
            (swap0.at[pl.ds(0, 2 * n0), :], t0),
            (swap1, t1.at[pl.ds(0, 3 * n1 // 2), :]),
            (swap2.at[pl.ds(0, n1 // 2), :], t1.at[pl.ds(3 * n1 // 2, n1 // 2), :]),
        ],
        sem,
    )
    total = None
    sums = 0.0
    for index, held in enumerate((h0, h1, t0, t1)):
        copies[index].wait()
        if index == 3:
            copies[4].wait()
        size = held.shape[0] // 2
        left, pre = held[0:size, :].astype(BF16), held[size:, :].astype(BF16)
        term = tn(left, pre)
        total = term if total is None else total + term
        sums = sums + column_sum(pre)
    total_ref[...] = total
    sums_ref[0:1, :] = sums
    cut_spans(total_ref, cuts, mine_ref, spans, count, axes)


def chunk_products(lows, near_ref, columns):
    at = 0
    total = None
    for low in lows:
        term = tn(low[...], near_ref[at : at + low.shape[0], columns].astype(BF16))
        total = term if total is None else total + term
        at += low.shape[0]
    return total


def heads_grad_kernel(
    core_ref, mine_ref, left_ref, ours_ref, theirs_ref, low0_ref, low1_ref, near_ref, out_w_ref,
    *refs, spans, count, axes,
):
    sums_ref, total_ref = refs[-2:]
    rows = left_ref.shape[0] // 2
    width = near_ref.shape[1] // 2
    ours = ours_ref[...]
    theirs = jnp.concatenate(
        [
            theirs_ref[0:rows, :],
            jnp.concatenate([theirs_ref[rows:, :width], theirs_ref[rows:, width:]], axis=0),
        ],
        axis=1,
    ).astype(BF16)
    left = left_ref[half_of(core_ref, left_ref), :]
    left_other = left_ref[pl.ds(pl.multiple_of((1 - core_ref[0]) * rows, BLOCK), rows), :]
    total_ref[:, : 3 * width] = tn(left, ours) + tn(left_other, theirs)
    out_w = jnp.concatenate([out_w_ref[:, :width], out_w_ref[:, width:]], axis=0)
    total_ref[:, 3 * width :] = out_w + chunk_products((low0_ref, low1_ref), near_ref, slice(0, width))
    sums_ref[...] = jnp.zeros_like(sums_ref)
    sums_ref[0:1, : 3 * width] = column_sum(ours) + column_sum(theirs)
    cut_spans(total_ref, refs[:-2], mine_ref, spans, count, axes)


def weight_grad(
    kernel, core, mine, operands, model, width, spans, count, axes, sums, far, held=(), after=()
):
    raw = tuple(range(len(operands))) if held else ()
    return call(
        functools.partial(kernel, spans=spans, count=count, axes=axes),
        "weight_grad",
        cut_shapes(model, spans) + ([shape_of((8, model), F32)] if sums else []),
        scalars=2,
        scratch=[pltpu.VMEM((model, width), F32), *held],
        after=after,
        raw_in=raw,
        vmem=60 if held else 20,
    )(core, mine, *operands)


def hop_kernel(mine_ref, *refs, pairs, spans, count, axes):
    total_ref = refs[-1]
    at = 0
    for pair in range(pairs):
        ours, theirs = refs[2 * pair], refs[2 * pair + 1]
        total_ref[:, at : at + ours.shape[1]] = ours[...] + theirs[...]
        at += ours.shape[1]
    cut_spans(total_ref, refs[2 * pairs : -1], mine_ref, spans, count, axes)


def hop(mine, pairs, count, axes, after=()):
    operands = [array for pair in pairs for array in pair]
    rows = operands[0].shape[0]
    width = sum(pair[0].shape[1] for pair in pairs)
    each = width // len(axes)
    spans = [slice(index * each, (index + 1) * each) for index in range(len(axes))]
    return call(
        functools.partial(hop_kernel, pairs=len(pairs), spans=spans, count=count, axes=axes),
        "hop",
        cut_shapes(rows, spans),
        scalars=1,
        scratch=[pltpu.VMEM((rows, width), F32)],
        after=after,
    )(mine, *operands)


def norm_back(grad, normal, factor, gain):
    scaled = grad * gain
    first = jnp.mean(scaled, axis=-1, keepdims=True)
    second = jnp.mean(scaled * normal, axis=-1, keepdims=True)
    return factor * (scaled - first - normal * second)


def second_back_kernel(core_ref, ours_ref, theirs_ref, kept_ref, dy_ref, vec_ref, *refs, start):
    grad_ref, low_ref, sums_ref, last_ref = refs[-4:]
    count = ours_ref.shape[0]
    grad = ours_ref[...] + theirs_ref[...]
    normal, factor = normalize(kept_ref[0:count, :])
    dy = dy_ref[half_of(core_ref, dy_ref, start, count), :].astype(F32)
    total = dy + norm_back(grad, normal, factor, vector(vec_ref, LN2_GAIN))
    grad_ref[...] = total
    low = total.astype(BF16)
    low_ref[...] = low
    for index, term in enumerate((grad * normal, grad, low.astype(F32))):
        sums_ref[index : index + 1, :] = column_sum(term)
    if start == 0:
        rows = last_ref.shape[0] - 8
        last_ref[0:rows, :] = kept_ref[count : count + rows, :]
    else:
        low0_ref, near_ref = refs[:2]
        width = near_ref.shape[1] // 2
        product = chunk_products((low0_ref, low_ref), near_ref, slice(width, 2 * width))
        last_ref[:, :width] = product[: product.shape[0] // 2]
        last_ref[:, width:] = product[product.shape[0] // 2 :]


def second_back(core, start, ours, theirs, kept, dy, vectors, others=(), after=()):
    rows, model = ours.shape
    out_shape = [shape_of((rows, model), F32), shape_of((rows, model), BF16), shape_of((8, model), F32)]
    if others:
        out_shape.append(shape_of((model // 2, others[1].shape[1]), F32))
    else:
        out_shape.append(shape_of((BLOCK + 8, model), F32))
    return call(
        functools.partial(second_back_kernel, start=start),
        "second_back",
        out_shape,
        scalars=1,
        after=after,
    )(core, ours, theirs, kept, dy, vectors, *others)


def attend_back_kernel(core_ref, low_ref, w0_ref, w1_ref, q_ref, k_ref, v_ref, total_ref, *refs, start):
    if start:
        dk0_ref, dv0_ref, dq_ref, dk_send_ref, dv_send_ref, dk_ref, dv_ref, scratch_ref = refs
    else:
        dq_ref, dk_ref, dv_ref = refs
    rows_here = slice(start, start + low_ref.shape[0])
    heads = q_ref.shape[1] // HD
    scale = jnp.asarray(1.0 / math.sqrt(HD), BF16)
    low = low_ref[...]
    outers = [nt(low, ref[...]).astype(BF16) for ref in (w0_ref, w1_ref)]
    outer = jnp.concatenate(outers, axis=1)
    dqs = []
    dks = []
    dvs = []
    for head in range(heads):
        at = slice(head * HD, (head + 1) * HD)
        queries = q_ref[rows_here, at] * scale
        keys = k_ref[:, at]
        outer_here = outer[:, at]
        probs = jnp.exp(nt(queries, keys) - total_ref[rows_here, head : head + 1])
        grad_probs = nt(outer_here, v_ref[:, at])
        inner = jnp.sum(probs * grad_probs, axis=1, keepdims=True)
        grad_scores = (probs * (grad_probs - inner)).astype(BF16)
        dvs.append(tn(outer_here, probs.astype(BF16)))
        dks.append(tn(queries, grad_scores))
        dqs.append(nn(grad_scores, keys))
    dq_ref[...] = (jnp.concatenate(dqs, axis=1) * (1.0 / math.sqrt(HD))).astype(BF16)
    if not start:
        dk_ref[...] = jnp.concatenate(dks, axis=0)
        dv_ref[...] = jnp.concatenate(dvs, axis=0)
        return
    for parts, before_ref, send_ref, keep_ref in (
        (dks, dk0_ref, dk_send_ref, dk_ref),
        (dvs, dv0_ref, dv_send_ref, dv_ref),
    ):
        scratch_ref[...] = jnp.transpose(before_ref[...] + jnp.concatenate(parts, axis=0))
        rows = scratch_ref.shape[0] // 2
        for ref, half in ((send_ref, 1 - core_ref[0]), (keep_ref, core_ref[0])):
            ref[...] = scratch_ref[pl.ds(pl.multiple_of(half * rows, BLOCK), rows), :]


def attend_back(core, start, low, out_weights, queries, keys, values, totals, before=(), after=()):
    rows, width = keys.shape
    sums = [shape_of((rows // 2, width), F32)] * 4 if before else [shape_of((width, rows), F32)] * 2
    return call(
        functools.partial(attend_back_kernel, start=start),
        "attend_back",
        [shape_of((low.shape[0], width), BF16)] + sums,
        scalars=1,
        scratch=[pltpu.VMEM((rows, width), F32)] if before else [],
        after=after,
    )(core, low, *out_weights, queries, keys, values, totals, *before)


def first_grad_kernel(
    dq0_ref, dq1_ref, dk_ref, dv_ref, dk_other_ref, dv_other_ref, w_ref, other_ref, out_ref, own_ref, send_ref
):
    width = w_ref.shape[1]
    total = None
    for part in range(3):
        for group in range(2):
            if part == 0:
                span = slice(group * width, (group + 1) * width)
                values = jnp.concatenate([dq0_ref[:, span], dq1_ref[:, span]], axis=0)
            else:
                ours_ref, theirs_ref = ((dk_ref, dk_other_ref), (dv_ref, dv_other_ref))[part - 1]
                at, other = group * width, (1 - group) * width
                values = ours_ref[:, at : at + width] + theirs_ref[:, other : other + width]
                values = values.astype(BF16)
            span = slice(part * width, (part + 1) * width)
            if group == 0:
                own_ref[:, span] = values
                term = nn(values, w_ref[part])
            else:
                rows = values.shape[0]
                if part < 2:
                    send_ref[0:rows, span] = values.astype(F32)
                else:
                    send_ref[rows:, :width] = values[: rows // 2].astype(F32)
                    send_ref[rows:, width:] = values[rows // 2 :].astype(F32)
                term = nn(values, other_ref[span, :])
            total = term if total is None else total + term
    out_ref[...] = total


def first_grad(dqs, ours, theirs, weight, other, after=()):
    rows = ours[0].shape[0]
    _, width, model = weight.shape
    return call(
        first_grad_kernel,
        "first_grad",
        [
            shape_of((rows, model), F32),
            shape_of((rows, 3 * width), BF16),
            shape_of((rows + rows // 2, 2 * width), F32),
        ],
        after=after,
    )(*dqs, *ours, *theirs, weight, other)


def first_back_kernel(
    core_ref, ours_ref, theirs_ref, x_ref, middle0_ref, middle1_ref, vec_ref, kept0_ref, kept1_ref,
    out_ref, sums_ref, *res_refs,
):
    gain_sum = bias_sum = 0.0
    start = 0
    for middle_ref, kept_ref, res_ref in zip((middle0_ref, middle1_ref), (kept0_ref, kept1_ref), res_refs):
        res_ref[...] = kept_ref[kept_ref.shape[0] - res_ref.shape[0] :, :]
        count = middle_ref.shape[0]
        at = slice(start, start + count)
        grad = ours_ref[at, :] + theirs_ref[at, :]
        normal, factor = normalize(x_ref[half_of(core_ref, x_ref, start, count), :].astype(F32))
        total = middle_ref[...] + norm_back(grad, normal, factor, vector(vec_ref, LN1_GAIN))
        out_ref[at, :] = total.astype(BF16).astype(F32)
        gain_sum = gain_sum + column_sum(grad * normal)
        bias_sum = bias_sum + column_sum(grad)
        start += count
    sums_ref[0:1, :] = gain_sum
    sums_ref[1:2, :] = bias_sum


def first_back(core, ours, theirs, x, middles, vectors, kepts, counts, after=()):
    rows, model = ours.shape
    return call(
        first_back_kernel,
        "first_back",
        [shape_of((rows, model), F32), shape_of((8, model), F32)]
        + [shape_of((count, model), F32) for count in counts],
        scalars=1,
        after=after,
    )(core, ours, theirs, x, *middles, vectors, *kepts)


def result_kernel(*refs, starts, placed):
    vec_ref, out_ref = refs[3 * len(starts)], refs[-1]
    at = 0
    if placed:
        done_ref = refs[3 * len(starts) + 1]
        at = done_ref.shape[0]
        out_ref[0:at, :] = done_ref[...]
    for part, (start, rows) in enumerate(starts):
        ours_ref, theirs_ref, kept_ref = refs[3 * part : 3 * part + 3]
        fed = ours_ref[0:rows, :] + theirs_ref[0:rows, :] + vector(vec_ref, FC2_BIAS)
        total = kept_ref[start : start + rows, :] + fed
        out_ref[at : at + rows, :] = total.astype(BF16).astype(F32)
        at += rows


def result_rows(parts, vectors, done=(), after=()):
    operands = [array for part in parts for array in part[:3]]
    rows = sum(part[4] for part in parts) + sum(array.shape[0] for array in done)
    return call(
        functools.partial(
            result_kernel, starts=[part[3:] for part in parts], placed=bool(done)
        ),
        "result_rows",
        [shape_of((rows, vectors.shape[1]), F32)],
        after=after,
    )(*operands, vectors, *done)[0]


def finish_kernel(core_ref, ours_ref, theirs_ref, out_ref, in_ref, low_ref, in_sem, out_sem):
    count = in_ref.shape[0] // 2
    rows = in_ref.shape[1]
    reads, writes = [], []
    for index in range(2 * count):
        ref = ours_ref if index < count else theirs_ref
        at = (index % count) * rows
        read = pltpu.make_async_copy(ref.at[pl.ds(at, rows), :], in_ref.at[index], in_sem.at[index])
        read.start()
        reads.append(read)
    for index, read in enumerate(reads):
        half = core_ref[0] if index < count else 1 - core_ref[0]
        place = pl.multiple_of(half * count * rows + (index % count) * rows, 128)
        read.wait()
        low_ref[index] = in_ref[index].astype(BF16)
        write = pltpu.make_async_copy(
            low_ref.at[index], out_ref.at[pl.ds(place, rows), :], out_sem.at[index]
        )
        write.start()
        writes.append(write)
    for write in writes:
        write.wait()


def finish(core, pairs, after=()):
    ((ours, theirs),) = pairs
    rows, model = ours.shape
    pieces = 4
    held = [pltpu.VMEM((2 * pieces, rows // pieces, model), dtype) for dtype in (F32, BF16)]

    def run(*refs):
        finish_kernel(*refs[:3], *refs[3 + len(after) :])

    return pl.pallas_call(
        run,
        in_specs=[pl.BlockSpec(memory_space=pltpu.SMEM)]
        + [pl.BlockSpec(memory_space=pltpu.HBM)] * 2
        + [pl.BlockSpec(memory_space=pl.ANY)] * len(after),
        out_specs=pl.BlockSpec(memory_space=pltpu.HBM),
        scratch_shapes=[*held, pltpu.SemaphoreType.DMA((8,)), pltpu.SemaphoreType.DMA((8,))],
        out_shape=shape_of((2 * rows, model), BF16),
        compiler_params=pltpu.CompilerParams(vmem_limit_bytes=60 * 1024 * 1024),
        name="finish",
    )(core, ours, theirs, *after)


def gather_sums_kernel(second0, second1, feed0, feed1, norm, fc1, heads, partial_ref, whole_ref):
    partial_ref[...] = jnp.zeros_like(partial_ref)
    whole_ref[...] = jnp.zeros_like(whole_ref)
    partial_ref[0:1, :] = second0[2:3, :] + second1[2:3, :]
    partial_ref[1:2, :] = feed0[0:1, :] + feed1[0:1, :]
    partial_ref[2:4, :] = second0[0:2, :] + second1[0:2, :]
    partial_ref[4:6, :] = norm[0:2, :]
    whole_ref[6:7, :] = fc1[0:1, :]
    whole_ref[7:8, :] = heads[0:1, :]


def gather_sums(arrays, after=()):
    shape = shape_of(arrays[0].shape, F32)
    return call(gather_sums_kernel, "gather_sums", [shape, shape], after=after)(*arrays)


def feed_sum_kernel(ours_ref, theirs_ref, fc2_ref, fc1_ref):
    units = fc2_ref.shape[1]
    total = ours_ref[...] + theirs_ref[...]
    fc2_ref[...] = total[:, :units]
    fc1_ref[...] = total[:, units:]


def feed_sum(ours, theirs, after=()):
    half = shape_of((ours.shape[0], ours.shape[1] // 2), F32)
    return call(
        feed_sum_kernel, "feed_sum", [half, half], after=after
    )(ours, theirs)


def heads_sum_kernel(ours_ref, theirs_ref, heads_ref, out_ref):
    width = heads_ref.shape[2]
    total = ours_ref[...] + theirs_ref[...]
    for part in range(3):
        heads_ref[part] = total[:, part * width : (part + 1) * width]
    out_ref[...] = jnp.transpose(total[:, 3 * width :])


def heads_sum(ours, theirs, after=()):
    rows, width = ours.shape[0], ours.shape[1] // 4
    shapes = [shape_of((3, rows, width), F32), shape_of((width, rows), F32)]
    return call(
        heads_sum_kernel, "heads_sum", shapes, after=after
    )(ours, theirs)


def body(
    tokens,
    ln1_gain,
    ln1_bias,
    qkv_weight,
    qkv_bias,
    out_weight,
    out_bias,
    ln2_gain,
    ln2_bias,
    fc1_weight,
    fc1_bias,
    fc2_weight,
    fc2_bias,
    cotangent,
    *,
    batch_count,
    tensor_count,
):
    rows, model = tokens.shape[1:]
    width = qkv_weight.shape[2]
    units = fc1_weight.shape[1]
    bits = batch_count.bit_length() - 1
    batch_at = lax.axis_index("batch")
    core = (lax.axis_index("tensor") % 2).astype(jnp.int32).reshape(1)

    def core_swap(v):
        return lax.ppermute(v, "tensor", [(i, i ^ 1) for i in range(tensor_count)])

    def chip_swap(v):
        return lax.ppermute(v, "tensor", [(i, i ^ 2) for i in range(tensor_count)])

    def batch_swap(v, bit):
        return lax.ppermute(v, "batch", [(i, i ^ (1 << bit)) for i in range(batch_count)])

    last = []

    def then(made, *others):
        last[:] = [made[0], *others]
        return made

    orders = ([0, *range(1, bits)], [1, 0, *range(2, bits)])

    def mine_of(some):
        return jnp.stack([(batch_at >> bit) & 1 for bit in some]).astype(jnp.int32)

    class Scatter:
        def __init__(self, cut, order, left=range(bits - 1, -1, -1)):
            self.order = list(order)
            self.left = list(left)
            self.cross(cut)

        def cross(self, cut):
            send, self.keep = cut
            bit = self.order.pop(0)
            self.left.remove(bit)
            self.theirs = batch_swap(send, bit)

        def step(self, *others):
            bit = self.order[0]
            pairs = [(v.keep, v.theirs) for v in (self, *others)]
            self.cross(
                then(hop(mine_of([bit]), pairs, 1 << len(self.left), [self.left.index(bit)], after=last))
            )

        def step_beside(self, other):
            both = (self, other)
            some = [v.order[0] for v in both]
            made = then(
                hop(
                    mine_of(some), [(v.keep, v.theirs) for v in both], 1 << len(self.left),
                    [v.left.index(bit) for v, bit in zip(both, some)], after=last,
                )
            )
            self.cross(made[:2])
            other.cross(made[2:])

        def end(self, summed):
            while self.order:
                self.step()
            return then(summed(self.keep, self.theirs, after=last))

    def weight_scatters(kernel, operands, widths, orders, held, sums=True):
        width = sum(widths)
        spans = [slice(sum(widths[:i]), sum(widths[: i + 1])) for i in range(len(widths))]
        firsts = [order[0] for order in orders]
        made = then(
            weight_grad(
                kernel, core, mine_of(firsts), operands, model, width, spans, batch_count,
                [bits - 1 - bit for bit in firsts], sums=sums, far=(), held=held, after=last,
            )
        )
        return [Scatter(made[2 * i : 2 * i + 2], order) for i, order in enumerate(orders)], made[-1]

    x = tokens.reshape(rows, model)
    dy = cotangent.reshape(rows, model)
    heads_weight = jnp.transpose(qkv_weight, (1, 2, 0))
    listed = (
        ln1_gain, ln1_bias, jnp.transpose(qkv_bias, (1, 0, 2)), out_bias, ln2_gain, ln2_bias, fc1_bias,
        fc2_bias,
    )
    vectors, heads_wide, out_weight_wide = pack(listed, heads_weight, out_weight)

    heads_other = core_swap(heads_wide)
    out_weight_far = chip_swap(out_weight_wide)
    others = then(
        widen([fc1_weight, fc2_weight, out_weight], after=[heads_wide])
    )
    others = [core_swap(v) for v in others]
    other_bias = heads_other[3 * width + FC1_BIAS :]

    left, queries, keys, values = then(
        project(core, x, vectors, heads_weight, heads_other, after=last)
    )
    near, totals = then(attend(queries, keys, values, after=last))
    far = chip_swap(near)
    fc1_other, fc2_other, out_weight_other, heads_other_low = then(
        convert([*others, heads_other], BF16, after=last)
    )
    dy_turned = then(turn(dy, after=last))[0]
    out_weight_both = core_swap(out_weight_far)
    out_weights = (out_weight, out_weight_other, out_weight_far, out_weight_both)

    half = rows // 2
    sizes = (3 * half // 4, half // 4)
    starts = (0, sizes[0])
    fed = []
    for start, size in zip(starts, sizes):
        fed.append(
            then(
                feed(
                    core, start, size, x, dy, near, far, out_weights, vectors, other_bias, fc1_weight,
                    fc2_weight, (fc1_other, fc2_other), after=last,
                )
            )
        )
    kepts, owns = [f[0] for f in fed], [f[1] for f in fed]
    grads, feed_sums = [f[-2] for f in fed], [f[-1] for f in fed]
    grads_far = [chip_swap(v) for v in grads]
    swaps = [core_swap(v) for f in fed for v in f[2:-2]]
    (fc2,), _ = weight_scatters(
        fc2_grad_kernel, [dy_turned, *owns, *swaps], [units], orders[1:],
        [
            pltpu.VMEM((model, rows), BF16),
            *(pltpu.VMEM((size, units), dtype) for dtype in (BF16, F32) for size in sizes),
            pltpu.SemaphoreType.DMA((5,)),
        ],
        sums=False
    )
    (fc1,), fc1_sums = weight_scatters(fc1_grad_kernel, [*owns, *swaps], [units], orders[:1],
        [
            *(pltpu.VMEM((2 * size, units), dtype) for dtype in (BF16, F32) for size in sizes),
            pltpu.SemaphoreType.DMA((5,)),
        ],
    )

    weights = (out_weight, out_weight_other)
    heads = (queries, keys, values, totals)
    middle0, low0, second_sums0, res0 = then(
        second_back(core, 0, grads[0], grads_far[0], kepts[0], dy, vectors, after=last)
    )
    res0_far = chip_swap(res0)
    dq0, dk0, dv0 = then(attend_back(core, 0, low0, weights, *heads, after=last))
    middle1, low1, second_sums1, out_w = then(
        second_back(
            core, starts[1], grads[1], grads_far[1], kepts[1], dy, vectors, (low0, near),
            after=last,
        )
    )
    out_w_other = core_swap(out_w)
    dq1, dk_send, dv_send, dk, dv = then(
        attend_back(core, starts[1], low1, weights, *heads, (dk0, dv0), after=last)
    )
    theirs = core_swap(dk_send), core_swap(dv_send)
    fc2.step_beside(fc1)
    grad_rows, heads_own, send = then(
        first_grad(
            (dq0, dq1), (dk, dv), theirs, heads_weight, heads_other_low, after=[*last, res0_far]
        )
    )
    grad_rows_far = chip_swap(grad_rows)
    heads_theirs = core_swap(send)
    heads, heads_sums = weight_scatters(
        heads_grad_kernel,
        [left, heads_own, heads_theirs, low0, low1, near, out_w_other],
        [8 * width // 3, 4 * width // 3],
        orders,
        (),
    )
    result0 = then([result_rows([(res0, res0_far, kepts[0], 0, BLOCK)], vectors, after=last)])[0]
    fc2.step(fc1)
    heads[1].step()
    heads[0].step()
    counts = (sizes[0] - BLOCK, sizes[1])
    grad_rows, norm_sums, *res1 = then(
        first_back(
            core, grad_rows, grad_rows_far, x, (middle0, middle1), vectors, kepts, counts, after=last
        )
    )
    grad_rows_other = core_swap(grad_rows)
    res1_far = [chip_swap(v) for v in res1]
    grad_fc2, grad_fc1 = fc2.end(feed_sum)
    heads[0].step(heads[1])
    partial, whole = then(
        gather_sums(
            (second_sums0, second_sums1, *feed_sums, norm_sums, fc1_sums, heads_sums), after=last
        )
    )
    small = partial + core_swap(partial) + whole
    for bit in range(bits):
        small = small + batch_swap(small, bit)
    grad_heads, grad_out = heads[0].end(heads_sum)
    last.append(small)
    parts = [
        (v, far, kept, start, count)
        for v, far, kept, start, count in zip(res1, res1_far, kepts, (BLOCK, 0), counts)
    ]
    result = then([result_rows(parts, vectors, [result0], after=last)])[0]
    result_other = core_swap(result)
    grad_tokens = then([finish(core, [(grad_rows, grad_rows_other)], after=last)])[0]
    result = then([finish(core, [(result, result_other)], after=last)])[0]
    share = HD // batch_count
    piece = model // batch_count
    shared = lax.dynamic_slice_in_dim(small[:6], batch_at * piece, piece, 1)
    own = lax.dynamic_slice_in_dim(
        small[6:].reshape(2, model // HD, HD), batch_at * share, share, 2
    )
    return (
        result.reshape(tokens.shape),
        grad_tokens.reshape(tokens.shape),
        jnp.transpose(grad_heads, (1, 0, 2)),
        own[1, : 3 * width // HD].reshape(3, width // HD, share)[::2],
        grad_out,
        shared[0],
        shared[4],
        shared[5],
        shared[2],
        shared[3],
        grad_fc1,
        own[0, : units // HD],
        grad_fc2.T,
        shared[1],
    )


def solution(mesh):
    placed = (
        P("batch", None, None),
        P(),
        P(),
        P(None, None, "tensor"),
        P(None, "tensor", None),
        P("tensor", None),
        P(),
        P(),
        P(),
        P(None, "tensor"),
        P("tensor", None),
        P("tensor", None),
        P(),
        P("batch", None, None),
    )
    return jax.shard_map(
        functools.partial(
            body, batch_count=mesh.shape["batch"], tensor_count=mesh.shape["tensor"]
        ),
        mesh=mesh,
        in_specs=placed,
        out_specs=(
            P("batch", None, None),
            P("batch", None, None),
            P("batch", None, "tensor"),
            P(None, "tensor", "batch"),
            P("tensor", "batch"),
            P("batch"),
            P("batch"),
            P("batch"),
            P("batch"),
            P("batch"),
            P("batch", "tensor"),
            P("tensor", "batch"),
            P("tensor", "batch"),
            P("batch"),
        ),
        check_vma=False,
    )
```
